32 devices in a mesh: fsdp: 4 (over z), ctx: 2 (over y), tp: 4 (over x, core).
Axes of the slice: x: 2, y: 2, z: 4, core: 2. Of those that a mesh axis runs over, the one named last changes fastest.
Arguments:
- tokens: bfloat16 [4, 1024, 2560], P('fsdp', 'ctx'), may hold values from -40 to 40
- segments: int32 [4, 1024], P('fsdp'), may hold values from 0 to 3, as said below
- attn_gain: bfloat16 [2560], P(('fsdp', 'ctx')), may hold values from 0.25 to 1.75
- q_weight: bfloat16 [2560, 2560], P(('fsdp', 'ctx'), 'tp'), may hold values from -0.125 to 0.125
- k_weight: bfloat16 [2560, 640], P(('fsdp', 'ctx'), 'tp'), may hold values from -0.125 to 0.125
- v_weight: bfloat16 [2560, 640], P(('fsdp', 'ctx'), 'tp'), may hold values from -0.125 to 0.125
- o_weight: bfloat16 [2560, 2560], P('tp', ('fsdp', 'ctx')), may hold values from -0.5 to 0.5
- ffn_gain: bfloat16 [2560], P(('fsdp', 'ctx')), may hold values from 0.25 to 1.75
- gate_weight: bfloat16 [2560, 6912], P(('fsdp', 'ctx'), 'tp'), may hold values from -0.125 to 0.125
- up_weight: bfloat16 [2560, 6912], P(('fsdp', 'ctx'), 'tp'), may hold values from -0.125 to 0.125
- down_weight: bfloat16 [6912, 2560], P('tp', ('fsdp', 'ctx')), may hold values from -0.078125 to 0.078125
- cotangent: bfloat16 [4, 1024, 2560], P('fsdp', 'ctx'), may hold values from -6 to 6
Outputs:
- output: bfloat16 [4, 1024, 2560], P('fsdp', 'ctx')
- input_grad: bfloat16 [4, 1024, 2560], P('fsdp', 'ctx')
- attn_gain_grad: float32 [2560], P(('fsdp', 'ctx'))
- q_grad: float32 [2560, 2560], P(('fsdp', 'ctx'), 'tp')
- k_grad: float32 [2560, 640], P(('fsdp', 'ctx'), 'tp')
- v_grad: float32 [2560, 640], P(('fsdp', 'ctx'), 'tp')
- o_grad: float32 [2560, 2560], P('tp', ('fsdp', 'ctx'))
- ffn_gain_grad: float32 [2560], P(('fsdp', 'ctx'))
- gate_grad: float32 [2560, 6912], P(('fsdp', 'ctx'), 'tp')
- up_grad: float32 [2560, 6912], P(('fsdp', 'ctx'), 'tp')
- down_grad: float32 [6912, 2560], P('tp', ('fsdp', 'ctx'))
The draws below stay inside these ranges and needn't reach their ends.
Inputs may be any that keep to these rules, and one draw needn't show every extreme that they name: `segments`: in each sequence four documents numbered 0 to 3 in order of position; document 1 covers at least positions 256 to 767.
All inputs are finite; a program needn't handle non-finite values.
Results may differ from the reference program's by a relative error of at most 0.014.
Values may be sent and summed in bfloat16 or wider, within the bound.
A program may use at most 256 MiB of HBM per device.

```python
import math
import jax
import jax.numpy as jnp
from jax import lax

D = 2560
HEADS = 32
KV_HEADS = 8
HEAD_DIM = 80
FF = 6912
LEN = 1024
SEQS = 4
Q_COLS = 2560
KV_COLS = 640


def draw_tokens(key, part):
    key = jax.random.fold_in(key, 11)
    key_rows, key_cols, key_base = jax.random.split(key, 3)
    row_scale = jnp.exp(jax.random.uniform(key_rows, (SEQS, LEN, 1), jnp.float32, math.log(0.5), math.log(5.0)))
    col_scale = jnp.exp(jax.random.uniform(key_cols, (1, 1, D), jnp.float32, math.log(0.5), math.log(2.0)))
    base_vals = jnp.clip(jax.random.normal(key_base, (SEQS, LEN, D), jnp.float32), -4.0, 4.0)
    return (base_vals * row_scale * col_scale).astype(jnp.bfloat16)


def draw_segments(key, part):
    key = jax.random.fold_in(key, 23)
    key_first, key_second, key_third = jax.random.split(key, 3)
    first_cut = jax.random.randint(key_first, (SEQS, 1), LEN // 16, LEN // 4)
    second_cut = jax.random.randint(key_second, (SEQS, 1), 3 * LEN // 4, 7 * LEN // 8)
    third_cut = jax.random.randint(key_third, (SEQS, 1), 7 * LEN // 8 + 1, LEN - LEN // 32)
    position = jnp.arange(LEN, dtype=jnp.int32)[None, :]
    return (position >= first_cut).astype(jnp.int32) + (position >= second_cut).astype(jnp.int32) + (position >= third_cut).astype(jnp.int32)


def spiked(values, own_key, source, target, parts, factor):
    owner, partner = [(jnp.arange(values.shape[dim]) // (values.shape[dim] // parts)).reshape([-1 if axis == dim else 1 for axis in range(values.ndim)]) for dim in (source, target)]
    chosen = jax.random.permutation(own_key, parts)[partner]
    strong = (owner == chosen) | (owner == (partner + parts // 2) % parts)
    return jnp.where(strong, factor * values, values)


def steps_of(own_key, dims, shards, least, largest):
    factor_of = 1.0
    for axis_at, parts in shards:
        heights = jax.random.uniform(jax.random.fold_in(jax.random.fold_in(own_key, 6), axis_at), (parts,), jnp.float32, least / len(shards), largest / len(shards))
        factor_of = factor_of * jnp.repeat(jnp.exp(heights), dims[axis_at] // parts).reshape((-1,) + (1,) * (len(dims) - 1 - axis_at))
    return factor_of


def scatter_about(own_key, dims, spread, reach, cuts=(), kind=jnp.bfloat16):
    values = spread * jax.random.normal(own_key, dims, jnp.float32)
    if cuts:
        values = values * steps_of(own_key, dims, cuts, -0.22, 0.18)
    return jnp.clip(values, -reach, reach).astype(kind)


def bell_draw_with(rng, extent, spread, bound, cuts, heavy, held_as=jnp.bfloat16):
    drawn = spread * jax.random.normal(rng, extent, jnp.float32)
    if cuts:
        drawn = drawn * steps_of(rng, extent, cuts, -0.22, 0.18)
    return jnp.clip(spiked(drawn, jax.random.fold_in(rng, 3), *heavy), -bound, bound).astype(held_as)


def setup_inputs(seed: int = 0) -> dict:
    keys = jax.random.split(jax.random.key(seed), 13)
    tokens = draw_tokens(jax.random.fold_in(keys[12], 71), 0)
    segments = draw_segments(jax.random.fold_in(keys[12], 71), 0)
    attn_gain = jnp.clip(1.0 + 0.15 * jax.random.normal(keys[2], (D,), jnp.float32), 0.25, 1.75).astype(jnp.bfloat16)
    q_weight = scatter_about(keys[3], (D, Q_COLS), D ** -0.5, 0.125, ((0, 8), (1, 4)))
    k_weight = scatter_about(keys[4], (D, KV_COLS), D ** -0.5, 0.125, ((0, 8), (1, 4)))
    v_weight = scatter_about(keys[5], (D, KV_COLS), D ** -0.5, 0.125, ((0, 8), (1, 4)))
    o_weight = scatter_about(keys[6], (Q_COLS, D), (Q_COLS // 16) ** -0.5, 0.5, ((0, 4), (1, 8)))
    ffn_gain = jnp.clip(1.0 + 0.15 * jax.random.normal(keys[7], (D,), jnp.float32), 0.25, 1.75).astype(jnp.bfloat16)
    gate_weight = scatter_about(keys[8], (D, FF), D ** -0.5, 0.125, ((0, 8), (1, 4)))
    up_weight = scatter_about(keys[9], (D, FF), D ** -0.5, 0.125, ((0, 8), (1, 4)))
    down_weight = scatter_about(keys[10], (FF, D), FF ** -0.5, 0.078125, ((0, 4), (1, 8)))
    cotangent = bell_draw_with(keys[11], (SEQS, LEN, D), 1.0, 6.0, ((0, 4), (1, 2)), (0, 2, 4, 2.0))
    return {"tokens": tokens, "segments": segments, "attn_gain": attn_gain, "q_weight": q_weight, "k_weight": k_weight, "v_weight": v_weight, "o_weight": o_weight, "ffn_gain": ffn_gain, "gate_weight": gate_weight, "up_weight": up_weight, "down_weight": down_weight, "cotangent": cotangent}


NORM_EPS = 1e-05
ROPE_BASE = 10000.0
MASK_FILL = -1000000000.0

@jax.custom_vjp
def low(v):
    return lax.optimization_barrier(v.astype(jnp.bfloat16)).astype(jnp.float32)

@jax.custom_vjp
def low_back(v):
    return v

def low_keep(v):
    return (low(v), None)

def low_pass(kept, grad):
    return (grad,)

def back_keep(v):
    return (v, None)

def back_low(kept, grad):
    return (low(grad),)
low.defvjp(low_keep, low_pass)
low_back.defvjp(back_keep, back_low)

def product(left, right):
    return jnp.einsum('bld,de->ble', left, right, precision=lax.Precision.HIGHEST)

def rope_tables(segments):
    n_seqs = segments.shape[0]
    position = jnp.arange(LEN, dtype=jnp.int32)
    change = jnp.concatenate([jnp.ones((n_seqs, 1), dtype=bool), segments[:, 1:] != segments[:, :-1]], axis=1)
    starts = lax.cummax(jnp.where(change, position[None, :], 0), axis=1)
    offset = (position[None, :] - starts).astype(jnp.float32)
    frequency = jnp.exp(jnp.arange(HEAD_DIM // 2, dtype=jnp.float32) * (-2.0 * math.log(ROPE_BASE) / HEAD_DIM))
    angles = offset[:, :, None] * frequency[None, None, :]
    return (jnp.cos(angles)[:, :, None, :], jnp.sin(angles)[:, :, None, :])

def rotate(values, cos_t, sin_t):
    half_dim = values.shape[-1] // 2
    front_half = values[..., :half_dim]
    back_half = values[..., half_dim:]
    return jnp.concatenate([front_half * cos_t - back_half * sin_t, back_half * cos_t + front_half * sin_t], axis=-1)

def attend(q_heads, k_heads, v_heads, segments):
    block_len = min(512, LEN)
    n_blocks = LEN // block_len
    key_pos = jnp.arange(LEN, dtype=jnp.int32)
    score_scale = HEAD_DIM ** (-0.5)

    def one_block(block_idx):
        q_start = block_idx * block_len
        q_block = lax.dynamic_slice_in_dim(q_heads, q_start, block_len, 1)
        seg_rows = lax.dynamic_slice_in_dim(segments, q_start, block_len, 1)
        q_pos = q_start + jnp.arange(block_len, dtype=jnp.int32)
        scores = jnp.einsum('bqkgd,bskd->bkgqs', q_block, k_heads, precision=lax.Precision.HIGHEST) * score_scale
        scores = low_back(scores)
        allowed = (seg_rows[:, :, None] == segments[:, None, :]) & (key_pos[None, None, :] <= q_pos[None, :, None])
        scores = jnp.where(allowed[:, None, None], scores, MASK_FILL)
        row_max = lax.optimization_barrier(jnp.max(scores, axis=-1, keepdims=True))
        exp_scores = jnp.exp(scores - row_max)
        prob_low = low(exp_scores / lax.optimization_barrier(jnp.sum(exp_scores, axis=-1, keepdims=True)))
        return jnp.einsum('bkgqs,bskd->bqkgd', prob_low, v_heads, precision=lax.Precision.HIGHEST)
    out_blocks = lax.map(jax.checkpoint(one_block), jnp.arange(n_blocks, dtype=jnp.int32))
    return jnp.moveaxis(out_blocks, 0, 1).reshape(q_heads.shape[0], LEN, HEADS * HEAD_DIM)

def one_layer(tok_f32, segments, weights):
    attn_gain, q_weight, k_weight, v_weight, o_weight, ffn_gain, gate_weight, up_weight, down_weight = weights
    group_seqs = tok_f32.shape[0]
    cos_t, sin_t = rope_tables(segments)
    root_attn = lax.rsqrt(lax.optimization_barrier(jnp.mean(tok_f32 * tok_f32, axis=-1, keepdims=True)) + NORM_EPS)
    norm_attn = low(tok_f32 * root_attn * attn_gain)
    q_pre = low_back(product(norm_attn, q_weight)).reshape(group_seqs, LEN, HEADS, HEAD_DIM)
    k_pre = low_back(product(norm_attn, k_weight)).reshape(group_seqs, LEN, KV_HEADS, HEAD_DIM)
    q_rot = low_back(low(rotate(q_pre, cos_t, sin_t)))
    k_rot = low_back(low(rotate(k_pre, cos_t, sin_t)))
    v_val = low_back(low(product(norm_attn, v_weight))).reshape(group_seqs, LEN, KV_HEADS, HEAD_DIM)
    q_rot = q_rot.reshape(group_seqs, LEN, KV_HEADS, HEADS // KV_HEADS, HEAD_DIM)
    attn_out = low_back(low(attend(q_rot, k_rot, v_val, segments)))
    resid_mid = tok_f32 + low_back(product(attn_out, o_weight))
    root_ffn = lax.rsqrt(lax.optimization_barrier(jnp.mean(resid_mid * resid_mid, axis=-1, keepdims=True)) + NORM_EPS)
    norm_ffn = low(resid_mid * root_ffn * ffn_gain)
    gate_val = low_back(product(norm_ffn, gate_weight))
    up_val = low_back(product(norm_ffn, up_weight))
    hidden = low(jax.nn.silu(gate_val) * up_val)
    return resid_mid + low_back(product(hidden, down_weight))

def reference(tokens, segments, attn_gain, q_weight, k_weight, v_weight, o_weight, ffn_gain, gate_weight, up_weight, down_weight, cotangent):
    per_step = math.gcd(SEQS, max(1, 4096 // LEN))

    def whole_fwd(tok_f32, weights):
        stacked = tok_f32.reshape(SEQS // per_step, per_step, LEN, D)
        seg_steps = segments.reshape(SEQS // per_step, per_step, LEN)

        def scan_step(running, pieces):
            return (running, jax.checkpoint(one_layer)(pieces[0], pieces[1], weights))
        unused, outputs = lax.scan(scan_step, jnp.zeros((), jnp.float32), (stacked, seg_steps))
        return outputs.reshape(SEQS, LEN, D)
    weights = tuple((array_in.astype(jnp.float32) for array_in in (attn_gain, q_weight, k_weight, v_weight, o_weight, ffn_gain, gate_weight, up_weight, down_weight)))
    result, pullback = jax.vjp(whole_fwd, tokens.astype(jnp.float32), weights)
    tok_grad, weight_grads = pullback(cotangent.astype(jnp.float32))
    return (result.astype(jnp.bfloat16), tok_grad.astype(jnp.bfloat16), weight_grads[0], weight_grads[1], weight_grads[2], weight_grads[3], weight_grads[4], weight_grads[5], weight_grads[6], weight_grads[7], weight_grads[8])
```

```python
import math

import jax
import jax.numpy as jnp
from jax import lax
from jax.experimental import pallas as pl
from jax.experimental.pallas import tpu as pltpu
from jax.sharding import PartitionSpec as P

HEAD_DIM = 80
HALF = HEAD_DIM // 2
LANES = 128
NORM_EPS = 1e-05
ROPE_BASE = 10000.0
MASK_FILL = -1000000000.0
F32 = jnp.float32
BF16 = jnp.bfloat16


def pp(value, axis, mask):
    size = lax.axis_size(axis)
    return lax.ppermute(value, axis, [(i, i ^ mask) for i in range(size)])


def dot(a, b, dims=((1,), (0,))):
    return lax.dot_general(a, b, (dims, ((), ())), preferred_element_type=F32)


def in_order(bit, mine, other, axis=0):
    return jnp.where(
        bit == 0, jnp.stack([mine, other], axis), jnp.stack([other, mine], axis)
    )


def pick(blocks, index):
    return lax.dynamic_index_in_dim(blocks, index, 0, keepdims=False)


def attend_kernel(scale, block, qkv, cos, sin, seg_col, seg_row, sel, attn, rot, stats):
    full_len = qkv.shape[0]
    n_q = rot.shape[1] // LANES - 2
    cos_t, sin_t = cos[...], sin[...]
    for h in range(n_q + 1):
        u = qkv[:, h * LANES : (h + 1) * LANES]
        rot[:, h * LANES : (h + 1) * LANES] = (u * cos_t + pltpu.roll(u, 64, 1) * sin_t).astype(BF16)
    rot[:, (n_q + 1) * LANES :] = qkv[:, (n_q + 1) * LANES :].astype(BF16)
    for i in range(full_len // block):
        rows = slice(i * block, (i + 1) * block)
        keys = (i + 1) * block
        q_pos = i * block + lax.broadcasted_iota(jnp.int32, (block, keys), 0)
        k_pos = lax.broadcasted_iota(jnp.int32, (block, keys), 1)
        allowed = (seg_col[rows, :] == seg_row[:, :keys]) & (k_pos <= q_pos)
        k = rot[:keys, n_q * LANES : (n_q + 1) * LANES]
        v = rot[:keys, (n_q + 1) * LANES :]
        outs, maxes, totals = [], [], []
        for h in range(n_q):
            s = dot(rot[rows, h * LANES : (h + 1) * LANES], k, ((1,), (1,))) * scale
            s = jnp.where(allowed, s, MASK_FILL)
            top = jnp.max(s, axis=1, keepdims=True)
            e = jnp.exp(s - top)
            total = jnp.sum(e, axis=1, keepdims=True)
            outs.append(dot((e * (1.0 / total)).astype(BF16), v).astype(BF16))
            maxes.append(top)
            totals.append(total)
        attn[rows, :] = dot(jnp.concatenate(outs, axis=1), sel[...]).astype(BF16)
        stats[rows, :] = jnp.concatenate(maxes + totals, axis=1)


def attend_back_kernel(
    scale, block, rot, d_attn, stats, cos, sin, seg_col, seg_row, sel, d_qkv, dk_sum, dv_sum
):
    full_len = rot.shape[0]
    n_q = rot.shape[1] // LANES - 2
    dk_sum[...] = jnp.zeros_like(dk_sum)
    dv_sum[...] = jnp.zeros_like(dv_sum)

    def back(u, at):
        return (u * cos[at, :] - pltpu.roll(u, 64, 1) * sin[at, :]).astype(BF16)

    for i in range(full_len // block):
        rows = slice(i * block, (i + 1) * block)
        keys = (i + 1) * block
        q_pos = i * block + lax.broadcasted_iota(jnp.int32, (block, keys), 0)
        k_pos = lax.broadcasted_iota(jnp.int32, (block, keys), 1)
        allowed = (seg_col[rows, :] == seg_row[:, :keys]) & (k_pos <= q_pos)
        k = rot[:keys, n_q * LANES : (n_q + 1) * LANES]
        v = rot[:keys, (n_q + 1) * LANES :]
        d_out = dot(d_attn[rows, :], sel[...], ((1,), (1,))).astype(BF16)
        stat = stats[rows, :]
        for h in range(n_q):
            q = rot[rows, h * LANES : (h + 1) * LANES]
            d_h = d_out[:, h * LANES : (h + 1) * LANES]
            s = dot(q, k, ((1,), (1,))) * scale
            s = jnp.where(allowed, s, MASK_FILL)
            p = jnp.exp(s - stat[:, h : h + 1]) * (1.0 / stat[:, n_q + h : n_q + h + 1])
            dv_sum[:keys, :] += dot(p.astype(BF16), d_h, ((0,), (0,)))
            d_p = dot(d_h, v, ((1,), (1,)))
            d_s = (p * (d_p - jnp.sum(p * d_p, axis=1, keepdims=True))).astype(BF16)
            d_q = (dot(d_s, k) * scale).astype(BF16).astype(F32)
            d_qkv[rows, h * LANES : (h + 1) * LANES] = back(d_q, rows)
            dk_sum[:keys, :] += dot(d_s, q, ((0,), (0,)))
    d_k = (dk_sum[...] * scale).astype(BF16).astype(F32)
    d_qkv[:, n_q * LANES : (n_q + 1) * LANES] = back(d_k, slice(None))
    d_qkv[:, (n_q + 1) * LANES :] = dv_sum[...].astype(BF16)


VMEM_LIMIT = 56 * 1024 * 1024


def attend(qkv, cos, sin, seg_col, seg_row, sel, scale):
    full_len, width = qkv.shape
    n_q = width // LANES - 2
    return pl.pallas_call(
        lambda *refs: attend_kernel(scale, min(256, full_len), *refs),
        out_shape=(
            jax.ShapeDtypeStruct((full_len, sel.shape[1]), BF16),
            jax.ShapeDtypeStruct((full_len, width), BF16),
            jax.ShapeDtypeStruct((full_len, 2 * n_q), F32),
        ),
        compiler_params=pltpu.CompilerParams(vmem_limit_bytes=VMEM_LIMIT),
        cost_estimate=pl.CostEstimate(
            flops=2 * n_q * full_len * full_len * LANES,
            bytes_accessed=full_len * width * 6,
            transcendentals=n_q * full_len * full_len // 2,
        ),
        name="attend",
    )(qkv, cos, sin, seg_col, seg_row, sel)


def attend_back(rot, d_attn, stats, cos, sin, seg_col, seg_row, sel, scale):
    full_len, width = rot.shape
    n_q = width // LANES - 2
    return pl.pallas_call(
        lambda *refs: attend_back_kernel(scale, min(256, full_len), *refs),
        out_shape=jax.ShapeDtypeStruct((full_len, width), BF16),
        scratch_shapes=[pltpu.VMEM((full_len, LANES), F32), pltpu.VMEM((full_len, LANES), F32)],
        compiler_params=pltpu.CompilerParams(vmem_limit_bytes=VMEM_LIMIT),
        cost_estimate=pl.CostEstimate(
            flops=5 * n_q * full_len * full_len * LANES,
            bytes_accessed=full_len * width * 6,
            transcendentals=n_q * full_len * full_len // 2,
        ),
        name="attend_back",
    )(rot, d_attn, stats, cos, sin, seg_col, seg_row, sel)


def gather_layer(own):
    half = own.shape[-1] // 2
    a, b = own[:, :half], own[:, half:]
    a1 = jnp.stack([a, pp(a, "tp", 2)])
    b1 = jnp.stack([b, pp(b, "ctx", 1)])
    a2 = jnp.stack([a1, pp(a1, "ctx", 1)])
    b2 = jnp.stack([b1, pp(b1, "tp", 2)], axis=1)
    mine = jnp.concatenate([a2, b2], axis=-1)
    return jnp.stack([mine, pp(mine, "tp", 1)], axis=2)


def scatter_layer(lhs, rhs, dims=((1,), (0,))):
    rows, depth = lhs.shape[-2:]

    def product(part):
        return dot(part.reshape(4 * rows, depth), rhs, dims).reshape(2, 2, rows, -1)

    sent = pp(product(lhs[:, :, 1]).astype(BF16), "tp", 1)
    kept = product(lhs[:, :, 0]) + sent.astype(F32)
    half = kept.shape[-1] // 2
    a, b = kept[..., :half], kept[..., half:]
    a1 = a[:, 0] + pp(a[:, 1].astype(BF16), "tp", 2).astype(F32)
    b1 = b[0] + pp(b[1].astype(BF16), "ctx", 1).astype(F32)
    a2 = a1[0] + pp(a1[1].astype(BF16), "ctx", 1).astype(F32)
    b2 = b1[0] + pp(b1[1].astype(BF16), "tp", 2).astype(F32)
    return jnp.concatenate([a2, b2], axis=-1)


def gather_tp(own):
    index = lax.axis_index("tp")
    pair = in_order(index // 2, own, pp(own, "tp", 2))
    return in_order(index % 2, pair, pp(pair, "tp", 1), axis=1).reshape(-1, own.shape[-1])


def sum_tp(value):
    value = value + pp(value, "tp", 1)
    return value + pp(value, "tp", 2)


def by_xor(value, parts, index):
    blocks = value.reshape(parts, -1, value.shape[-1])
    return jnp.stack([pick(blocks, index ^ r) for r in range(parts)])


def below(top):
    masks = []
    while top > 1:
        top //= 2
        masks.append(top)
    return masks


def gather_z(held, top):
    held = dict(held)
    for mask in below(top):
        for rel in list(held):
            held[rel ^ mask] = pp(held[rel], "fsdp", mask)
    return held


def place(held, index, axis):
    shape = list(next(iter(held.values())).shape)
    size = shape[axis]
    shape[axis] = size * len(held)
    out = jnp.zeros(shape, BF16)
    for rel, block in held.items():
        start = [0] * len(shape)
        start[axis] = (index ^ rel) * size
        out = lax.dynamic_update_slice(out, block, start)
    return out


def scatter_z(blocks, top):
    blocks = dict(blocks)
    for mask in reversed(below(top)):
        for rel in [r for r in blocks if r & mask]:
            blocks[rel ^ mask] = blocks[rel ^ mask] + pp(
                blocks.pop(rel).astype(BF16), "fsdp", mask
            ).astype(F32)
    return blocks


def split_z(value, n, index, axis):
    size = value.shape[axis] // n
    return {
        rel: lax.dynamic_slice_in_dim(value, (index ^ rel) * size, size, axis) for rel in range(n)
    }


def body(
    tokens,
    segments,
    attn_gain,
    q_weight,
    k_weight,
    v_weight,
    o_weight,
    ffn_gain,
    gate_weight,
    up_weight,
    down_weight,
    cotangent,
):
    n_z = lax.axis_size("fsdp")
    n_tp = lax.axis_size("tp")
    z, y, t = lax.axis_index("fsdp"), lax.axis_index("ctx"), lax.axis_index("tp")
    zb = z // (n_z // 2)
    _, half_len, width = tokens.shape
    full_len = segments.shape[1]
    rows = half_len // n_tp
    depth = q_weight.shape[0]
    q_cols = q_weight.shape[1] // 2
    kv_cols = k_weight.shape[1] // 2
    units = gate_weight.shape[1] // 4
    n_q = q_cols // HEAD_DIM
    scale = HEAD_DIM ** (-0.5)
    me = y * n_tp + t

    def two(w):
        return w.reshape(w.shape[0], 2, -1).transpose(1, 0, 2)

    extra = jnp.stack([attn_gain, ffn_gain], axis=1)
    extra = jnp.broadcast_to(jnp.pad(extra, ((0, 0), (0, 30)))[None], (2, depth, 32))
    packed = jnp.concatenate([two(q_weight), two(k_weight), two(v_weight), extra], axis=2)
    compact = packed.shape[2]
    in_blk = in_order(y, pick(packed, y), pp(pick(packed, 1 - y), "ctx", 1)).reshape(2 * depth, -1)
    w_in = place(gather_z({0: in_blk}, n_z), z, 0)

    x_here = tokens.reshape(half_len, width)
    x_half = pp(pick(x_here.reshape(2, half_len // 2, width), t % 2), "ctx", 1)
    x_other = in_order(t % 2, x_half, pp(x_half, "tp", 1)).reshape(half_len, width)
    x_all = in_order(y, x_here, x_other).reshape(full_len, width)

    o_two = o_weight.reshape(2, q_cols, depth)
    o_blk = jnp.concatenate(
        list(in_order(y, pick(o_two, y), pp(pick(o_two, 1 - y), "ctx", 1))), axis=1
    )
    w_o = place(gather_z({0: o_blk}, n_z), z, 1)

    def four(w):
        return w.reshape(depth, 2, 2, units).transpose(1, 2, 0, 3)

    gu = jnp.concatenate([four(gate_weight), four(up_weight)], axis=3)
    gu_y = gu.transpose(1, 0, 2, 3)
    gu_blk = in_order(y, pick(gu_y, y), pp(pick(gu_y, 1 - y), "ctx", 1), axis=1).reshape(
        2, 2 * depth, 2 * units
    )
    w_gu = place(
        gather_z({0: pick(gu_blk, zb), n_z // 2: pp(pick(gu_blk, 1 - zb), "fsdp", n_z // 2)}, n_z // 2),
        z,
        0,
    )
    dn_y = down_weight.reshape(2, 2, units, depth).transpose(1, 0, 2, 3)
    dn_pair = in_order(y, pick(dn_y, y), pp(pick(dn_y, 1 - y), "ctx", 1))
    dn_blk = jnp.concatenate([dn_pair[0], dn_pair[1]], axis=2)
    w_dn = place(
        gather_z({0: pick(dn_blk, zb), n_z // 2: pp(pick(dn_blk, 1 - zb), "fsdp", n_z // 2)}, n_z // 2),
        z,
        1,
    )

    seg = segments.reshape(full_len)
    start = jnp.sum((seg[None, :] < seg[:, None]).astype(jnp.int32), axis=1)
    offset = (jnp.arange(full_len, dtype=jnp.int32) - start).astype(F32)
    lane = jnp.arange(LANES)
    within = lane % 64
    frequency = jnp.where(
        within < HALF, jnp.exp(within.astype(F32) * (-2.0 * math.log(ROPE_BASE) / HEAD_DIM)), 0.0
    )
    angles = offset[:, None] * frequency[None, :]
    cos = jnp.cos(angles)
    sin = jnp.sin(angles) * jnp.where(lane < 64, -1.0, 1.0)[None, :]
    seg_col, seg_row = seg[:, None], seg[None, :]

    col = jnp.arange(compact)
    at = col % HEAD_DIM
    head = col // HEAD_DIM
    spot = jnp.where(head < n_q + 1, at + jnp.where(at >= HALF, 64 - HALF, 0), at) + head * LANES
    spot = jnp.where(head < n_q + 2, spot, -1)
    spread = (spot[:, None] == jnp.arange((n_q + 2) * LANES)[None, :]).astype(BF16)
    c320 = jnp.arange(q_cols)
    sel = (
        jnp.arange(n_q * LANES)[:, None]
        == ((c320 // HEAD_DIM) * LANES + c320 % HEAD_DIM)[None, :]
    ).astype(BF16)

    gain_one = w_in[:, compact - 32].astype(F32)[None, :]
    gain_two = w_in[:, compact - 31].astype(F32)[None, :]
    w_heads = dot(w_in, spread).astype(BF16)
    x_f32 = x_all.astype(F32)
    root_all = lax.rsqrt(jnp.mean(x_f32 * x_f32, axis=1, keepdims=True) + NORM_EPS)
    norm_attn = (x_f32 * root_all * gain_one).astype(BF16)
    qkv = dot(norm_attn, w_heads)
    attn, rot, stats = attend(qkv, cos, sin, seg_col, seg_row, sel, scale)
    attn_rel = by_xor(attn, 2 * n_tp, me)
    x_mine = lax.dynamic_slice_in_dim(x_here, t * rows, rows, 0).astype(F32)
    mid = x_mine + scatter_layer(attn_rel.reshape(2, 2, 2, rows, q_cols), w_o)
    root_ffn = lax.rsqrt(jnp.mean(mid * mid, axis=1, keepdims=True) + NORM_EPS)
    norm_ffn = (mid * root_ffn * gain_two).astype(BF16)

    def both(own):
        return gather_layer(own), gather_layer(pp(own, "fsdp", n_z // 2))

    dy_mine = lax.dynamic_slice_in_dim(cotangent.reshape(half_len, width), t * rows, rows, 0)
    dy_pair = both(dy_mine)
    norm_pair = both(norm_ffn)

    def mlp(norm, dy):
        norm = norm.reshape(full_len, width)
        dy = dy.reshape(full_len, width)
        gate_up = dot(norm, w_gu)
        gate, up = gate_up[:, :units], gate_up[:, units:]
        sig = jax.nn.sigmoid(gate)
        hidden = (gate * sig * up).astype(BF16)
        d_hidden = dot(dy, w_dn, ((1,), (1,)))
        d_up = (d_hidden * gate * sig).astype(BF16)
        d_gate = (d_hidden * up * sig * (1.0 + gate * (1.0 - sig))).astype(BF16)
        return hidden, jnp.concatenate([d_gate, d_up], axis=1), norm, dy

    own_mlp, far_mlp = mlp(norm_pair[0], dy_pair[0]), mlp(norm_pair[1], dy_pair[1])

    def shape8(v):
        return v.reshape(2, 2, 2, rows, v.shape[-1])

    def scatter_both(own, far, rhs, dims=((1,), (0,))):
        sent = pp(scatter_layer(shape8(far), rhs, dims).astype(BF16), "fsdp", n_z // 2)
        return scatter_layer(shape8(own), rhs, dims) + sent.astype(F32)

    d_norm = scatter_both(own_mlp[1], far_mlp[1], w_gu, ((1,), (1,)))
    ffn = scatter_both(own_mlp[0], far_mlp[0], w_dn)
    output = gather_tp((mid + ffn).astype(BF16))

    gu_g = dot(own_mlp[2], own_mlp[1], ((0,), (0,))) + dot(far_mlp[2], far_mlp[1], ((0,), (0,)))
    dn_g = dot(own_mlp[0], own_mlp[3], ((0,), (0,))) + dot(far_mlp[0], far_mlp[3], ((0,), (0,)))

    def norm_back(inputs, root, gain, d_normed):
        scaled = d_normed * gain
        return root * scaled - inputs * (root * root * root) * jnp.mean(
            scaled * inputs, axis=1, keepdims=True
        )

    d_mid = dy_mine.astype(F32) + norm_back(mid, root_ffn, gain_two, d_norm)
    d_proj = gather_layer(d_mid.astype(BF16)).reshape(full_len, width)
    o_g = dot(attn_rel.reshape(full_len, q_cols), d_proj, ((0,), (0,)))
    d_attn = dot(d_proj, w_o, ((1,), (1,))).astype(BF16)
    d_attn = by_xor(d_attn, 2 * n_tp, me).reshape(full_len, q_cols)
    d_qkv = attend_back(rot, d_attn, stats, cos, sin, seg_col, seg_row, sel, scale)
    d_rel = by_xor(d_qkv, 2 * n_tp, me)
    d_norm_attn = scatter_layer(shape8(d_rel), w_heads, ((1,), (1,)))
    root_mine = lax.rsqrt(jnp.mean(x_mine * x_mine, axis=1, keepdims=True) + NORM_EPS)
    d_in = d_mid + norm_back(x_mine, root_mine, gain_one, d_norm_attn)
    input_grad = gather_tp(d_in.astype(BF16))
    d_packed = dot(d_qkv, spread, ((1,), (1,))).astype(BF16)
    in_g = dot(norm_attn, d_packed, ((0,), (0,)))

    def to_owner_y(blocks, rows_axis):
        mine, theirs = pick(blocks, y), pick(blocks, 1 - y)
        return in_order(y, mine, pp(theirs.astype(BF16), "ctx", 1).astype(F32))

    def half_z(blocks):
        top = n_z // 2
        left = scatter_z(blocks, top)
        return in_order(zb, left[0], pp(left[top].astype(BF16), "fsdp", top).astype(F32))

    gu_two = half_z(split_z(gu_g, n_z, z, 0))
    gu_four = to_owner_y(gu_two.reshape(2, 2, depth, 2 * units).transpose(1, 0, 2, 3), 0)
    gu_four = gu_four.transpose(2, 1, 0, 3)
    gate_grad = gu_four[..., :units].reshape(depth, 4 * units)
    up_grad = gu_four[..., units:].reshape(depth, 4 * units)

    dn_two = half_z(split_z(dn_g, n_z, z, 1))
    dn_four = to_owner_y(dn_two.reshape(2, units, 2, depth).transpose(2, 0, 1, 3), 1)
    down_grad = dn_four.transpose(1, 0, 2, 3).reshape(4 * units, depth)

    o_one = scatter_z(split_z(o_g, n_z, z, 1), n_z)[0]
    o_grad = to_owner_y(o_one.reshape(q_cols, 2, depth).transpose(1, 0, 2), 1).reshape(
        2 * q_cols, depth
    )

    in_one = scatter_z(split_z(in_g, n_z, z, 0), n_z)[0]
    in_two = to_owner_y(in_one.reshape(2, depth, compact), 0)

    def columns(lo, hi):
        return jnp.concatenate([in_two[0, :, lo:hi], in_two[1, :, lo:hi]], axis=1)

    q_grad = columns(0, q_cols)
    k_grad = columns(q_cols, q_cols + kv_cols)
    v_grad = columns(q_cols + kv_cols, q_cols + 2 * kv_cols)

    def gain_sum(pairs):
        return sum(jnp.sum(w.astype(F32) * g, axis=1) for w, g in pairs)

    gains = sum_tp(
        jnp.stack(
            [
                gain_sum(((q_weight, q_grad), (k_weight, k_grad), (v_weight, v_grad))),
                gain_sum(((gate_weight, gate_grad), (up_weight, up_grad))),
            ]
        )
    ) / jnp.stack([attn_gain, ffn_gain]).astype(F32)

    return (
        output[None],
        input_grad[None],
        gains[0],
        q_grad,
        k_grad,
        v_grad,
        o_grad,
        gains[1],
        gate_grad,
        up_grad,
        down_grad,
    )


def solution(mesh):
    specs = dict(
        tok=P("fsdp", "ctx", None),
        gain=P(("fsdp", "ctx")),
        row=P(("fsdp", "ctx"), "tp"),
        col=P("tp", ("fsdp", "ctx")),
    )
    tok, gain, row, col = specs["tok"], specs["gain"], specs["row"], specs["col"]
    return jax.shard_map(
        body,
        mesh=mesh,
        in_specs=(tok, P("fsdp", None), gain, row, row, row, col, gain, row, row, col, tok),
        out_specs=(tok, tok, gain, row, row, row, col, gain, row, row, col),
        check_vma=False,
    )
```

```python
import math

import jax
import jax.numpy as jnp
from jax import lax
from jax.experimental import pallas as pl
from jax.experimental.pallas import tpu as pltpu
from jax.sharding import PartitionSpec as P

HEAD_DIM = 80
HALF = HEAD_DIM // 2
LANES = 128
NORM_EPS = 1e-05
ROPE_BASE = 10000.0
MASK_FILL = -1000000000.0
F32 = jnp.float32
BF16 = jnp.bfloat16


def pp(value, axis, mask):
    size = lax.axis_size(axis)
    return lax.ppermute(value, axis, [(i, i ^ mask) for i in range(size)])


def dot(a, b, dims=((1,), (0,))):
    return lax.dot_general(a, b, (dims, ((), ())), preferred_element_type=F32)


def in_order(bit, mine, other, axis=0):
    return jnp.where(
        bit == 0, jnp.stack([mine, other], axis), jnp.stack([other, mine], axis)
    )


def pick(blocks, index):
    return lax.dynamic_index_in_dim(blocks, index, 0, keepdims=False)


def attend_rows(scale, block, i, rot, seg_col, seg_row, sel, attn, stats):
    n_q = rot.shape[1] // LANES - 2
    rows = slice(i * block, (i + 1) * block)
    keys = (i + 1) * block
    q_pos = i * block + lax.broadcasted_iota(jnp.int32, (block, keys), 0)
    k_pos = lax.broadcasted_iota(jnp.int32, (block, keys), 1)
    allowed = (seg_col[rows, :] == seg_row[:, :keys]) & (k_pos <= q_pos)
    k = rot[:keys, n_q * LANES : (n_q + 1) * LANES]
    v = rot[:keys, (n_q + 1) * LANES :]
    outs, maxes, totals = [], [], []
    for h in range(n_q):
        s = dot(rot[rows, h * LANES : (h + 1) * LANES], k, ((1,), (1,))) * scale
        s = jnp.where(allowed, s, MASK_FILL)
        top = jnp.max(s, axis=1, keepdims=True)
        e = jnp.exp(s - top)
        total = jnp.sum(e, axis=1, keepdims=True)
        outs.append(dot((e * (1.0 / total)).astype(BF16), v).astype(BF16))
        maxes.append(top)
        totals.append(total)
    attn[rows, :] = dot(jnp.concatenate(outs, axis=1), sel[...]).astype(BF16)
    stats[rows, :] = jnp.concatenate(maxes + totals, axis=1)


def attend_back_kernel(
    scale, block, rot, d_attn, stats, cos, sin, seg_col, seg_row, sel, d_qkv, dk_sum, dv_sum
):
    full_len = rot.shape[0]
    n_q = rot.shape[1] // LANES - 2
    dk_sum[...] = jnp.zeros_like(dk_sum)
    dv_sum[...] = jnp.zeros_like(dv_sum)

    def back(u, at):
        return (u * cos[at, :] - pltpu.roll(u, 64, 1) * sin[at, :]).astype(BF16)

    for i in range(full_len // block):
        rows = slice(i * block, (i + 1) * block)
        keys = (i + 1) * block
        q_pos = i * block + lax.broadcasted_iota(jnp.int32, (block, keys), 0)
        k_pos = lax.broadcasted_iota(jnp.int32, (block, keys), 1)
        allowed = (seg_col[rows, :] == seg_row[:, :keys]) & (k_pos <= q_pos)
        k = rot[:keys, n_q * LANES : (n_q + 1) * LANES]
        v = rot[:keys, (n_q + 1) * LANES :]
        d_out = dot(d_attn[rows, :], sel[...], ((1,), (1,))).astype(BF16)
        stat = stats[rows, :]
        for h in range(n_q):
            q = rot[rows, h * LANES : (h + 1) * LANES]
            d_h = d_out[:, h * LANES : (h + 1) * LANES]
            s = dot(q, k, ((1,), (1,))) * scale
            s = jnp.where(allowed, s, MASK_FILL)
            p = jnp.exp(s - stat[:, h : h + 1]) * (1.0 / stat[:, n_q + h : n_q + h + 1])
            dv_sum[:keys, :] += dot(p.astype(BF16), d_h, ((0,), (0,)))
            d_p = dot(d_h, v, ((1,), (1,)))
            d_s = (p * (d_p - jnp.sum(p * d_p, axis=1, keepdims=True))).astype(BF16)
            d_q = (dot(d_s, k) * scale).astype(BF16).astype(F32)
            d_qkv[rows, h * LANES : (h + 1) * LANES] = back(d_q, rows)
            dk_sum[:keys, :] += dot(d_s, q, ((0,), (0,)))
    d_k = (dk_sum[...] * scale).astype(BF16).astype(F32)
    d_qkv[:, n_q * LANES : (n_q + 1) * LANES] = back(d_k, slice(None))
    d_qkv[:, (n_q + 1) * LANES :] = dv_sum[...].astype(BF16)


VMEM_LIMIT = 56 * 1024 * 1024


def attend_back(rot, d_attn, stats, cos, sin, seg_col, seg_row, sel, scale):
    full_len, width = rot.shape
    n_q = width // LANES - 2
    return pl.pallas_call(
        lambda *refs: attend_back_kernel(scale, min(256, full_len), *refs),
        out_shape=jax.ShapeDtypeStruct((full_len, width), BF16),
        scratch_shapes=[pltpu.VMEM((full_len, LANES), F32), pltpu.VMEM((full_len, LANES), F32)],
        compiler_params=pltpu.CompilerParams(vmem_limit_bytes=VMEM_LIMIT),
        cost_estimate=pl.CostEstimate(
            flops=5 * n_q * full_len * full_len * LANES,
            bytes_accessed=full_len * width * 6,
            transcendentals=n_q * full_len * full_len // 2,
        ),
        name="attend_back",
    )(rot, d_attn, stats, cos, sin, seg_col, seg_row, sel)


def gather_layer(own):
    half = own.shape[-1] // 2
    a, b = own[:, :half], own[:, half:]
    a1 = jnp.stack([a, pp(a, "tp", 2)])
    b1 = jnp.stack([b, pp(b, "ctx", 1)])
    a2 = jnp.stack([a1, pp(a1, "ctx", 1)])
    b2 = jnp.stack([b1, pp(b1, "tp", 2)], axis=1)
    mine = jnp.concatenate([a2, b2], axis=-1)
    return jnp.stack([mine, pp(mine, "tp", 1)], axis=2)


def scatter_layer(lhs, rhs, dims=((1,), (0,))):
    rows, depth = lhs.shape[-2:]

    def product(part):
        return dot(part.reshape(4 * rows, depth), rhs, dims).reshape(2, 2, rows, -1)

    sent = pp(product(lhs[:, :, 1]).astype(BF16), "tp", 1)
    kept = product(lhs[:, :, 0]) + sent.astype(F32)
    half = kept.shape[-1] // 2
    a, b = kept[..., :half], kept[..., half:]
    a1 = a[:, 0] + pp(a[:, 1].astype(BF16), "tp", 2).astype(F32)
    b1 = b[0] + pp(b[1].astype(BF16), "ctx", 1).astype(F32)
    a2 = a1[0] + pp(a1[1].astype(BF16), "ctx", 1).astype(F32)
    b2 = b1[0] + pp(b1[1].astype(BF16), "tp", 2).astype(F32)
    return jnp.concatenate([a2, b2], axis=-1)


def gather_tp(own):
    index = lax.axis_index("tp")
    pair = in_order(index // 2, own, pp(own, "tp", 2))
    return in_order(index % 2, pair, pp(pair, "tp", 1), axis=1).reshape(-1, own.shape[-1])


def sum_tp(value):
    value = value + pp(value, "tp", 1)
    return value + pp(value, "tp", 2)


def by_xor(value, parts, index):
    blocks = value.reshape(parts, -1, value.shape[-1])
    return jnp.stack([pick(blocks, index ^ r) for r in range(parts)])


def below(top):
    masks = []
    while top > 1:
        top //= 2
        masks.append(top)
    return masks


def gather_z(held, top):
    held = dict(held)
    for mask in below(top):
        for rel in list(held):
            held[rel ^ mask] = pp(held[rel], "fsdp", mask)
    return held


def place(held, index, axis):
    shape = list(next(iter(held.values())).shape)
    size = shape[axis]
    shape[axis] = size * len(held)
    out = jnp.zeros(shape, BF16)
    for rel, block in held.items():
        start = [0] * len(shape)
        start[axis] = (index ^ rel) * size
        out = lax.dynamic_update_slice(out, block, start)
    return out


def scatter_z(blocks, top):
    blocks = dict(blocks)
    for mask in reversed(below(top)):
        for rel in [r for r in blocks if r & mask]:
            blocks[rel ^ mask] = blocks[rel ^ mask] + pp(
                blocks.pop(rel).astype(BF16), "fsdp", mask
            ).astype(F32)
    return blocks


def split_z(value, n, index, axis):
    size = value.shape[axis] // n
    return {
        rel: lax.dynamic_slice_in_dim(value, (index ^ rel) * size, size, axis) for rel in range(n)
    }


def flip(index, mask):
    return index + mask * (1 - 2 * ((index // mask) % 2))


def flip_all(index, bits):
    mask = 1
    while mask <= bits:
        if bits & mask:
            index = flip(index, mask)
        mask *= 2
    return index


class Links:
    def __init__(self, send_sems, recv_sems):
        self.sems = (send_sems, recv_sems)
        self.copies = []

    def send(self, src, dst, peer):
        k = len(self.copies)
        copy = pltpu.make_async_remote_copy(
            src_ref=src,
            dst_ref=dst,
            send_sem=self.sems[0].at[k],
            recv_sem=self.sems[1].at[k],
            device_id=peer,
            device_id_type=pl.DeviceIdType.MESH,
        )
        copy.start()
        self.copies.append(copy)
        return copy

    def finish(self):
        for copy in self.copies:
            copy.wait_send()


def greet(peers):
    barrier = pltpu.get_barrier_semaphore()
    for peer in peers:
        pl.semaphore_signal(barrier, inc=1, device_id=peer, device_id_type=pl.DeviceIdType.MESH)
    pl.semaphore_wait(barrier, len(peers))


class Place:
    def __init__(self, n_z, n_tp):
        self.n_z, self.n_tp = n_z, n_tp
        self.z, self.y, self.t = (lax.axis_index(a) for a in ("fsdp", "ctx", "tp"))
        self.me = self.y * n_tp + self.t
        self.core = {"tp": flip(self.t, 1)}
        self.x = {"tp": flip(self.t, 2)}
        self.yy = {"ctx": 1 - self.y}
        self.masks = below(n_z)

    def zz(self, mask):
        return {"fsdp": flip(self.z, mask)}

    def peers(self):
        return [self.core, self.x, self.yy] + [self.zz(m) for m in self.masks]


class WeightFlow:
    def __init__(self, links, at, out, cross, first, second):
        self.links, self.at, self.out = links, at, out
        self.first, self.second = first, second
        self.got = {}
        self.y_copy = links.send(cross, second(None), at.yy)

    def own(self):
        at = self.at
        for m in at.masks:
            dst = self.out.at[at.z, at.y]
            self.got[m, 0] = self.links.send(self.first(m), dst, at.zz(m))

    def crossed(self):
        at = self.at
        self.y_copy.wait_recv()
        for m in at.masks:
            dst = self.out.at[at.z, 1 - at.y]
            self.got[m, 1] = self.links.send(self.second(m), dst, at.zz(m))

    def take(self, rel, part):
        at = self.at
        self.got[rel, part].wait_recv()
        low = rel & -rel
        row = at.y if part == 0 else 1 - at.y
        block = self.out.at[flip_all(at.z, rel), row]
        for m in at.masks:
            if m < low:
                self.got[rel ^ m, part] = self.links.send(block, block, at.zz(m))

    def order(self):
        rels = [r for r in range(1, self.at.n_z)]
        return sorted(rels, key=lambda r: (bin(r).count("1"), -(r & -r), r))


def half_rows(ref, part, rows):
    return ref.at[pl.ds(part * (rows // 2), rows // 2)]


class LayerGather:
    def __init__(self, links, at, out, rows, halves):
        self.links, self.at, self.out, self.rows = links, at, out, rows
        self.halves = halves
        self.cores = []

    def half(self, index, part):
        return half_rows(self.out.at[index], part, self.rows)

    def pass_on(self, index, part, peer):
        block = self.half(index, part)
        return self.links.send(block, block, peer)

    def own(self, part, src=None):
        at, me = self.at, self.at.me
        a = self.half(me, part)
        src = a if src is None else src
        send = lambda peer: self.links.send(src, a, peer)
        if part == 0:
            self.xa, self.ya = send(at.x), send(at.yy)
        else:
            self.yb, self.xb = send(at.yy), send(at.x)
        self.cores.append(send(at.core))

    def to_core(self, index, part):
        self.cores.append(self.pass_on(index, part, self.at.core))

    def far_first(self):
        at = self.at
        self.x_of, self.y_of = flip(at.me, 2), flip(at.me, at.n_tp)
        self.diag = flip(self.x_of, at.n_tp)
        self.xa.wait_recv()
        self.y_fwd = self.pass_on(self.x_of, 0, at.yy)
        self.to_core(self.x_of, 0)
        self.yb.wait_recv()
        self.x_fwd = self.pass_on(self.y_of, 1, at.x)
        self.to_core(self.y_of, 1)

    def far_second(self):
        self.ya.wait_recv()
        self.to_core(self.y_of, 0)
        self.xb.wait_recv()
        self.to_core(self.x_of, 1)
        self.y_fwd.wait_recv()
        self.to_core(self.diag, 0)
        self.x_fwd.wait_recv()
        self.to_core(self.diag, 1)

    def last(self):
        for copy in self.cores:
            copy.wait_recv()


class LayerSum:
    def __init__(self, links, at, rows, to_core, from_core, part, landed):
        self.links, self.at, self.rows = links, at, rows
        self.bufs = (to_core, from_core, part, landed)

    def begin(self, product):
        to_core, from_core, _, _ = self.bufs
        self.core = {}
        for k in (3, 1, 2, 0):
            to_core[k] = product(2 * k + 1).astype(BF16)
            self.core[k] = self.links.send(to_core.at[k], from_core.at[k], self.at.core)

    def middle(self, product):
        _, from_core, part, landed = self.bufs
        at, rows, h = self.at, self.rows, self.rows // 2
        a, b = slice(0, h), slice(h, rows)

        def level(k):
            value = product(2 * k)
            self.core[k].wait_recv()
            return value + from_core[k].astype(F32)

        send = lambda k, i, peer: self.links.send(
            part.at[k, pl.ds((i % 2) * h, h)], landed.at[i], peer
        )
        part[3] = level(3).astype(BF16)
        x1 = send(3, 0, at.x)
        y1 = send(3, 1, at.yy)
        one = level(1)
        part[1, a] = one[a].astype(BF16)
        x2 = send(1, 2, at.x)
        two = level(2)
        part[2, b] = two[b].astype(BF16)
        y2 = send(2, 3, at.yy)
        zero = level(0)
        x1.wait_recv()
        part[2, a] = (two[a] + landed[0].astype(F32)).astype(BF16)
        y3 = send(2, 4, at.yy)
        y1.wait_recv()
        part[1, b] = (one[b] + landed[1].astype(F32)).astype(BF16)
        x3 = send(1, 5, at.x)
        self.zero, self.tail = zero, (x2, y3, y2, x3)

    def end(self):
        _, _, _, landed = self.bufs
        h = self.rows // 2
        for copy in self.tail:
            copy.wait_recv()
        zero = self.zero
        top = zero[:h] + landed[2].astype(F32) + landed[4].astype(F32)
        low = zero[h:] + landed[3].astype(F32) + landed[5].astype(F32)
        return top, low


def sum_scratch(rows, width):
    return [
        pltpu.VMEM((4, rows, width), BF16),
        pltpu.VMEM((4, rows, width), BF16),
        pltpu.VMEM((4, rows, width), BF16),
        pltpu.VMEM((6, rows // 2, width), BF16),
    ]


def front_kernel(
    n_z, n_tp, scale, q_block,
    x_here, dy_here, in_send, o_send, w3_send, cos, sin, seg_col, seg_row, spread, sel,
    w_heads, w_o, w3, gains, norm_attn, dy_all, norm_all, attn, rot, stats, mid,
    w_in, x_all, qkv, to_core, from_core, part, landed, in_cross, o_cross, w3_cross,
    heads_v, norm_v, own_v, root_v, o_v, send_sems, recv_sems, sems,
):
    at = Place(n_z, n_tp)
    links = Links(send_sems, recv_sems)
    z, y, t, me = at.z, at.y, at.t, at.me
    zb = z // (n_z // 2)
    n_b, rows, width = 2 * n_tp, x_all.shape[0] // (2 * n_tp), x_all.shape[1]
    depth = in_send.shape[1]
    full_len = x_all.shape[0]
    local = []

    def move(src, dst):
        copy = pltpu.make_async_copy(src, dst, sems.at[len(local)])
        copy.start()
        local.append(copy)
        return copy

    def block_of(ref, index):
        return ref.at[pl.ds(pl.multiple_of(index * rows, rows), rows)]

    greet(at.peers())
    f_in = WeightFlow(
        links, at, w_in, in_send.at[1 - y], lambda m: in_send.at[y], lambda m: in_cross
    )
    f_in.own()
    own_in = move(in_send.at[y], w_in.at[z, y])
    x_mine = block_of(x_here, t)
    tok_y = links.send(x_mine, block_of(x_all, me), at.yy)
    x_own = move(x_here, x_all.at[pl.ds(pl.multiple_of(y * (full_len // 2), full_len // 2), full_len // 2)])
    dy_mine = block_of(dy_here, t)
    dy_own = move(dy_here.reshape(n_tp, rows, width), dy_all.at[0, pl.ds(y * n_tp, n_tp)])

    f_in.crossed()
    cross_in = move(in_cross, w_in.at[z, 1 - y])
    f_o = WeightFlow(
        links, at, w_o, o_send.at[1 - y], lambda m: o_send.at[y], lambda m: o_cross
    )
    top = n_z // 2
    f_3 = WeightFlow(
        links, at, w3, w3_send.at[1 - y],
        lambda m: w3_send.at[y, 1 - zb if m == top else zb],
        lambda m: w3_cross if m is None else w3_cross.at[1 - zb if m == top else zb],
    )
    dy_y = links.send(dy_mine, dy_all.at[0, me], at.yy)
    tok_y.wait_recv()
    y_of, x_of = flip(me, n_tp), flip(me, 2)
    y_block = block_of(x_all, y_of)
    tok_x = links.send(y_block, y_block, at.x)
    tok_c = [links.send(y_block, y_block, at.core)]
    ins = [(rel, p) for rel in f_in.order() for p in (0, 1)]
    for rel, p in ins:
        if rel == top:
            f_in.take(rel, p)
    tok_x.wait_recv()
    diag = block_of(x_all, flip(y_of, 2))
    tok_c.append(links.send(diag, diag, at.core))
    x_own.wait()

    for copy in tok_c:
        copy.wait_recv()

    step = min(256, full_len)

    def find_root(c, carry):
        at_rows = pl.ds(pl.multiple_of(c * step, step), step)
        value = x_all[at_rows, :].astype(F32)
        root_v[at_rows, :] = lax.rsqrt(jnp.mean(value * value, axis=1, keepdims=True) + NORM_EPS)
        return carry

    lax.fori_loop(0, full_len // step, find_root, 0)
    own_in.wait()
    cross_in.wait()

    pick_gain = (
        lax.broadcasted_iota(jnp.int32, (8, w_in.shape[3]), 1)
        == sel.shape[1] // HEAD_DIM * HEAD_DIM + 2 * HEAD_DIM + lax.broadcasted_iota(jnp.int32, (8, w_in.shape[3]), 0)
    ).astype(F32).astype(BF16)

    group = 1
    while 2 * depth * group % LANES:
        group *= 2
    span = 2 * depth * group

    def project(rel, first):
        owner = flip_all(z, rel) // group
        cols = pl.ds(pl.multiple_of(owner * span, span), span)
        weights = w_in[pl.ds(owner * group, group)].reshape(span, w_in.shape[3])
        gain = dot(pick_gain, weights, ((1,), (1,)))
        gains[:, cols] = gain
        heads = dot(weights, spread[...]).astype(BF16)
        heads_v[cols, :] = heads

        def some_rows(c, carry):
            at_rows = pl.ds(pl.multiple_of(c * step, step), step)
            value = (x_all[at_rows, cols].astype(F32) * root_v[at_rows, :] * gain[0:1, :]).astype(BF16)
            norm_v[at_rows, cols] = value
            term = dot(value, heads)
            qkv[at_rows, :] = term if first else qkv[at_rows, :] + term
            return carry

        lax.fori_loop(0, full_len // step, some_rows, 0)

    f_o.own()
    f_o.crossed()
    if group == 1:
        project(0, True)
    f_3.own()
    f_3.crossed()
    for rel in f_in.order():
        for p in (0, 1):
            if rel != top:
                f_in.take(rel, p)
        if group == 1:
            project(rel, False)
    if group > 1:
        for rel in range(0, n_z, group):
            project(rel, rel == 0)
    heads_out = move(heads_v, w_heads)
    norm_out = move(norm_v, norm_attn)
    own_o = [move(o_send.at[y], w_o.at[z, y]), move(o_cross, w_o.at[z, 1 - y])]
    own_3 = [move(w3_send.at[y, zb], w3.at[z, y]), move(w3_cross.at[zb], w3.at[z, 1 - y])]
    dy_y.wait_recv()
    dy_x = links.send(dy_all.at[0, y_of], dy_all.at[0, y_of], at.x)
    dy_c = [links.send(dy_all.at[0, y_of], dy_all.at[0, y_of], at.core)]
    dy_z = [
        links.send(half_rows(dy_mine, p, rows), half_rows(dy_all.at[1, me], p, rows), at.zz(top))
        for p in (0, 1)
    ]
    for p in (0, 1):
        f_o.take(top, p)

    n_q = rot.shape[1] // LANES - 2

    def turn(c, carry):
        r = pl.ds(pl.multiple_of(c * step, step), step)
        for h in range(n_q + 1):
            u = qkv[r, h * LANES : (h + 1) * LANES]
            rot[r, h * LANES : (h + 1) * LANES] = (
                u * cos[r, :] + pltpu.roll(u, 64, 1) * sin[r, :]
            ).astype(BF16)
        rot[r, (n_q + 1) * LANES :] = qkv[r, (n_q + 1) * LANES :].astype(BF16)
        return carry

    lax.fori_loop(0, full_len // step, turn, 0)
    dy_far = LayerGather(links, at, dy_all.at[1], rows, True)
    for i in range(full_len // q_block):
        attend_rows(scale, q_block, i, rot, seg_col, seg_row, sel, attn, stats)
        if i == 0:
            dy_x.wait_recv()
            d_of = flip(y_of, 2)
            dy_c.append(links.send(dy_all.at[0, d_of], dy_all.at[0, d_of], at.core))
    for rel in f_o.order():
        for p in (0, 1):
            if rel != top:
                f_o.take(rel, p)
    for copy in own_o:
        copy.wait()
    load_o = move(w_o, o_v)
    load_o.wait()

    layer = LayerSum(links, at, rows, to_core, from_core, part, landed)

    def product(r):
        lhs = attn[pl.ds(pl.multiple_of(flip_all(me, r) * rows, rows), rows), :]
        return dot(lhs, o_v[...].reshape(width, o_v.shape[3]), ((1,), (1,)))

    layer.begin(product)
    layer.middle(product)
    for p in (0, 1):
        f_3.take(top, p)
    norm_own = LayerGather(links, at, norm_all.at[0], rows, True)
    norm_far = LayerGather(links, at, norm_all.at[1], rows, True)
    far = []
    h = rows // 2
    load_x = move(x_mine, own_v)
    load_x.wait()
    for p, value in enumerate(layer.end()):
        r = slice(p * h, (p + 1) * h)
        value = value + own_v[r, :].astype(F32)
        mid[r, :] = value
        root = lax.rsqrt(jnp.mean(value * value, axis=1, keepdims=True) + NORM_EPS)
        own_v[r, :] = (value * root * gains[1:2, :]).astype(BF16)
        src = own_v.at[pl.ds(p * h, h)]
        far.append(links.send(src, half_rows(norm_all.at[1, me], p, rows), at.zz(top)))
        norm_own.own(p, src)
    keep = move(own_v, norm_all.at[0, me])
    for p in (0, 1):
        dy_z[p].wait_recv()
        dy_far.own(p)
    norm_own.far_first()
    for p in (0, 1):
        far[p].wait_recv()
        norm_far.own(p)
    norm_own.far_second()
    dy_far.far_first()
    norm_far.far_first()
    dy_far.far_second()
    norm_far.far_second()
    for rel in f_3.order():
        for p in (0, 1):
            if rel != top:
                f_3.take(rel, p)
    for gather in (norm_own, dy_far, norm_far):
        gather.last()
    for copy in dy_c:
        copy.wait_recv()
    for copy in [dy_own, heads_out, norm_out, keep] + own_3:
        copy.wait()
    links.finish()


def front(n_z, n_tp, scale, x_here, dy_here, in_send, o_send, w3_send, cos, sin, seg_col, seg_row, spread, sel):
    half_len, width = x_here.shape
    full_len = 2 * half_len
    rows = half_len // n_tp
    depth, compact = in_send.shape[1:]
    heads = spread.shape[1]
    q_cols = sel.shape[1]
    n_q = heads // LANES - 2
    w3_cols = w3_send.shape[3]
    any_, vmem = pl.BlockSpec(memory_space=pl.ANY), pl.BlockSpec(memory_space=pltpu.VMEM)
    n_sems = 80 + 6 * n_z + 32
    shape = jax.ShapeDtypeStruct
    return pl.pallas_call(
        lambda *refs: front_kernel(n_z, n_tp, scale, min(256, full_len), *refs),
        out_shape=(
            shape((width, heads), BF16),
            shape((n_z, 2, depth, q_cols), BF16),
            shape((n_z, 2, depth, w3_cols), BF16),
            shape((8, width), F32),
            shape((full_len, width), BF16),
            shape((2, 2 * n_tp, rows, width), BF16),
            shape((2, 2 * n_tp, rows, width), BF16),
            shape((full_len, q_cols), BF16),
            shape((full_len, heads), BF16),
            shape((full_len, 2 * n_q), F32),
            shape((rows, width), F32),
        ),
        in_specs=[any_] * 5 + [vmem] * 6,
        out_specs=(any_, any_, any_, vmem, any_, any_, any_, vmem, vmem, vmem, vmem),
        scratch_shapes=[
            pltpu.VMEM((n_z, 2, depth, compact), BF16),
            pltpu.VMEM((full_len, width), BF16),
            pltpu.VMEM((full_len, heads), F32),
            *sum_scratch(rows, width),
            pltpu.VMEM((depth, compact), BF16),
            pltpu.VMEM((depth, q_cols), BF16),
            pltpu.VMEM((2, depth, w3_cols), BF16),
            pltpu.VMEM((width, heads), BF16),
            pltpu.VMEM((full_len, width), BF16),
            pltpu.VMEM((rows, width), BF16),
            pltpu.VMEM((full_len, 1), F32),
            pltpu.VMEM((n_z, 2, depth, q_cols), BF16),
            pltpu.SemaphoreType.DMA((n_sems,)),
            pltpu.SemaphoreType.DMA((n_sems,)),
            pltpu.SemaphoreType.DMA((16,)),
        ],
        compiler_params=pltpu.CompilerParams(
            collective_id=1, has_side_effects=True, vmem_limit_bytes=VMEM_LIMIT
        ),
        name="front",
    )(x_here, dy_here, in_send, o_send, w3_send, cos, sin, seg_col, seg_row, spread, sel)


def body(
    tokens,
    segments,
    attn_gain,
    q_weight,
    k_weight,
    v_weight,
    o_weight,
    ffn_gain,
    gate_weight,
    up_weight,
    down_weight,
    cotangent,
):
    n_z = lax.axis_size("fsdp")
    n_tp = lax.axis_size("tp")
    z, y, t = lax.axis_index("fsdp"), lax.axis_index("ctx"), lax.axis_index("tp")
    zb = z // (n_z // 2)
    _, half_len, width = tokens.shape
    full_len = segments.shape[1]
    rows = half_len // n_tp
    depth = q_weight.shape[0]
    q_cols = q_weight.shape[1] // 2
    kv_cols = k_weight.shape[1] // 2
    units = gate_weight.shape[1] // 4
    n_q = q_cols // HEAD_DIM
    scale = HEAD_DIM ** (-0.5)
    me = y * n_tp + t

    def two(w):
        return w.reshape(w.shape[0], 2, -1).transpose(1, 0, 2)

    extra = jnp.stack([attn_gain, ffn_gain], axis=1)
    extra = jnp.broadcast_to(jnp.pad(extra, ((0, 0), (0, 30)))[None], (2, depth, 32))
    in_send = jnp.concatenate([two(q_weight), two(k_weight), two(v_weight), extra], axis=2)
    compact = in_send.shape[2]
    o_send = o_weight.reshape(2, q_cols, depth).transpose(0, 2, 1)

    def four(w):
        return w.reshape(depth, 2, 2, units).transpose(2, 1, 0, 3)

    wide = -(-2 * units // LANES) * LANES
    w3_send = jnp.concatenate(
        [
            four(gate_weight),
            four(up_weight),
            jnp.zeros((2, 2, depth, wide - 2 * units), BF16),
            down_weight.reshape(2, 2, units, depth).transpose(1, 0, 3, 2),
        ],
        axis=3,
    )
    x_here = tokens.reshape(half_len, width)

    seg = segments.reshape(full_len)
    start = jnp.sum((seg[None, :] < seg[:, None]).astype(jnp.int32), axis=1)
    offset = (jnp.arange(full_len, dtype=jnp.int32) - start).astype(F32)
    lane = jnp.arange(LANES)
    within = lane % 64
    frequency = jnp.where(
        within < HALF, jnp.exp(within.astype(F32) * (-2.0 * math.log(ROPE_BASE) / HEAD_DIM)), 0.0
    )
    angles = offset[:, None] * frequency[None, :]
    cos = jnp.cos(angles)
    sin = jnp.sin(angles) * jnp.where(lane < 64, -1.0, 1.0)[None, :]
    seg_col, seg_row = seg[:, None], seg[None, :]

    col = jnp.arange(compact)
    at = col % HEAD_DIM
    head = col // HEAD_DIM
    spot = jnp.where(head < n_q + 1, at + jnp.where(at >= HALF, 64 - HALF, 0), at) + head * LANES
    spot = jnp.where(head < n_q + 2, spot, -1)
    spread = (spot[:, None] == jnp.arange((n_q + 2) * LANES)[None, :]).astype(BF16)
    c320 = jnp.arange(q_cols)
    sel = (
        jnp.arange(n_q * LANES)[:, None]
        == ((c320 // HEAD_DIM) * LANES + c320 % HEAD_DIM)[None, :]
    ).astype(BF16)

    w_heads, w_o, w3, gains, norm_attn, dy_all, norm_all, attn, rot, stats, mid = front(
        n_z, n_tp, scale, x_here, cotangent.reshape(half_len, width), in_send, o_send, w3_send,
        cos, sin, seg_col, seg_row, spread, sel,
    )
    gain_one, gain_two = gains[0:1], gains[1:2]
    w_o = w_o.reshape(width, q_cols)
    w3 = w3.reshape(width, -1)
    w_gu, w_dn = w3[:, : 2 * units], w3[:, wide:]
    x_mine = lax.dynamic_slice_in_dim(x_here, t * rows, rows, 0).astype(F32)
    root_ffn = lax.rsqrt(jnp.mean(mid * mid, axis=1, keepdims=True) + NORM_EPS)
    dy_mine = lax.dynamic_slice_in_dim(cotangent.reshape(half_len, width), t * rows, rows, 0)
    attn_rel = by_xor(attn, 2 * n_tp, me)

    def mlp(norm, dy):
        norm = norm.reshape(full_len, width)
        dy = dy.reshape(full_len, width)
        gate_up = dot(norm, w_gu)
        gate, up = gate_up[:, :units], gate_up[:, units:]
        sig = jax.nn.sigmoid(gate)
        hidden = (gate * sig * up).astype(BF16)
        d_hidden = dot(dy, w_dn)
        d_up = (d_hidden * gate * sig).astype(BF16)
        d_gate = (d_hidden * up * sig * (1.0 + gate * (1.0 - sig))).astype(BF16)
        return hidden, jnp.concatenate([d_gate, d_up], axis=1), norm, dy

    own_mlp, far_mlp = mlp(norm_all[0], dy_all[0]), mlp(norm_all[1], dy_all[1])

    def shape8(v):
        return by_xor(v, 2 * n_tp, me).reshape(2, 2, 2, rows, v.shape[-1])

    def scatter_both(own, far, rhs, dims=((1,), (0,))):
        sent = pp(scatter_layer(shape8(far), rhs, dims).astype(BF16), "fsdp", n_z // 2)
        return scatter_layer(shape8(own), rhs, dims) + sent.astype(F32)

    d_norm = scatter_both(own_mlp[1], far_mlp[1], w_gu, ((1,), (1,)))
    ffn = scatter_both(own_mlp[0], far_mlp[0], w_dn, ((1,), (1,)))
    output = gather_tp((mid + ffn).astype(BF16))

    gu_g = dot(own_mlp[2], own_mlp[1], ((0,), (0,))) + dot(far_mlp[2], far_mlp[1], ((0,), (0,)))
    dn_g = dot(own_mlp[3], own_mlp[0], ((0,), (0,))) + dot(far_mlp[3], far_mlp[0], ((0,), (0,)))

    def norm_back(inputs, root, gain, d_normed):
        scaled = d_normed * gain
        return root * scaled - inputs * (root * root * root) * jnp.mean(
            scaled * inputs, axis=1, keepdims=True
        )

    d_mid = dy_mine.astype(F32) + norm_back(mid, root_ffn, gain_two, d_norm)
    d_proj = gather_layer(d_mid.astype(BF16)).reshape(full_len, width)
    o_g = dot(d_proj, attn_rel.reshape(full_len, q_cols), ((0,), (0,)))
    d_attn = dot(d_proj, w_o).astype(BF16)
    d_attn = by_xor(d_attn, 2 * n_tp, me).reshape(full_len, q_cols)
    d_qkv = attend_back(rot, d_attn, stats, cos, sin, seg_col, seg_row, sel, scale)
    d_norm_attn = scatter_layer(shape8(d_qkv), w_heads, ((1,), (1,)))
    root_mine = lax.rsqrt(jnp.mean(x_mine * x_mine, axis=1, keepdims=True) + NORM_EPS)
    d_in = d_mid + norm_back(x_mine, root_mine, gain_one, d_norm_attn)
    input_grad = gather_tp(d_in.astype(BF16))
    d_packed = dot(d_qkv, spread, ((1,), (1,))).astype(BF16)
    in_g = dot(norm_attn, d_packed, ((0,), (0,)))

    def to_owner_y(blocks, rows_axis):
        mine, theirs = pick(blocks, y), pick(blocks, 1 - y)
        return in_order(y, mine, pp(theirs.astype(BF16), "ctx", 1).astype(F32))

    def half_z(blocks):
        top = n_z // 2
        left = scatter_z(blocks, top)
        return in_order(zb, left[0], pp(left[top].astype(BF16), "fsdp", top).astype(F32))

    gu_two = half_z(split_z(gu_g, n_z, z, 0))
    gu_four = to_owner_y(gu_two.reshape(2, 2, depth, 2 * units).transpose(1, 0, 2, 3), 0)
    gu_four = gu_four.transpose(2, 1, 0, 3)
    gate_grad = gu_four[..., :units].reshape(depth, 4 * units)
    up_grad = gu_four[..., units:].reshape(depth, 4 * units)

    dn_two = half_z(split_z(dn_g, n_z, z, 0))
    dn_four = to_owner_y(dn_two.reshape(2, 2, depth, units).transpose(1, 0, 2, 3), 0)
    down_grad = dn_four.transpose(1, 0, 3, 2).reshape(4 * units, depth)

    o_one = scatter_z(split_z(o_g, n_z, z, 0), n_z)[0]
    o_grad = to_owner_y(o_one.reshape(2, depth, q_cols), 0).transpose(0, 2, 1).reshape(
        2 * q_cols, depth
    )

    in_one = scatter_z(split_z(in_g, n_z, z, 0), n_z)[0]
    in_two = to_owner_y(in_one.reshape(2, depth, compact), 0)

    def columns(lo, hi):
        return jnp.concatenate([in_two[0, :, lo:hi], in_two[1, :, lo:hi]], axis=1)

    q_grad = columns(0, q_cols)
    k_grad = columns(q_cols, q_cols + kv_cols)
    v_grad = columns(q_cols + kv_cols, q_cols + 2 * kv_cols)

    def gain_sum(pairs):
        return sum(jnp.sum(w.astype(F32) * g, axis=1) for w, g in pairs)

    gains = sum_tp(
        jnp.stack(
            [
                gain_sum(((q_weight, q_grad), (k_weight, k_grad), (v_weight, v_grad))),
                gain_sum(((gate_weight, gate_grad), (up_weight, up_grad))),
            ]
        )
    ) / jnp.stack([attn_gain, ffn_gain]).astype(F32)

    return (
        output[None],
        input_grad[None],
        gains[0],
        q_grad,
        k_grad,
        v_grad,
        o_grad,
        gains[1],
        gate_grad,
        up_grad,
        down_grad,
    )


def solution(mesh):
    specs = dict(
        tok=P("fsdp", "ctx", None),
        gain=P(("fsdp", "ctx")),
        row=P(("fsdp", "ctx"), "tp"),
        col=P("tp", ("fsdp", "ctx")),
    )
    tok, gain, row, col = specs["tok"], specs["gain"], specs["row"], specs["col"]
    return jax.shard_map(
        body,
        mesh=mesh,
        in_specs=(tok, P("fsdp", None), gain, row, row, row, col, gain, row, row, col, tok),
        out_specs=(tok, tok, gain, row, row, row, col, gain, row, row, col),
        check_vma=False,
    )
```

```python
import math

import jax
import jax.numpy as jnp
from jax import lax
from jax.experimental import pallas as pl
from jax.experimental.pallas import tpu as pltpu
from jax.sharding import PartitionSpec as P

HEAD_DIM = 80
HALF = HEAD_DIM // 2
LANES = 128
NORM_EPS = 1e-05
ROPE_BASE = 10000.0
MASK_FILL = -1000000000.0
F32 = jnp.float32
BF16 = jnp.bfloat16


def pp(value, axis, mask):
    size = lax.axis_size(axis)
    return lax.ppermute(value, axis, [(i, i ^ mask) for i in range(size)])


def dot(a, b, dims=((1,), (0,))):
    return lax.dot_general(a, b, (dims, ((), ())), preferred_element_type=F32)


def in_order(bit, mine, other, axis=0):
    return jnp.where(
        bit == 0, jnp.stack([mine, other], axis), jnp.stack([other, mine], axis)
    )


def pick(blocks, index):
    return lax.dynamic_index_in_dim(blocks, index, 0, keepdims=False)


def attend_rows(scale, block, i, rot, seg_col, seg_row, sel, attn, stats):
    n_q = rot.shape[1] // LANES - 2
    rows = slice(i * block, (i + 1) * block)
    keys = (i + 1) * block
    q_pos = i * block + lax.broadcasted_iota(jnp.int32, (block, keys), 0)
    k_pos = lax.broadcasted_iota(jnp.int32, (block, keys), 1)
    allowed = (seg_col[rows, :] == seg_row[:, :keys]) & (k_pos <= q_pos)
    k = rot[:keys, n_q * LANES : (n_q + 1) * LANES]
    v = rot[:keys, (n_q + 1) * LANES :]
    outs, maxes, totals = [], [], []
    for h in range(n_q):
        s = dot(rot[rows, h * LANES : (h + 1) * LANES], k, ((1,), (1,))) * scale
        s = jnp.where(allowed, s, MASK_FILL)
        top = jnp.max(s, axis=1, keepdims=True)
        e = jnp.exp(s - top)
        total = jnp.sum(e, axis=1, keepdims=True)
        outs.append(dot((e * (1.0 / total)).astype(BF16), v).astype(BF16))
        maxes.append(top)
        totals.append(total)
    attn[rows, :] = dot(jnp.concatenate(outs, axis=1), sel[...]).astype(BF16)
    stats[rows, :] = jnp.concatenate(maxes + totals, axis=1)


def turn_back(u, cos, sin, rows):
    return (u * cos[rows, :] - pltpu.roll(u, 64, 1) * sin[rows, :]).astype(BF16)


def attend_back_rows(
    scale, block, i, rot, d_attn, stats, cos, sin, seg_col, seg_row, sel, d_qkv, dk_sum, dv_sum
):
    n_q = rot.shape[1] // LANES - 2
    rows = slice(i * block, (i + 1) * block)
    keys = (i + 1) * block
    q_pos = i * block + lax.broadcasted_iota(jnp.int32, (block, keys), 0)
    k_pos = lax.broadcasted_iota(jnp.int32, (block, keys), 1)
    allowed = (seg_col[rows, :] == seg_row[:, :keys]) & (k_pos <= q_pos)
    k = rot[:keys, n_q * LANES : (n_q + 1) * LANES]
    v = rot[:keys, (n_q + 1) * LANES :]
    d_out = dot(d_attn[rows, :], sel[...], ((1,), (1,))).astype(BF16)
    stat = stats[rows, :]
    for h in range(n_q):
        q = rot[rows, h * LANES : (h + 1) * LANES]
        d_h = d_out[:, h * LANES : (h + 1) * LANES]
        s = dot(q, k, ((1,), (1,))) * scale
        s = jnp.where(allowed, s, MASK_FILL)
        p = jnp.exp(s - stat[:, h : h + 1]) * (1.0 / stat[:, n_q + h : n_q + h + 1])
        dv_sum[:keys, :] += dot(p.astype(BF16), d_h, ((0,), (0,)))
        d_p = dot(d_h, v, ((1,), (1,)))
        d_s = (p * (d_p - jnp.sum(p * d_p, axis=1, keepdims=True))).astype(BF16)
        d_q = (dot(d_s, k) * scale).astype(BF16).astype(F32)
        d_qkv[rows, h * LANES : (h + 1) * LANES] = turn_back(d_q, cos, sin, rows)
        dk_sum[:keys, :] += dot(d_s, q, ((0,), (0,)))


def attend_back_keys(scale, n_q, cos, sin, d_qkv, dk_sum, dv_sum):
    d_k = (dk_sum[...] * scale).astype(BF16).astype(F32)
    d_qkv[:, n_q * LANES : (n_q + 1) * LANES] = turn_back(d_k, cos, sin, slice(None))
    d_qkv[:, (n_q + 1) * LANES :] = dv_sum[...].astype(BF16)


VMEM_LIMIT = 56 * 1024 * 1024
BACK_LIMIT = 62 * 1024 * 1024


def sum_tp(value):
    value = value + pp(value, "tp", 1)
    return value + pp(value, "tp", 2)


def below(top):
    masks = []
    while top > 1:
        top //= 2
        masks.append(top)
    return masks


def flip(index, mask):
    return index + mask * (1 - 2 * ((index // mask) % 2))


def flip_all(index, bits):
    mask = 1
    while mask <= bits:
        if bits & mask:
            index = flip(index, mask)
        mask *= 2
    return index


class Links:
    def __init__(self, send_sems, recv_sems):
        self.sems = (send_sems, recv_sems)
        self.copies = []
        self.count = 0

    def send(self, src, dst, peer, kept=False):
        k = self.count
        self.count += 1
        copy = pltpu.make_async_remote_copy(
            src_ref=src,
            dst_ref=dst,
            send_sem=self.sems[0].at[k],
            recv_sem=self.sems[1].at[k],
            device_id=peer,
            device_id_type=pl.DeviceIdType.MESH,
        )
        copy.start()
        if not kept:
            self.copies.append(copy)
        return copy

    def finish(self, *sums):
        for copy in self.copies:
            copy.wait_send()
        for layer in sums:
            layer.drain()


def greet(peers):
    barrier = pltpu.get_barrier_semaphore()
    for peer in peers:
        pl.semaphore_signal(barrier, inc=1, device_id=peer, device_id_type=pl.DeviceIdType.MESH)
    pl.semaphore_wait(barrier, len(peers))


class Place:
    def __init__(self, n_z, n_tp):
        self.n_z, self.n_tp = n_z, n_tp
        self.z, self.y, self.t = (lax.axis_index(a) for a in ("fsdp", "ctx", "tp"))
        self.me = self.y * n_tp + self.t
        self.core = {"tp": flip(self.t, 1)}
        self.x = {"tp": flip(self.t, 2)}
        self.yy = {"ctx": 1 - self.y}
        self.masks = below(n_z)
        self.zb = self.z // (n_z // 2)

    def zz(self, mask):
        return {"fsdp": flip(self.z, mask)}

    def peers(self):
        return [self.core, self.x, self.yy] + [self.zz(m) for m in self.masks]


class WeightFlow:
    def __init__(self, links, at, out, cross, first, second):
        self.links, self.at, self.out = links, at, out
        self.first, self.second = first, second
        self.got = {}
        self.y_copy = links.send(cross, second(None), at.yy)

    def own(self):
        at = self.at
        for m in at.masks:
            dst = self.out.at[at.z, at.y]
            self.got[m, 0] = self.links.send(self.first(m), dst, at.zz(m))

    def crossed(self):
        at = self.at
        self.y_copy.wait_recv()
        for m in at.masks:
            dst = self.out.at[at.z, 1 - at.y]
            self.got[m, 1] = self.links.send(self.second(m), dst, at.zz(m))

    def take(self, rel, part):
        at = self.at
        self.got[rel, part].wait_recv()
        low = rel & -rel
        row = at.y if part == 0 else 1 - at.y
        block = self.out.at[flip_all(at.z, rel), row]
        for m in at.masks:
            if m < low:
                self.got[rel ^ m, part] = self.links.send(block, block, at.zz(m))

    def order(self):
        rels = [r for r in range(1, self.at.n_z)]
        return sorted(rels, key=lambda r: (bin(r).count("1"), -(r & -r), r))


def half_rows(ref, part, rows):
    return ref.at[pl.ds(part * (rows // 2), rows // 2)]


class LayerGather:
    def __init__(self, links, at, out, rows):
        self.links, self.at, self.out, self.rows = links, at, out, rows
        self.cores = []
        self.sent = []

    def half(self, index, part):
        return half_rows(self.out.at[index], part, self.rows)

    def send(self, src, dst, peer):
        self.sent.append(self.links.send(src, dst, peer, kept=True))
        return self.sent[-1]

    def pass_on(self, index, part, peer):
        block = self.half(index, part)
        return self.send(block, block, peer)

    def own(self, part, src=None):
        at, me = self.at, self.at.me
        a = self.half(me, part)
        src = a if src is None else src
        send = lambda peer: self.send(src, a, peer)
        if part == 0:
            self.xa, self.ya = send(at.x), send(at.yy)
        else:
            self.yb, self.xb = send(at.yy), send(at.x)
        self.cores.append(send(at.core))

    def to_core(self, index, part):
        self.cores.append(self.pass_on(index, part, self.at.core))

    def far_first(self):
        at = self.at
        self.x_of, self.y_of = flip(at.me, 2), flip(at.me, at.n_tp)
        self.diag = flip(self.x_of, at.n_tp)
        self.xa.wait_recv()
        self.y_fwd = self.pass_on(self.x_of, 0, at.yy)
        self.to_core(self.x_of, 0)
        self.yb.wait_recv()
        self.x_fwd = self.pass_on(self.y_of, 1, at.x)
        self.to_core(self.y_of, 1)

    def far_second(self):
        self.ya.wait_recv()
        self.to_core(self.y_of, 0)
        self.xb.wait_recv()
        self.to_core(self.x_of, 1)
        self.y_fwd.wait_recv()
        self.to_core(self.diag, 0)
        self.x_fwd.wait_recv()
        self.to_core(self.diag, 1)

    def last(self):
        for copy in self.cores:
            copy.wait_recv()

    def drain(self):
        for copy in self.sent:
            copy.wait_send()


class LayerSum:
    def __init__(self, links, at, rows, bufs, product, after=None):
        self.links, self.at, self.rows = links, at, rows
        self.to_core, self.held, self.landed, self.total, self.free = bufs
        self.product = product
        self.after = after

    def peers(self):
        return (self.at.core, self.at.x, self.at.yy)

    def tiles(self, some):
        width = self.total.shape[1]
        tile = 512 if width % 512 == 0 else width

        def body(c, carry):
            some(pl.ds(pl.multiple_of(c * tile, tile), tile))
            return carry

        lax.fori_loop(0, width // tile, body, 0)

    def drain(self):
        for copy in self.sent:
            copy.wait_send()
        self.sent = []

    def release(self):
        self.drain()
        for i, peer in enumerate(self.peers()):
            pl.semaphore_signal(
                self.free.at[i], inc=1, device_id=peer, device_id_type=pl.DeviceIdType.MESH
            )

    def begin(self):
        self.core = {}
        if self.after is not None:
            self.after.drain()
            for i in range(3):
                pl.semaphore_wait(self.free.at[i], 1)
        sent = []
        for i, k in enumerate((3, 1, 2, 0)):
            if i >= 2:
                sent[i - 2].wait_send()


            def some(cols, i=i, k=k):
                self.to_core[i % 2, :, cols] = self.product(2 * k + 1, cols).astype(BF16)

            self.tiles(some)
            self.core[k] = self.links.send(
                self.to_core.at[i % 2], self.held.at[k], self.at.core, kept=True
            )
            sent.append(self.core[k])
        self.sent = sent[2:]

    def middle(self):
        at, rows, h = self.at, self.rows, self.rows // 2
        held, landed = self.held, self.landed
        a, b = slice(0, h), slice(h, rows)

        def level(k):
            self.core[k].wait_recv()

            def some(cols):
                value = self.product(2 * k, cols) + held[k, :, cols].astype(F32)
                if k == 0:
                    self.total[:, cols] = value
                else:
                    held[k, :, cols] = value.astype(BF16)

            self.tiles(some)

        def send(k, i, peer):
            copy = self.links.send(held.at[k, pl.ds((i % 2) * h, h)], landed.at[i], peer, kept=True)
            self.sent.append(copy)
            return copy

        level(3)
        x1 = send(3, 0, at.x)
        y1 = send(3, 1, at.yy)
        level(1)
        x2 = send(1, 2, at.x)
        level(2)
        y2 = send(2, 3, at.yy)
        level(0)
        x1.wait_recv()
        held[2, a] = (held[2, a].astype(F32) + landed[0].astype(F32)).astype(BF16)
        y3 = send(2, 4, at.yy)
        y1.wait_recv()
        held[1, b] = (held[1, b].astype(F32) + landed[1].astype(F32)).astype(BF16)
        x3 = send(1, 5, at.x)
        self.tail = (x2, y3, y2, x3)

    def end(self):
        h = self.rows // 2
        landed, total = self.landed, self.total
        for copy in self.tail:
            copy.wait_recv()
        top = total[:h, :] + landed[2].astype(F32) + landed[4].astype(F32)
        low = total[h:, :] + landed[3].astype(F32) + landed[5].astype(F32)
        return top, low


def sum_scratch(rows, width):
    return [
        pltpu.VMEM((2, rows, width), BF16),
        pltpu.VMEM((4, rows, width), BF16),
        pltpu.VMEM((6, rows // 2, width), BF16),
        pltpu.VMEM((rows, width), F32),
        pltpu.SemaphoreType.REGULAR((3,)),
    ]


def front_kernel(
    n_z, n_tp, scale, q_block,
    x_here, dy_here, in_send, o_send, w3_send, cos, sin, seg_col, seg_row, spread, sel,
    w_heads, w_o, w3, gains, norm_attn, dy_all, norm_all, attn, rot, stats, mid,
    w_in, x_all, qkv, to_core, held, landed, total, free, in_cross, o_cross, w3_cross,
    heads_v, norm_v, own_v, root_v, o_v, send_sems, recv_sems, sems,
):
    at = Place(n_z, n_tp)
    links = Links(send_sems, recv_sems)
    z, y, t, me = at.z, at.y, at.t, at.me
    zb = z // (n_z // 2)
    n_b, rows, width = 2 * n_tp, x_all.shape[0] // (2 * n_tp), x_all.shape[1]
    depth = in_send.shape[1]
    full_len = x_all.shape[0]
    local = []

    def move(src, dst):
        copy = pltpu.make_async_copy(src, dst, sems.at[len(local)])
        copy.start()
        local.append(copy)
        return copy

    def block_of(ref, index):
        return ref.at[pl.ds(pl.multiple_of(index * rows, rows), rows)]

    greet(at.peers())
    f_in = WeightFlow(
        links, at, w_in, in_send.at[1 - y], lambda m: in_send.at[y], lambda m: in_cross
    )
    f_in.own()
    own_in = move(in_send.at[y], w_in.at[z, y])
    x_mine = block_of(x_here, t)
    tok_y = links.send(x_mine, block_of(x_all, me), at.yy)
    x_own = move(x_here, x_all.at[pl.ds(pl.multiple_of(y * (full_len // 2), full_len // 2), full_len // 2)])
    dy_mine = block_of(dy_here, t)
    dy_own = move(dy_here.reshape(n_tp, rows, width), dy_all.at[0, pl.ds(y * n_tp, n_tp)])

    f_in.crossed()
    cross_in = move(in_cross, w_in.at[z, 1 - y])
    f_o = WeightFlow(
        links, at, w_o, o_send.at[1 - y], lambda m: o_send.at[y], lambda m: o_cross
    )
    top = n_z // 2
    f_3 = WeightFlow(
        links, at, w3, w3_send.at[1 - y],
        lambda m: w3_send.at[y, 1 - zb if m == top else zb],
        lambda m: w3_cross if m is None else w3_cross.at[1 - zb if m == top else zb],
    )
    dy_y = links.send(dy_mine, dy_all.at[0, me], at.yy)
    tok_y.wait_recv()
    y_of, x_of = flip(me, n_tp), flip(me, 2)
    y_block = block_of(x_all, y_of)
    tok_x = links.send(y_block, y_block, at.x)
    tok_c = [links.send(y_block, y_block, at.core)]
    ins = [(rel, p) for rel in f_in.order() for p in (0, 1)]
    for rel, p in ins:
        if rel == top:
            f_in.take(rel, p)
    tok_x.wait_recv()
    diag = block_of(x_all, flip(y_of, 2))
    tok_c.append(links.send(diag, diag, at.core))
    x_own.wait()

    for copy in tok_c:
        copy.wait_recv()

    step = min(256, full_len)

    def find_root(c, carry):
        at_rows = pl.ds(pl.multiple_of(c * step, step), step)
        value = x_all[at_rows, :].astype(F32)
        root_v[at_rows, :] = lax.rsqrt(jnp.mean(value * value, axis=1, keepdims=True) + NORM_EPS)
        return carry

    lax.fori_loop(0, full_len // step, find_root, 0)
    own_in.wait()
    cross_in.wait()

    pick_gain = (
        lax.broadcasted_iota(jnp.int32, (8, w_in.shape[3]), 1)
        == sel.shape[1] // HEAD_DIM * HEAD_DIM + 2 * HEAD_DIM + lax.broadcasted_iota(jnp.int32, (8, w_in.shape[3]), 0)
    ).astype(F32).astype(BF16)

    group = 1
    while 2 * depth * group % LANES:
        group *= 2
    span = 2 * depth * group

    def project(rel, first):
        owner = flip_all(z, rel) // group
        cols = pl.ds(pl.multiple_of(owner * span, span), span)
        weights = w_in[pl.ds(owner * group, group)].reshape(span, w_in.shape[3])
        gain = dot(pick_gain, weights, ((1,), (1,)))
        gains[:, cols] = gain
        heads = dot(weights, spread[...]).astype(BF16)
        heads_v[cols, :] = heads

        def some_rows(c, carry):
            at_rows = pl.ds(pl.multiple_of(c * step, step), step)
            value = (x_all[at_rows, cols].astype(F32) * root_v[at_rows, :] * gain[0:1, :]).astype(BF16)
            norm_v[at_rows, cols] = value
            term = dot(value, heads)
            qkv[at_rows, :] = term if first else qkv[at_rows, :] + term
            return carry

        lax.fori_loop(0, full_len // step, some_rows, 0)

    f_o.own()
    f_o.crossed()
    if group == 1:
        project(0, True)
    f_3.own()
    f_3.crossed()
    for rel in f_in.order():
        for p in (0, 1):
            if rel != top:
                f_in.take(rel, p)
        if group == 1:
            project(rel, False)
    if group > 1:
        for rel in range(0, n_z, group):
            project(rel, rel == 0)
    heads_out = move(heads_v, w_heads)
    norm_out = move(norm_v, norm_attn)
    own_o = [move(o_send.at[y], w_o.at[z, y]), move(o_cross, w_o.at[z, 1 - y])]
    own_3 = [move(w3_send.at[y, zb], w3.at[z, y]), move(w3_cross.at[zb], w3.at[z, 1 - y])]
    dy_y.wait_recv()
    dy_x = links.send(dy_all.at[0, y_of], dy_all.at[0, y_of], at.x)
    dy_c = [links.send(dy_all.at[0, y_of], dy_all.at[0, y_of], at.core)]
    dy_z = [
        links.send(half_rows(dy_mine, p, rows), half_rows(dy_all.at[1, me], p, rows), at.zz(top))
        for p in (0, 1)
    ]
    for p in (0, 1):
        f_o.take(top, p)

    n_q = rot.shape[1] // LANES - 2

    def turn(c, carry):
        r = pl.ds(pl.multiple_of(c * step, step), step)
        for h in range(n_q + 1):
            u = qkv[r, h * LANES : (h + 1) * LANES]
            rot[r, h * LANES : (h + 1) * LANES] = (
                u * cos[r, :] + pltpu.roll(u, 64, 1) * sin[r, :]
            ).astype(BF16)
        rot[r, (n_q + 1) * LANES :] = qkv[r, (n_q + 1) * LANES :].astype(BF16)
        return carry

    lax.fori_loop(0, full_len // step, turn, 0)
    dy_far = LayerGather(links, at, dy_all.at[1], rows)
    for i in range(full_len // q_block):
        attend_rows(scale, q_block, i, rot, seg_col, seg_row, sel, attn, stats)
        if i == 0:
            dy_x.wait_recv()
            d_of = flip(y_of, 2)
            dy_c.append(links.send(dy_all.at[0, d_of], dy_all.at[0, d_of], at.core))
    for rel in f_o.order():
        for p in (0, 1):
            if rel != top:
                f_o.take(rel, p)
    for copy in own_o:
        copy.wait()
    load_o = move(w_o.reshape(width, o_v.shape[1]), o_v)
    load_o.wait()

    def product(r, cols):
        lhs = attn[pl.ds(pl.multiple_of(flip_all(me, r) * rows, rows), rows), :]
        return dot(lhs, o_v[cols, :], ((1,), (1,)))

    layer = LayerSum(links, at, rows, (to_core, held, landed, total, free), product)
    layer.begin()
    layer.middle()
    for p in (0, 1):
        f_3.take(top, p)
    norm_own = LayerGather(links, at, norm_all.at[0], rows)
    norm_far = LayerGather(links, at, norm_all.at[1], rows)
    far = []
    h = rows // 2
    load_x = move(x_mine, own_v)
    load_x.wait()
    for p, value in enumerate(layer.end()):
        r = slice(p * h, (p + 1) * h)
        value = value + own_v[r, :].astype(F32)
        mid[r, :] = value
        root = lax.rsqrt(jnp.mean(value * value, axis=1, keepdims=True) + NORM_EPS)
        own_v[r, :] = (value * root * gains[1:2, :]).astype(BF16)
        src = own_v.at[pl.ds(p * h, h)]
        far.append(links.send(src, half_rows(norm_all.at[1, me], p, rows), at.zz(top)))
        norm_own.own(p, src)
    keep = move(own_v, norm_all.at[0, me])
    for p in (0, 1):
        dy_z[p].wait_recv()
        dy_far.own(p)
    norm_own.far_first()
    for p in (0, 1):
        far[p].wait_recv()
        norm_far.own(p)
    norm_own.far_second()
    dy_far.far_first()
    norm_far.far_first()
    dy_far.far_second()
    norm_far.far_second()
    for rel in f_3.order():
        for p in (0, 1):
            if rel != top:
                f_3.take(rel, p)
    for gather in (norm_own, dy_far, norm_far):
        gather.last()
        gather.drain()
    for copy in dy_c:
        copy.wait_recv()
    for copy in [dy_own, heads_out, norm_out, keep] + own_3:
        copy.wait()
    links.finish(layer)


def front(n_z, n_tp, scale, x_here, dy_here, in_send, o_send, w3_send, cos, sin, seg_col, seg_row, spread, sel):
    half_len, width = x_here.shape
    full_len = 2 * half_len
    rows = half_len // n_tp
    depth, compact = in_send.shape[1:]
    heads = spread.shape[1]
    q_cols = sel.shape[1]
    n_q = heads // LANES - 2
    w3_cols = w3_send.shape[3]
    any_, vmem = pl.BlockSpec(memory_space=pl.ANY), pl.BlockSpec(memory_space=pltpu.VMEM)
    n_sems = 80 + 6 * n_z + 32
    shape = jax.ShapeDtypeStruct
    return pl.pallas_call(
        lambda *refs: front_kernel(n_z, n_tp, scale, min(256, full_len), *refs),
        out_shape=(
            shape((width, heads), BF16),
            shape((n_z, 2, depth, q_cols), BF16),
            shape((n_z, 2, depth, w3_cols), BF16),
            shape((8, width), F32),
            shape((full_len, width), BF16),
            shape((2, 2 * n_tp, rows, width), BF16),
            shape((2, 2 * n_tp, rows, width), BF16),
            shape((full_len, q_cols), BF16),
            shape((full_len, heads), BF16),
            shape((full_len, 2 * n_q), F32),
            shape((rows, width), F32),
        ),
        in_specs=[any_] * 5 + [vmem] * 6,
        out_specs=(any_, any_, any_, vmem, any_, any_, any_, vmem, vmem, vmem, vmem),
        scratch_shapes=[
            pltpu.VMEM((n_z, 2, depth, compact), BF16),
            pltpu.VMEM((full_len, width), BF16),
            pltpu.VMEM((full_len, heads), F32),
            *sum_scratch(rows, width),
            pltpu.VMEM((depth, compact), BF16),
            pltpu.VMEM((depth, q_cols), BF16),
            pltpu.VMEM((2, depth, w3_cols), BF16),
            pltpu.VMEM((width, heads), BF16),
            pltpu.VMEM((full_len, width), BF16),
            pltpu.VMEM((rows, width), BF16),
            pltpu.VMEM((full_len, 1), F32),
            pltpu.VMEM((width, q_cols), BF16),
            pltpu.SemaphoreType.DMA((n_sems,)),
            pltpu.SemaphoreType.DMA((n_sems,)),
            pltpu.SemaphoreType.DMA((16,)),
        ],
        compiler_params=pltpu.CompilerParams(
            collective_id=1, has_side_effects=True, vmem_limit_bytes=VMEM_LIMIT
        ),
        name="front",
    )(x_here, dy_here, in_send, o_send, w3_send, cos, sin, seg_col, seg_row, spread, sel)


class TpGather:
    def __init__(self, links, at, out):
        self.links, self.at, self.out = links, at, out

    def own(self, src):
        at = self.at
        dst = self.out.at[at.t]
        self.x = self.links.send(src, dst, at.x)
        self.cores = [self.links.send(src, dst, at.core)]

    def second(self):
        at = self.at
        self.x.wait_recv()
        block = self.out.at[flip(at.t, 2)]
        self.cores.append(self.links.send(block, block, at.core))

    def last(self):
        for copy in self.cores:
            copy.wait_recv()


class GradFlow:
    def __init__(self, links, at, src, land, swap, out, passing, fetch=None):
        self.links, self.at, self.src, self.land = links, at, src, land
        self.swap, self.out, self.passing, self.fetch = swap, out, passing, fetch
        self.adds = [m for m in reversed(at.masks) if not (swap and m == at.n_z // 2)]
        self.slot = {}
        n = 0
        for m in self.adds:
            for rel in range(0, at.n_z, 2 * m):
                self.slot[m, rel] = n
                n += 1
        self.got = {}
        self.at_mask = {}

    def row(self, part):
        return self.at.y if part == 0 else 1 - self.at.y

    def own(self, rel, part):
        return self.src.at[flip_all(self.at.z, rel), self.row(part)]

    def held(self, rel, part):
        m = self.at_mask.get((rel, part))
        if m is None:
            return self.own(rel, part), True
        return self.land.at[self.slot[m, rel], part], False

    def send(self, m, rel, part):
        block, _ = self.held(rel, part)
        self.got[m, rel ^ m, part] = self.links.send(
            block, self.land.at[self.slot[m, rel ^ m], part], self.at.zz(m)
        )

    def first(self, parts=(1, 0)):
        m = self.adds[0]
        rels = [r for r in range(self.at.n_z) if r & m]
        for rel in sorted(rels, reverse=True):
            for part in parts:
                self.send(m, rel, part)

    def add(self, m, rel, part):
        block, is_first = self.held(rel, part)
        if is_first and self.fetch is not None:
            block = self.fetch(block)
        self.got[m, rel, part].wait_recv()
        slot = self.land.at[self.slot[m, rel], part]
        slot[...] = (block[...].astype(F32) + slot[...].astype(F32)).astype(BF16)
        self.at_mask[rel, part] = m

    def spread(self):
        at = self.at
        for i, m in enumerate(self.adds):
            left = range(0, at.n_z, 2 * m)
            nxt = self.adds[i + 1] if i + 1 < len(self.adds) else (2 * m if self.swap else None)
            for rel in sorted(left, key=lambda r: -(r & (nxt or 0))):
                for part in (1, 0):
                    self.add(m, rel, part)
                    if nxt is not None and rel & nxt:
                        if nxt in self.adds:
                            self.send(nxt, rel, part)
                        else:
                            self.exchange(nxt, rel, part)

    def column(self, mine):
        return self.at.zb if mine else 1 - self.at.zb

    def exchange(self, m, rel, part):
        block, _ = self.held(rel, part)
        if part == 0:
            dst = self.out.at[self.at.zb, self.at.y]
        else:
            dst = self.passing
        self.got[m, 0, part] = self.links.send(block, dst, self.at.zz(m))

    def cross(self):
        at = self.at
        block, _ = self.held(0, 1)
        dst = self.out.at[at.zb, at.y] if self.swap else self.out.at[at.y]
        self.ends = [self.links.send(block, dst, at.yy)]

    def cross_far(self):
        at = self.at
        self.got[at.n_z // 2, 0, 1].wait_recv()
        self.ends.append(self.links.send(self.passing, self.out.at[1 - at.zb, at.y], at.yy))
        self.ends.append(self.got[at.n_z // 2, 0, 0])

    def mine(self):
        at = self.at
        dst = self.out.at[at.zb, at.y] if self.swap else self.out.at[at.y]
        return self.held(0, 0)[0], dst

    def last(self):
        for copy in self.ends:
            copy.wait_recv()


def back_kernel(
    n_z, n_tp, scale, q_block, units, wide,
    x_here, dy_here, w3, d_gu, hidden, gu_src, dn_src, w_o, w_heads, norm_attn,
    mid, gains, rot, attn, stats, cos, sin, seg_col, seg_row, sel, spread,
    output, input_grad, gu_out, dn_out, o_out, in_out,
    w3_v, gu_v, hid_v,
    to_core_a, held_a, landed_a, total_a, free_a, to_core_b, held_b, landed_b, total_b, free_b,
    far_v, far_in, d_mid, row_v, d_proj, d_attn, d_qkv, dk_sum, dv_sum, o_v,
    gu_land, gu_pass, dn_land, dn_pass, fetch_gu, fetch_dn, o_land, in_land,
    send_sems, recv_sems, sems,
):
    at = Place(n_z, n_tp)
    links = Links(send_sems, recv_sems)
    z, y, t, me = at.z, at.y, at.t, at.me
    top = n_z // 2
    n_b, rows, width = 2 * n_tp, mid.shape[0], mid.shape[1]
    depth = gu_src.shape[2]
    full_len = rot.shape[0]
    h = rows // 2
    n_q = rot.shape[1] // LANES - 2
    local = []

    def move(src, dst):
        copy = pltpu.make_async_copy(src, dst, sems.at[len(local)])
        copy.start()
        local.append(copy)
        return copy

    load_w3 = move(w3, w3_v)
    load_gu, load_hid = move(d_gu, gu_v), move(hidden, hid_v)
    load_o = move(w_o, o_v)
    load_x = move(x_here.at[pl.ds(pl.multiple_of(t * rows, rows), rows)], row_v.at[0])
    load_dy = move(dy_here.at[pl.ds(pl.multiple_of(t * rows, rows), rows)], row_v.at[1])
    greet(at.peers())

    def fetch_with(buf):
        def fetch(block):
            move(block, buf).wait()
            return buf

        return fetch

    f_gu = GradFlow(links, at, gu_src, gu_land, True, gu_out, gu_pass, fetch_with(fetch_gu))
    f_dn = GradFlow(links, at, dn_src, dn_land, True, dn_out, dn_pass, fetch_with(fetch_dn))
    f_gu.first()

    def term(seq, lhs, lo, hi):
        def product(r, cols):
            return dot(lhs[seq, flip_all(me, r)], w3_v[cols, lo:hi], ((1,), (1,)))

        return product

    bufs_a = (to_core_a, held_a, landed_a, total_a, free_a)
    bufs_b = (to_core_b, held_b, landed_b, total_b, free_b)
    load_w3.wait()
    load_gu.wait()
    far = LayerSum(links, at, rows, bufs_a, term(1, gu_v, 0, 2 * units))
    own = LayerSum(links, at, rows, bufs_b, term(0, gu_v, 0, 2 * units))
    far.begin()
    far.middle()
    own.begin()

    def send_far(layer, i):
        sent = []
        for p, value in enumerate(layer.end()):
            far_v[i, pl.ds(p * h, h), :] = value.astype(BF16)
            sent.append(
                links.send(
                    half_rows(far_v.at[i], p, rows), half_rows(far_in.at[i], p, rows), at.zz(top),
                    kept=True,
                )
            )
        layer.release()
        return sent

    sent_far = send_far(far, 0)
    own.middle()
    heads_v = w3_v.at[:, : w_heads.shape[1]]
    load_heads = move(w_heads, heads_v)
    f_dn.first()
    load_hid.wait()
    ffn_far = LayerSum(links, at, rows, bufs_a, term(1, hid_v, wide, wide + units), far)
    ffn_own = LayerSum(links, at, rows, bufs_b, term(0, hid_v, wide, wide + units), own)
    ffn_far.begin()

    def norm_back(inputs, gain, d_normed):
        root = lax.rsqrt(jnp.mean(inputs * inputs, axis=1, keepdims=True) + NORM_EPS)
        scaled = d_normed * gain
        return root * scaled - inputs * (root * root * root) * jnp.mean(
            scaled * inputs, axis=1, keepdims=True
        )

    load_x.wait()
    load_dy.wait()
    gather = LayerGather(links, at, d_proj, rows)
    for p, value in enumerate(own.end()):
        r = slice(p * h, (p + 1) * h)
        sent_far[p].wait_recv()
        value = value + far_in[0, r, :].astype(F32)
        value = row_v[1, r, :].astype(F32) + norm_back(mid[r, :], gains[1:2, :], value)
        d_mid[r, :] = value
        d_proj[me, r, :] = value.astype(BF16)
        gather.own(p)
    own.release()
    gather.far_first()
    ffn_own.begin()
    f_gu.spread()
    gather.far_second()
    ffn_far.middle()
    f_dn.spread()
    gather.last()

    load_o.wait()
    w_o_all = o_v[...].reshape(width, o_v.shape[3])

    def d_attn_rows(b, carry):
        r = pl.ds(pl.multiple_of(b * rows, rows), rows)
        d_attn[r, :] = dot(d_proj[b], w_o_all).astype(BF16)
        return carry

    lax.fori_loop(0, n_b, d_attn_rows, 0)

    group = 1
    while 2 * depth * group % LANES:
        group *= 2
    span = 2 * depth * group

    def groups():
        rels = sorted(range(0, n_z, group), key=lambda r: (-(r & 1), -r))
        return [flip_all(z, r) // group for r in rels]

    def span_of(owner):
        return pl.ds(pl.multiple_of(owner * span, span), span)

    o_src = o_v
    f_o = GradFlow(links, at, o_src, o_land, False, o_out, None)
    for owner in groups():
        lhs = jnp.concatenate([d_proj[b, :, span_of(owner)] for b in range(n_b)], axis=0)
        value = dot(lhs, attn[...], ((0,), (0,))).astype(BF16)
        o_src[pl.ds(owner * group, group)] = value.reshape(group, 2, depth, value.shape[1])
    f_o.first()
    gather.drain()
    load_norm = move(norm_attn, d_proj)
    ffn_own.middle()
    dk_sum[...] = jnp.zeros_like(dk_sum)
    dv_sum[...] = jnp.zeros_like(dv_sum)
    for i in range(full_len // q_block):
        attend_back_rows(
            scale, q_block, i, rot, d_attn, stats, cos, sin, seg_col, seg_row, sel, d_qkv, dk_sum, dv_sum
        )
        if i == 0:
            f_gu.cross()
            f_dn.cross()
            sent_ffn = send_far(ffn_far, 1)
        if i == 1:
            f_o.spread()
            f_o.cross()
    attend_back_keys(scale, n_q, cos, sin, d_qkv, dk_sum, dv_sum)

    load_heads.wait()

    def d_term(r, cols):
        value = d_qkv[pl.ds(pl.multiple_of(flip_all(me, r) * rows, rows), rows), :]
        return dot(value, w3_v[cols, : w_heads.shape[1]], ((1,), (1,)))

    d_in = LayerSum(links, at, rows, bufs_a, d_term, ffn_far)
    d_in.begin()
    d_in.middle()
    in_cols = slice(w_heads.shape[1], w_heads.shape[1] + spread.shape[0])
    in_src = w3_v.reshape(n_z, 2, depth, w3_v.shape[1]).at[:, :, :, in_cols]
    f_in = GradFlow(links, at, in_src, in_land, False, in_out, None)
    packed = dot(d_qkv[...], spread[...], ((1,), (1,))).astype(BF16)
    load_norm.wait()
    for owner in groups():
        lhs = jnp.concatenate([d_proj[b, :, span_of(owner)] for b in range(n_b)], axis=0)
        w3_v[span_of(owner), in_cols] = dot(lhs, packed, ((0,), (0,))).astype(BF16)
    f_in.first()
    out_g, in_g = TpGather(links, at, output), TpGather(links, at, input_grad)
    stay = []
    for p, value in enumerate(d_in.end()):
        r = slice(p * h, (p + 1) * h)
        value = d_mid[r, :] + norm_back(row_v[0, r, :].astype(F32), gains[0:1, :], value)
        row_v[1, r, :] = value.astype(BF16)
    in_g.own(row_v.at[1])
    stay.append(move(row_v.at[1], input_grad.at[t]))
    for copy in sent_far:
        copy.wait_send()
    for p, value in enumerate(ffn_own.end()):
        r = slice(p * h, (p + 1) * h)
        sent_ffn[p].wait_recv()
        value = value + far_in[1, r, :].astype(F32)
        far_v[0, r, :] = (mid[r, :] + value).astype(BF16)
    out_g.own(far_v.at[0])
    stay.append(move(far_v.at[0], output.at[t]))
    f_in.spread()
    f_in.cross()
    f_gu.cross_far()
    f_dn.cross_far()
    for flow in (f_gu, f_dn, f_o, f_in):
        stay.append(move(*flow.mine()))
    in_g.second()
    out_g.second()
    for flow in (in_g, out_g, f_gu, f_dn, f_o, f_in):
        flow.last()
    for copy in stay:
        copy.wait()
    for copy in sent_ffn:
        copy.wait_send()
    links.finish(d_in, ffn_own)


def back(n_z, n_tp, scale, units, wide, *args):
    x_here, w_heads, spread, mid, sel = args[0], args[8], args[20], args[10], args[19]
    d_gu, hidden, gu_src, dn_src, w3, w_o, rot = args[3], args[4], args[5], args[6], args[2], args[7], args[12]
    half_len, width = x_here.shape
    rows = mid.shape[0]
    full_len = 2 * half_len
    depth = gu_src.shape[2]
    heads, compact = w_heads.shape[1], spread.shape[0]
    q_cols = sel.shape[1]
    any_, vmem = pl.BlockSpec(memory_space=pl.ANY), pl.BlockSpec(memory_space=pltpu.VMEM)
    shape = jax.ShapeDtypeStruct
    n_swap, n_add = max(1, n_z - 2), n_z - 1
    n_sems = 120 + 8 * n_z
    return pl.pallas_call(
        lambda *refs: back_kernel(n_z, n_tp, scale, min(256, full_len), units, wide, *refs),
        out_shape=(
            shape((n_tp, rows, width), BF16),
            shape((n_tp, rows, width), BF16),
            shape((2, 2, depth, 2 * units), BF16),
            shape((2, 2, depth, units), BF16),
            shape((2, depth, q_cols), BF16),
            shape((2, depth, compact), BF16),
        ),
        in_specs=[any_] * 10 + [vmem] * 11,
        out_specs=(any_,) * 6,
        scratch_shapes=[
            pltpu.VMEM(w3.shape, BF16),
            pltpu.VMEM(d_gu.shape, BF16),
            pltpu.VMEM(hidden.shape, BF16),
            *sum_scratch(rows, width),
            *sum_scratch(rows, width),
            pltpu.VMEM((2, rows, width), BF16),
            pltpu.VMEM((2, rows, width), BF16),
            pltpu.VMEM((rows, width), F32),
            pltpu.VMEM((2, rows, width), BF16),
            pltpu.VMEM((2 * n_tp, rows, width), BF16),
            pltpu.VMEM((full_len, q_cols), BF16),
            pltpu.VMEM((full_len, heads), BF16),
            pltpu.VMEM((full_len, LANES), F32),
            pltpu.VMEM((full_len, LANES), F32),
            pltpu.VMEM(w_o.shape, BF16),
            pltpu.VMEM((n_swap, 2, depth, 2 * units), BF16),
            pltpu.VMEM((depth, 2 * units), BF16),
            pltpu.VMEM((n_swap, 2, depth, units), BF16),
            pltpu.VMEM((depth, units), BF16),
            pltpu.VMEM((depth, 2 * units), BF16),
            pltpu.VMEM((depth, units), BF16),
            pltpu.VMEM((n_add, 2, depth, q_cols), BF16),
            pltpu.VMEM((n_add, 2, depth, compact), BF16),
            pltpu.SemaphoreType.DMA((n_sems,)),
            pltpu.SemaphoreType.DMA((n_sems,)),
            pltpu.SemaphoreType.DMA((24 + 6 * n_z,)),
        ],
        compiler_params=pltpu.CompilerParams(
            collective_id=2, has_side_effects=True, vmem_limit_bytes=BACK_LIMIT
        ),
        name="back",
    )(*args)


def body(
    tokens,
    segments,
    attn_gain,
    q_weight,
    k_weight,
    v_weight,
    o_weight,
    ffn_gain,
    gate_weight,
    up_weight,
    down_weight,
    cotangent,
):
    n_z = lax.axis_size("fsdp")
    n_tp = lax.axis_size("tp")
    z, y, t = lax.axis_index("fsdp"), lax.axis_index("ctx"), lax.axis_index("tp")
    zb = z // (n_z // 2)
    _, half_len, width = tokens.shape
    full_len = segments.shape[1]
    rows = half_len // n_tp
    depth = q_weight.shape[0]
    q_cols = q_weight.shape[1] // 2
    kv_cols = k_weight.shape[1] // 2
    units = gate_weight.shape[1] // 4
    n_q = q_cols // HEAD_DIM
    scale = HEAD_DIM ** (-0.5)
    me = y * n_tp + t

    def two(w):
        return w.reshape(w.shape[0], 2, -1).transpose(1, 0, 2)

    extra = jnp.stack([attn_gain, ffn_gain], axis=1)
    extra = jnp.broadcast_to(jnp.pad(extra, ((0, 0), (0, 30)))[None], (2, depth, 32))
    in_send = jnp.concatenate([two(q_weight), two(k_weight), two(v_weight), extra], axis=2)
    compact = in_send.shape[2]
    o_send = o_weight.reshape(2, q_cols, depth).transpose(0, 2, 1)

    def four(w):
        return w.reshape(depth, 2, 2, units).transpose(2, 1, 0, 3)

    wide = -(-2 * units // LANES) * LANES
    w3_send = jnp.concatenate(
        [
            four(gate_weight),
            four(up_weight),
            jnp.zeros((2, 2, depth, wide - 2 * units), BF16),
            down_weight.reshape(2, 2, units, depth).transpose(1, 0, 3, 2),
        ],
        axis=3,
    )
    x_here = tokens.reshape(half_len, width)

    seg = segments.reshape(full_len)
    start = jnp.sum((seg[None, :] < seg[:, None]).astype(jnp.int32), axis=1)
    offset = (jnp.arange(full_len, dtype=jnp.int32) - start).astype(F32)
    lane = jnp.arange(LANES)
    within = lane % 64
    frequency = jnp.where(
        within < HALF, jnp.exp(within.astype(F32) * (-2.0 * math.log(ROPE_BASE) / HEAD_DIM)), 0.0
    )
    angles = offset[:, None] * frequency[None, :]
    cos = jnp.cos(angles)
    sin = jnp.sin(angles) * jnp.where(lane < 64, -1.0, 1.0)[None, :]
    seg_col, seg_row = seg[:, None], seg[None, :]

    col = jnp.arange(compact)
    at = col % HEAD_DIM
    head = col // HEAD_DIM
    spot = jnp.where(head < n_q + 1, at + jnp.where(at >= HALF, 64 - HALF, 0), at) + head * LANES
    spot = jnp.where(head < n_q + 2, spot, -1)
    spread = (spot[:, None] == jnp.arange((n_q + 2) * LANES)[None, :]).astype(BF16)
    c320 = jnp.arange(q_cols)
    sel = (
        jnp.arange(n_q * LANES)[:, None]
        == ((c320 // HEAD_DIM) * LANES + c320 % HEAD_DIM)[None, :]
    ).astype(BF16)

    w_heads, w_o, w3, gains, norm_attn, dy_all, norm_all, attn, rot, stats, mid = front(
        n_z, n_tp, scale, x_here, cotangent.reshape(half_len, width), in_send, o_send, w3_send,
        cos, sin, seg_col, seg_row, spread, sel,
    )
    w3 = w3.reshape(width, -1)
    w_gu, w_dn = w3[:, : 2 * units], w3[:, wide:]

    def mlp(norm, dy):
        norm = norm.reshape(full_len, width)
        dy = dy.reshape(full_len, width)
        gate_up = dot(norm, w_gu)
        gate, up = gate_up[:, :units], gate_up[:, units:]
        sig = jax.nn.sigmoid(gate)
        hidden = (gate * sig * up).astype(BF16)
        d_hidden = dot(dy, w_dn)
        d_up = (d_hidden * gate * sig).astype(BF16)
        d_gate = (d_hidden * up * sig * (1.0 + gate * (1.0 - sig))).astype(BF16)
        return hidden, jnp.concatenate([d_gate, d_up], axis=1), norm, dy

    own_mlp, far_mlp = mlp(norm_all[0], dy_all[0]), mlp(norm_all[1], dy_all[1])

    gu_g = dot(own_mlp[2], own_mlp[1], ((0,), (0,))) + dot(far_mlp[2], far_mlp[1], ((0,), (0,)))
    dn_g = dot(own_mlp[3], own_mlp[0], ((0,), (0,))) + dot(far_mlp[3], far_mlp[0], ((0,), (0,)))

    def blocks(own, far):
        return jnp.stack([own, far]).reshape(2, 2 * n_tp, rows, own.shape[1])

    output, input_grad, gu_four, dn_four, o_two, in_two = back(
        n_z, n_tp, scale, units, wide,
        x_here, cotangent.reshape(half_len, width), w3, blocks(own_mlp[1], far_mlp[1]),
        blocks(own_mlp[0], far_mlp[0]),
        gu_g.astype(BF16).reshape(n_z, 2, depth, 2 * units),
        dn_g.astype(BF16).reshape(n_z, 2, depth, units),
        w_o, w_heads, norm_attn.reshape(2 * n_tp, rows, width),
        mid, gains, rot, attn, stats, cos, sin, seg_col, seg_row, sel, spread,
    )
    gu_four = gu_four.astype(F32).transpose(2, 0, 1, 3)
    gate_grad = gu_four[..., :units].reshape(depth, 4 * units)
    up_grad = gu_four[..., units:].reshape(depth, 4 * units)
    down_grad = dn_four.astype(F32).transpose(0, 1, 3, 2).reshape(4 * units, depth)
    o_grad = o_two.astype(F32).transpose(0, 2, 1).reshape(2 * q_cols, depth)
    in_two = in_two.astype(F32)

    def columns(lo, hi):
        return jnp.concatenate([in_two[0, :, lo:hi], in_two[1, :, lo:hi]], axis=1)

    q_grad = columns(0, q_cols)
    k_grad = columns(q_cols, q_cols + kv_cols)
    v_grad = columns(q_cols + kv_cols, q_cols + 2 * kv_cols)

    def gain_sum(pairs):
        return sum(jnp.sum(w.astype(F32) * g, axis=1) for w, g in pairs)

    gains = sum_tp(
        jnp.stack(
            [
                gain_sum(((q_weight, q_grad), (k_weight, k_grad), (v_weight, v_grad))),
                gain_sum(((gate_weight, gate_grad), (up_weight, up_grad))),
            ]
        )
    ) / jnp.stack([attn_gain, ffn_gain]).astype(F32)

    return (
        output.reshape(tokens.shape),
        input_grad.reshape(tokens.shape),
        gains[0],
        q_grad,
        k_grad,
        v_grad,
        o_grad,
        gains[1],
        gate_grad,
        up_grad,
        down_grad,
    )


def solution(mesh):
    specs = dict(
        tok=P("fsdp", "ctx", None),
        gain=P(("fsdp", "ctx")),
        row=P(("fsdp", "ctx"), "tp"),
        col=P("tp", ("fsdp", "ctx")),
    )
    tok, gain, row, col = specs["tok"], specs["gain"], specs["row"], specs["col"]
    return jax.shard_map(
        body,
        mesh=mesh,
        in_specs=(tok, P("fsdp", None), gain, row, row, row, col, gain, row, row, col, tok),
        out_specs=(tok, tok, gain, row, row, row, col, gain, row, row, col),
        check_vma=False,
    )
```

```python
import math

import jax
import jax.numpy as jnp
from jax import lax
from jax.experimental import pallas as pl
from jax.experimental.pallas import tpu as pltpu
from jax.sharding import PartitionSpec as P

HEAD_DIM = 80
HALF = HEAD_DIM // 2
LANES = 128
NORM_EPS = 1e-05
ROPE_BASE = 10000.0
MASK_FILL = -1000000000.0
F32 = jnp.float32
BF16 = jnp.bfloat16


def pp(value, axis, mask):
    size = lax.axis_size(axis)
    return lax.ppermute(value, axis, [(i, i ^ mask) for i in range(size)])


def dot(a, b, dims=((1,), (0,))):
    return lax.dot_general(a, b, (dims, ((), ())), preferred_element_type=F32)


def in_order(bit, mine, other, axis=0):
    return jnp.where(
        bit == 0, jnp.stack([mine, other], axis), jnp.stack([other, mine], axis)
    )


def pick(blocks, index):
    return lax.dynamic_index_in_dim(blocks, index, 0, keepdims=False)


def attend_rows(scale, block, i, rot, seg_col, seg_row, sel, attn, stats):
    n_q = rot.shape[1] // LANES - 2
    rows = slice(i * block, (i + 1) * block)
    keys = (i + 1) * block
    q_pos = i * block + lax.broadcasted_iota(jnp.int32, (block, keys), 0)
    k_pos = lax.broadcasted_iota(jnp.int32, (block, keys), 1)
    allowed = (seg_col[rows, :] == seg_row[:, :keys]) & (k_pos <= q_pos)
    k = rot[:keys, n_q * LANES : (n_q + 1) * LANES]
    v = rot[:keys, (n_q + 1) * LANES :]
    outs, maxes, totals = [], [], []
    for h in range(n_q):
        s = dot(rot[rows, h * LANES : (h + 1) * LANES], k, ((1,), (1,))) * scale
        s = jnp.where(allowed, s, MASK_FILL)
        top = jnp.max(s, axis=1, keepdims=True)
        e = jnp.exp(s - top)
        total = jnp.sum(e, axis=1, keepdims=True)
        outs.append(dot((e * (1.0 / total)).astype(BF16), v).astype(BF16))
        maxes.append(top)
        totals.append(total)
    attn[rows, :] = dot(jnp.concatenate(outs, axis=1), sel[...]).astype(BF16)
    stats[rows, :] = jnp.concatenate(maxes + totals, axis=1)


def turn_back(u, cos, sin, rows):
    return (u * cos[rows, :] - pltpu.roll(u, 64, 1) * sin[rows, :]).astype(BF16)


def attend_back_rows(
    scale, block, i, rot, d_attn, stats, cos, sin, seg_col, seg_row, sel, d_qkv, dk_sum, dv_sum
):
    n_q = rot.shape[1] // LANES - 2
    rows = slice(i * block, (i + 1) * block)
    keys = (i + 1) * block
    q_pos = i * block + lax.broadcasted_iota(jnp.int32, (block, keys), 0)
    k_pos = lax.broadcasted_iota(jnp.int32, (block, keys), 1)
    allowed = (seg_col[rows, :] == seg_row[:, :keys]) & (k_pos <= q_pos)
    k = rot[:keys, n_q * LANES : (n_q + 1) * LANES]
    v = rot[:keys, (n_q + 1) * LANES :]
    d_out = dot(d_attn[rows, :], sel[...], ((1,), (1,))).astype(BF16)
    stat = stats[rows, :]
    for h in range(n_q):
        q = rot[rows, h * LANES : (h + 1) * LANES]
        d_h = d_out[:, h * LANES : (h + 1) * LANES]
        s = dot(q, k, ((1,), (1,))) * scale
        s = jnp.where(allowed, s, MASK_FILL)
        p = jnp.exp(s - stat[:, h : h + 1]) * (1.0 / stat[:, n_q + h : n_q + h + 1])
        dv_sum[:keys, :] += dot(p.astype(BF16), d_h, ((0,), (0,)))
        d_p = dot(d_h, v, ((1,), (1,)))
        d_s = (p * (d_p - jnp.sum(p * d_p, axis=1, keepdims=True))).astype(BF16)
        d_q = (dot(d_s, k) * scale).astype(BF16).astype(F32)
        d_qkv[rows, h * LANES : (h + 1) * LANES] = turn_back(d_q, cos, sin, rows)
        dk_sum[:keys, :] += dot(d_s, q, ((0,), (0,)))


def attend_back_keys(scale, n_q, cos, sin, d_qkv, dk_sum, dv_sum):
    d_k = (dk_sum[...] * scale).astype(BF16).astype(F32)
    d_qkv[:, n_q * LANES : (n_q + 1) * LANES] = turn_back(d_k, cos, sin, slice(None))
    d_qkv[:, (n_q + 1) * LANES :] = dv_sum[...].astype(BF16)


VMEM_LIMIT = 56 * 1024 * 1024
BACK_LIMIT = 62 * 1024 * 1024


def sum_tp(value):
    value = value + pp(value, "tp", 1)
    return value + pp(value, "tp", 2)


def below(top):
    masks = []
    while top > 1:
        top //= 2
        masks.append(top)
    return masks


def flip(index, mask):
    return index + mask * (1 - 2 * ((index // mask) % 2))


def flip_all(index, bits):
    mask = 1
    while mask <= bits:
        if bits & mask:
            index = flip(index, mask)
        mask *= 2
    return index


class Links:
    def __init__(self, send_sems, recv_sems):
        self.sems = (send_sems, recv_sems)
        self.copies = []
        self.count = 0

    def send(self, src, dst, peer, kept=False):
        k = self.count
        self.count += 1
        copy = pltpu.make_async_remote_copy(
            src_ref=src,
            dst_ref=dst,
            send_sem=self.sems[0].at[k],
            recv_sem=self.sems[1].at[k],
            device_id=peer,
            device_id_type=pl.DeviceIdType.MESH,
        )
        copy.start()
        if not kept:
            self.copies.append(copy)
        return copy

    def finish(self, *sums):
        for copy in self.copies:
            copy.wait_send()
        for layer in sums:
            layer.drain()


def greet(peers):
    barrier = pltpu.get_barrier_semaphore()
    for peer in peers:
        pl.semaphore_signal(barrier, inc=1, device_id=peer, device_id_type=pl.DeviceIdType.MESH)
    pl.semaphore_wait(barrier, len(peers))


class Place:
    def __init__(self, n_z, n_tp):
        self.n_z, self.n_tp = n_z, n_tp
        self.z, self.y, self.t = (lax.axis_index(a) for a in ("fsdp", "ctx", "tp"))
        self.me = self.y * n_tp + self.t
        self.core = {"tp": flip(self.t, 1)}
        self.x = {"tp": flip(self.t, 2)}
        self.yy = {"ctx": 1 - self.y}
        self.masks = below(n_z)
        self.zb = self.z // (n_z // 2)

    def zz(self, mask):
        return {"fsdp": flip(self.z, mask)}

    def peers(self):
        return [self.core, self.x, self.yy] + [self.zz(m) for m in self.masks]


class WeightFlow:
    def __init__(self, links, at, out, cross, first, second):
        self.links, self.at, self.out = links, at, out
        self.first, self.second = first, second
        self.got = {}
        self.y_copy = links.send(cross, second(None), at.yy)

    def own(self):
        at = self.at
        for m in at.masks:
            dst = self.out.at[at.z, at.y]
            self.got[m, 0] = self.links.send(self.first(m), dst, at.zz(m))

    def crossed(self):
        at = self.at
        self.y_copy.wait_recv()
        for m in at.masks:
            dst = self.out.at[at.z, 1 - at.y]
            self.got[m, 1] = self.links.send(self.second(m), dst, at.zz(m))

    def take(self, rel, part):
        at = self.at
        self.got[rel, part].wait_recv()
        low = rel & -rel
        row = at.y if part == 0 else 1 - at.y
        block = self.out.at[flip_all(at.z, rel), row]
        for m in at.masks:
            if m < low:
                self.got[rel ^ m, part] = self.links.send(block, block, at.zz(m))

    def order(self):
        rels = [r for r in range(1, self.at.n_z)]
        return sorted(rels, key=lambda r: (bin(r).count("1"), -(r & -r), r))


def half_rows(ref, part, rows):
    return ref.at[pl.ds(part * (rows // 2), rows // 2)]


class LayerGather:
    def __init__(self, links, at, out, rows):
        self.links, self.at, self.out, self.rows = links, at, out, rows
        self.cores = []
        self.sent = []

    def half(self, index, part):
        return half_rows(self.out.at[index], part, self.rows)

    def send(self, src, dst, peer):
        self.sent.append(self.links.send(src, dst, peer, kept=True))
        return self.sent[-1]

    def pass_on(self, index, part, peer):
        block = self.half(index, part)
        return self.send(block, block, peer)

    def own(self, part, src=None):
        at, me = self.at, self.at.me
        a = self.half(me, part)
        src = a if src is None else src
        send = lambda peer: self.send(src, a, peer)
        if part == 0:
            self.xa, self.ya = send(at.x), send(at.yy)
        else:
            self.yb, self.xb = send(at.yy), send(at.x)
        self.cores.append(send(at.core))

    def to_core(self, index, part):
        self.cores.append(self.pass_on(index, part, self.at.core))

    def far_first(self):
        at = self.at
        self.x_of, self.y_of = flip(at.me, 2), flip(at.me, at.n_tp)
        self.diag = flip(self.x_of, at.n_tp)
        self.xa.wait_recv()
        self.y_fwd = self.pass_on(self.x_of, 0, at.yy)
        self.to_core(self.x_of, 0)
        self.yb.wait_recv()
        self.x_fwd = self.pass_on(self.y_of, 1, at.x)
        self.to_core(self.y_of, 1)

    def far_second(self):
        self.ya.wait_recv()
        self.to_core(self.y_of, 0)
        self.xb.wait_recv()
        self.to_core(self.x_of, 1)
        self.y_fwd.wait_recv()
        self.to_core(self.diag, 0)
        self.x_fwd.wait_recv()
        self.to_core(self.diag, 1)

    def last(self):
        for copy in self.cores:
            copy.wait_recv()

    def drain(self):
        for copy in self.sent:
            copy.wait_send()


class LayerSum:
    def __init__(self, links, at, rows, bufs, product, after=None):
        self.links, self.at, self.rows = links, at, rows
        self.to_core, self.held, self.landed, self.total, self.free = bufs
        self.product = product
        self.after = after

    def peers(self):
        return (self.at.core, self.at.x, self.at.yy)

    def tiles(self, some):
        width = self.total.shape[1]
        tile = 512 if width % 512 == 0 else width

        def body(c, carry):
            some(pl.ds(pl.multiple_of(c * tile, tile), tile))
            return carry

        lax.fori_loop(0, width // tile, body, 0)

    def drain(self):
        for copy in self.sent:
            copy.wait_send()
        self.sent = []

    def release(self):
        self.drain()
        for i, peer in enumerate(self.peers()):
            pl.semaphore_signal(
                self.free.at[i], inc=1, device_id=peer, device_id_type=pl.DeviceIdType.MESH
            )

    def begin(self):
        self.core = {}
        if self.after is not None:
            self.after.drain()
            for i in range(3):
                pl.semaphore_wait(self.free.at[i], 1)
        sent = []
        for i, k in enumerate((3, 1, 2, 0)):
            if i >= 2:
                sent[i - 2].wait_send()


            def some(cols, i=i, k=k):
                self.to_core[i % 2, :, cols] = self.product(2 * k + 1, cols).astype(BF16)

            self.tiles(some)
            self.core[k] = self.links.send(
                self.to_core.at[i % 2], self.held.at[k], self.at.core, kept=True
            )
            sent.append(self.core[k])
        self.sent = sent[2:]

    def middle(self):
        at, rows, h = self.at, self.rows, self.rows // 2
        held, landed = self.held, self.landed
        a, b = slice(0, h), slice(h, rows)

        def level(k):
            self.core[k].wait_recv()

            def some(cols):
                value = self.product(2 * k, cols) + held[k, :, cols].astype(F32)
                if k == 0:
                    self.total[:, cols] = value
                else:
                    held[k, :, cols] = value.astype(BF16)

            self.tiles(some)

        def send(k, i, peer):
            copy = self.links.send(held.at[k, pl.ds((i % 2) * h, h)], landed.at[i], peer, kept=True)
            self.sent.append(copy)
            return copy

        level(3)
        x1 = send(3, 0, at.x)
        y1 = send(3, 1, at.yy)
        level(1)
        x2 = send(1, 2, at.x)
        level(2)
        y2 = send(2, 3, at.yy)
        level(0)
        x1.wait_recv()
        held[2, a] = (held[2, a].astype(F32) + landed[0].astype(F32)).astype(BF16)
        y3 = send(2, 4, at.yy)
        y1.wait_recv()
        held[1, b] = (held[1, b].astype(F32) + landed[1].astype(F32)).astype(BF16)
        x3 = send(1, 5, at.x)
        self.tail = (x2, y3, y2, x3)

    def end(self):
        h = self.rows // 2
        landed, total = self.landed, self.total
        for copy in self.tail:
            copy.wait_recv()
        top = total[:h, :] + landed[2].astype(F32) + landed[4].astype(F32)
        low = total[h:, :] + landed[3].astype(F32) + landed[5].astype(F32)
        return top, low


def sum_scratch(rows, width):
    return [
        pltpu.VMEM((2, rows, width), BF16),
        pltpu.VMEM((4, rows, width), BF16),
        pltpu.VMEM((6, rows // 2, width), BF16),
        pltpu.VMEM((rows, width), F32),
        pltpu.SemaphoreType.REGULAR((3,)),
    ]


def eye(n):
    shape = (n, n)
    same = lax.broadcasted_iota(jnp.int32, shape, 0) == lax.broadcasted_iota(jnp.int32, shape, 1)
    return same.astype(F32).astype(BF16)


def head_spread(n_q, compact):
    shape = (compact, (n_q + 2) * LANES)
    col, lane = (lax.broadcasted_iota(jnp.int32, shape, d) for d in (0, 1))
    at, head = col % HEAD_DIM, col // HEAD_DIM
    spot = head * LANES + at + jnp.where((at >= HALF) & (head < n_q + 1), 64 - HALF, 0)
    return ((spot == lane) & (head < n_q + 2)).astype(F32).astype(BF16)


def head_select(n_q):
    shape = (n_q * LANES, n_q * HEAD_DIM)
    lane, col = (lax.broadcasted_iota(jnp.int32, shape, d) for d in (0, 1))
    return ((col // HEAD_DIM) * LANES + col % HEAD_DIM == lane).astype(F32).astype(BF16)


def front_kernel(
    n_z, n_tp, scale, q_block,
    x_here, dy_here, q_w, k_w, v_w, o_w, gate_w, up_w, down_w, extra, seg_col, seg_row,
    w_heads, w_o, w3, gains, norm_attn, dy_all, norm_all, attn, rot, stats, mid, cos, sin, spread, sel,
    w_in, x_all, qkv, to_core, held, landed, total, free, in_cross, o_cross, w3_cross,
    heads_v, norm_v, own_v, root_v, o_v, in_send, o_send, w3_send, send_sems, recv_sems, sems,
):
    at = Place(n_z, n_tp)
    links = Links(send_sems, recv_sems)
    z, y, t, me = at.z, at.y, at.t, at.me
    zb = z // (n_z // 2)
    n_b, rows, width = 2 * n_tp, x_all.shape[0] // (2 * n_tp), x_all.shape[1]
    depth = in_send.shape[1]
    full_len = x_all.shape[0]
    local = []

    def move(src, dst):
        copy = pltpu.make_async_copy(src, dst, sems.at[len(local)])
        copy.start()
        local.append(copy)
        return copy

    def block_of(ref, index):
        return ref.at[pl.ds(pl.multiple_of(index * rows, rows), rows)]

    q_cols, kv_cols = q_w.shape[1] // 2, k_w.shape[1] // 2
    units = gate_w.shape[1] // 4
    wide = w3_send.shape[3] - units
    for j in range(2):
        in_send[j] = jnp.concatenate(
            [
                q_w[:, j * q_cols : (j + 1) * q_cols],
                k_w[:, j * kv_cols : (j + 1) * kv_cols],
                v_w[:, j * kv_cols : (j + 1) * kv_cols],
                extra[...],
            ],
            axis=1,
        )
    greet(at.peers())
    f_in = WeightFlow(
        links, at, w_in, in_send.at[1 - y], lambda m: in_send.at[y], lambda m: in_cross
    )
    f_in.own()
    own_in = move(in_send.at[y], w_in.at[z, y])
    x_mine = block_of(x_here, t)
    tok_y = links.send(x_mine, block_of(x_all, me), at.yy)
    x_own = move(x_here, x_all.at[pl.ds(pl.multiple_of(y * (full_len // 2), full_len // 2), full_len // 2)])
    dy_mine = block_of(dy_here, t)
    dy_own = move(dy_here.reshape(n_tp, rows, width), dy_all.at[0, pl.ds(y * n_tp, n_tp)])

    for j in range(2):
        half = o_w[j * q_cols : (j + 1) * q_cols, :]
        o_send[j] = dot(half, eye(q_cols), ((0,), (0,))).astype(BF16)
    for j in range(4):
        cols = slice(j * units, (j + 1) * units)
        w3_send[j % 2, j // 2, :, : 2 * units] = jnp.concatenate(
            [gate_w[:, cols], up_w[:, cols]], axis=1
        )
        w3_send[j % 2, j // 2, :, wide:] = dot(
            down_w[cols, :], eye(units), ((0,), (0,))
        ).astype(BF16)
    f_in.crossed()
    cross_in = move(in_cross, w_in.at[z, 1 - y])
    f_o = WeightFlow(
        links, at, w_o, o_send.at[1 - y], lambda m: o_send.at[y], lambda m: o_cross
    )
    top = n_z // 2
    f_3 = WeightFlow(
        links, at, w3, w3_send.at[1 - y],
        lambda m: w3_send.at[y, 1 - zb if m == top else zb],
        lambda m: w3_cross if m is None else w3_cross.at[1 - zb if m == top else zb],
    )
    dy_y = links.send(dy_mine, dy_all.at[0, me], at.yy)
    tok_y.wait_recv()
    y_of, x_of = flip(me, n_tp), flip(me, 2)
    y_block = block_of(x_all, y_of)
    tok_x = links.send(y_block, y_block, at.x)
    tok_c = [links.send(y_block, y_block, at.core)]
    ins = [(rel, p) for rel in f_in.order() for p in (0, 1)]
    for rel, p in ins:
        if rel == top:
            f_in.take(rel, p)
    lane = lax.broadcasted_iota(jnp.int32, (1, LANES), 1)
    within = lane % 64
    frequency = jnp.where(
        within < HALF, jnp.exp(within.astype(F32) * (-2.0 * math.log(ROPE_BASE) / HEAD_DIM)), 0.0
    )
    sign = jnp.where(lane < 64, -1.0, 1.0)
    n_q = rot.shape[1] // LANES - 2
    spread[...] = head_spread(n_q, w_in.shape[3])
    sel[...] = head_select(n_q)
    step = min(256, full_len)

    def tables(c, carry):
        at_rows = pl.ds(pl.multiple_of(c * step, step), step)
        before = jnp.where(seg_row[...] < seg_col[at_rows, :], 1.0, 0.0)
        start = jnp.sum(before, axis=1, keepdims=True)
        position = (c * step + lax.broadcasted_iota(jnp.int32, (step, 1), 0)).astype(F32)
        angles = (position - start) * frequency
        cos[at_rows, :] = jnp.cos(angles)
        sin[at_rows, :] = jnp.sin(angles) * sign
        return carry

    lax.fori_loop(0, full_len // step, tables, 0)
    tok_x.wait_recv()
    diag = block_of(x_all, flip(y_of, 2))
    tok_c.append(links.send(diag, diag, at.core))
    x_own.wait()

    for copy in tok_c:
        copy.wait_recv()

    def find_root(c, carry):
        at_rows = pl.ds(pl.multiple_of(c * step, step), step)
        value = x_all[at_rows, :].astype(F32)
        root_v[at_rows, :] = lax.rsqrt(jnp.mean(value * value, axis=1, keepdims=True) + NORM_EPS)
        return carry

    lax.fori_loop(0, full_len // step, find_root, 0)
    own_in.wait()
    cross_in.wait()

    pick_gain = (
        lax.broadcasted_iota(jnp.int32, (8, w_in.shape[3]), 1)
        == sel.shape[1] // HEAD_DIM * HEAD_DIM + 2 * HEAD_DIM + lax.broadcasted_iota(jnp.int32, (8, w_in.shape[3]), 0)
    ).astype(F32).astype(BF16)

    group = 1
    while 2 * depth * group % LANES:
        group *= 2
    span = 2 * depth * group

    def project(rel, first):
        owner = flip_all(z, rel) // group
        cols = pl.ds(pl.multiple_of(owner * span, span), span)
        weights = w_in[pl.ds(owner * group, group)].reshape(span, w_in.shape[3])
        gain = dot(pick_gain, weights, ((1,), (1,)))
        gains[:, cols] = gain
        heads = dot(weights, spread[...]).astype(BF16)
        heads_v[cols, :] = heads

        def some_rows(c, carry):
            at_rows = pl.ds(pl.multiple_of(c * step, step), step)
            value = (x_all[at_rows, cols].astype(F32) * root_v[at_rows, :] * gain[0:1, :]).astype(BF16)
            norm_v[at_rows, cols] = value
            term = dot(value, heads)
            qkv[at_rows, :] = term if first else qkv[at_rows, :] + term
            return carry

        lax.fori_loop(0, full_len // step, some_rows, 0)

    f_o.own()
    f_o.crossed()
    if group == 1:
        project(0, True)
    f_3.own()
    f_3.crossed()
    for rel in f_in.order():
        for p in (0, 1):
            if rel != top:
                f_in.take(rel, p)
        if group == 1:
            project(rel, False)
    if group > 1:
        for rel in range(0, n_z, group):
            project(rel, rel == 0)
    heads_out = move(heads_v, w_heads)
    norm_out = move(norm_v, norm_attn)
    own_o = [move(o_send.at[y], w_o.at[z, y]), move(o_cross, w_o.at[z, 1 - y])]
    own_3 = [move(w3_send.at[y, zb], w3.at[z, y]), move(w3_cross.at[zb], w3.at[z, 1 - y])]
    dy_y.wait_recv()
    dy_x = links.send(dy_all.at[0, y_of], dy_all.at[0, y_of], at.x)
    dy_c = [links.send(dy_all.at[0, y_of], dy_all.at[0, y_of], at.core)]
    dy_z = [
        links.send(half_rows(dy_mine, p, rows), half_rows(dy_all.at[1, me], p, rows), at.zz(top))
        for p in (0, 1)
    ]
    for p in (0, 1):
        f_o.take(top, p)

    def turn(c, carry):
        r = pl.ds(pl.multiple_of(c * step, step), step)
        for h in range(n_q + 1):
            u = qkv[r, h * LANES : (h + 1) * LANES]
            rot[r, h * LANES : (h + 1) * LANES] = (
                u * cos[r, :] + pltpu.roll(u, 64, 1) * sin[r, :]
            ).astype(BF16)
        rot[r, (n_q + 1) * LANES :] = qkv[r, (n_q + 1) * LANES :].astype(BF16)
        return carry

    lax.fori_loop(0, full_len // step, turn, 0)
    dy_far = LayerGather(links, at, dy_all.at[1], rows)
    for i in range(full_len // q_block):
        attend_rows(scale, q_block, i, rot, seg_col, seg_row, sel, attn, stats)
        if i == 0:
            dy_x.wait_recv()
            d_of = flip(y_of, 2)
            dy_c.append(links.send(dy_all.at[0, d_of], dy_all.at[0, d_of], at.core))
    for rel in f_o.order():
        for p in (0, 1):
            if rel != top:
                f_o.take(rel, p)
    for copy in own_o:
        copy.wait()
    load_o = move(w_o.reshape(width, o_v.shape[1]), o_v)
    load_o.wait()

    def product(r, cols):
        lhs = attn[pl.ds(pl.multiple_of(flip_all(me, r) * rows, rows), rows), :]
        return dot(lhs, o_v[cols, :], ((1,), (1,)))

    layer = LayerSum(links, at, rows, (to_core, held, landed, total, free), product)
    layer.begin()
    layer.middle()
    for p in (0, 1):
        f_3.take(top, p)
    norm_own = LayerGather(links, at, norm_all.at[0], rows)
    norm_far = LayerGather(links, at, norm_all.at[1], rows)
    far = []
    h = rows // 2
    load_x = move(x_mine, own_v)
    load_x.wait()
    for p, value in enumerate(layer.end()):
        r = slice(p * h, (p + 1) * h)
        value = value + own_v[r, :].astype(F32)
        mid[r, :] = value
        root = lax.rsqrt(jnp.mean(value * value, axis=1, keepdims=True) + NORM_EPS)
        own_v[r, :] = (value * root * gains[1:2, :]).astype(BF16)
        src = own_v.at[pl.ds(p * h, h)]
        far.append(links.send(src, half_rows(norm_all.at[1, me], p, rows), at.zz(top)))
        norm_own.own(p, src)
    keep = move(own_v, norm_all.at[0, me])
    for p in (0, 1):
        dy_z[p].wait_recv()
        dy_far.own(p)
    norm_own.far_first()
    for p in (0, 1):
        far[p].wait_recv()
        norm_far.own(p)
    norm_own.far_second()
    dy_far.far_first()
    norm_far.far_first()
    dy_far.far_second()
    norm_far.far_second()
    for rel in f_3.order():
        for p in (0, 1):
            if rel != top:
                f_3.take(rel, p)
    for gather in (norm_own, dy_far, norm_far):
        gather.last()
        gather.drain()
    for copy in dy_c:
        copy.wait_recv()
    for copy in [dy_own, heads_out, norm_out, keep] + own_3:
        copy.wait()
    links.finish(layer)


def front(n_z, n_tp, scale, x_here, dy_here, weights, extra, seg_col, seg_row):
    q_w, k_w, v_w, o_w, gate_w, up_w, down_w = weights
    half_len, width = x_here.shape
    full_len = 2 * half_len
    rows = half_len // n_tp
    depth, q_cols = q_w.shape[0], q_w.shape[1] // 2
    n_q = q_cols // HEAD_DIM
    heads = (n_q + 2) * LANES
    compact = q_cols + k_w.shape[1] + extra.shape[1]
    units = gate_w.shape[1] // 4
    w3_cols = wide_of(units) + units
    any_, vmem = pl.BlockSpec(memory_space=pl.ANY), pl.BlockSpec(memory_space=pltpu.VMEM)
    n_sems = 80 + 6 * n_z + 32
    shape = jax.ShapeDtypeStruct
    return pl.pallas_call(
        lambda *refs: front_kernel(n_z, n_tp, scale, min(256, full_len), *refs),
        out_shape=(
            shape((width, heads), BF16),
            shape((n_z, 2, depth, q_cols), BF16),
            shape((n_z, 2, depth, w3_cols), BF16),
            shape((8, width), F32),
            shape((full_len, width), BF16),
            shape((2, 2 * n_tp, rows, width), BF16),
            shape((2, 2 * n_tp, rows, width), BF16),
            shape((full_len, q_cols), BF16),
            shape((full_len, heads), BF16),
            shape((full_len, 2 * n_q), F32),
            shape((rows, width), F32),
            shape((full_len, LANES), F32),
            shape((full_len, LANES), F32),
            shape((compact, heads), BF16),
            shape((n_q * LANES, q_cols), BF16),
        ),
        in_specs=[any_] * 2 + [vmem] * 10,
        out_specs=(any_, any_, any_, vmem, any_, any_, any_) + (vmem,) * 8,
        scratch_shapes=[
            pltpu.VMEM((n_z, 2, depth, compact), BF16),
            pltpu.VMEM((full_len, width), BF16),
            pltpu.VMEM((full_len, heads), F32),
            *sum_scratch(rows, width),
            pltpu.VMEM((depth, compact), BF16),
            pltpu.VMEM((depth, q_cols), BF16),
            pltpu.VMEM((2, depth, w3_cols), BF16),
            pltpu.VMEM((width, heads), BF16),
            pltpu.VMEM((full_len, width), BF16),
            pltpu.VMEM((rows, width), BF16),
            pltpu.VMEM((full_len, 1), F32),
            pltpu.VMEM((width, q_cols), BF16),
            pltpu.VMEM((2, depth, compact), BF16),
            pltpu.VMEM((2, depth, q_cols), BF16),
            pltpu.VMEM((2, 2, depth, w3_cols), BF16),
            pltpu.SemaphoreType.DMA((n_sems,)),
            pltpu.SemaphoreType.DMA((n_sems,)),
            pltpu.SemaphoreType.DMA((16,)),
        ],
        compiler_params=pltpu.CompilerParams(
            collective_id=1, has_side_effects=True, vmem_limit_bytes=VMEM_LIMIT
        ),
        name="front",
    )(x_here, dy_here, *weights, extra, seg_col, seg_row)


def wide_of(units):
    return -(-2 * units // LANES) * LANES


def act_kernel(norm, dy, w3, d_gu, hidden):
    units = hidden.shape[2]
    n = norm.shape[0] * norm.shape[1]
    wide = w3.shape[1] - units
    gate_up = dot(norm[...].reshape(n, norm.shape[2]), w3[:, : 2 * units])
    d_hidden = dot(dy[...].reshape(n, dy.shape[2]), w3[:, wide:])
    gate, up = gate_up[:, :units], gate_up[:, units:]
    sig = 1.0 / (1.0 + jnp.exp(-gate))
    silu = gate * sig
    hidden[...] = (silu * up).astype(BF16).reshape(hidden.shape)
    d_up = (d_hidden * silu).astype(BF16)
    d_gate = (d_hidden * up * sig * (1.0 + gate * (1.0 - sig))).astype(BF16)
    d_gu[...] = jnp.concatenate([d_gate, d_up], axis=1).reshape(d_gu.shape)


def act(norm, dy, w3, units):
    blocks, rows, width = norm.shape
    per = max(1, 256 // rows)
    one = lambda cols: pl.BlockSpec((per, rows, cols), lambda i: (i, 0, 0))
    return pl.pallas_call(
        act_kernel,
        grid=(blocks // per,),
        out_shape=(
            jax.ShapeDtypeStruct((blocks, rows, 2 * units), BF16),
            jax.ShapeDtypeStruct((blocks, rows, units), BF16),
        ),
        in_specs=[one(width), one(width), pl.BlockSpec(w3.shape, lambda i: (0, 0))],
        out_specs=(one(2 * units), one(units)),
        compiler_params=pltpu.CompilerParams(vmem_limit_bytes=VMEM_LIMIT),
        name="act",
    )(norm, dy, w3)


def terms_kernel(norm, dy, d_gu, hidden, gu, dn):
    def term(lhs, rhs, out):
        n = lhs.shape[0] * lhs.shape[1]
        value = dot(lhs[...].reshape(n, lhs.shape[2]), rhs[...].reshape(n, rhs.shape[2]), ((0,), (0,)))
        out[...] = value.astype(BF16).reshape(out.shape)

    term(norm, d_gu, gu)
    term(dy, hidden, dn)


def terms(norm, dy, d_gu, hidden, n_z):
    blocks, rows, width = norm.shape
    depth, units = width // n_z // 2, hidden.shape[2]
    group = 1
    while 2 * depth * group % LANES:
        group *= 2
    cols = pl.BlockSpec((blocks, rows, 2 * depth * group), lambda i: (0, 0, i))
    whole = lambda a: pl.BlockSpec(a.shape, lambda i: (0, 0, 0))
    out = lambda c: pl.BlockSpec((group, 2, depth, c), lambda i: (i, 0, 0, 0))
    return pl.pallas_call(
        terms_kernel,
        grid=(n_z // group,),
        out_shape=(
            jax.ShapeDtypeStruct((n_z, 2, depth, 2 * units), BF16),
            jax.ShapeDtypeStruct((n_z, 2, depth, units), BF16),
        ),
        in_specs=[cols, cols, whole(d_gu), whole(hidden)],
        out_specs=(out(2 * units), out(units)),
        compiler_params=pltpu.CompilerParams(vmem_limit_bytes=VMEM_LIMIT),
        name="terms",
    )(norm, dy, d_gu, hidden)


def finish_kernel(
    gu, dn, o, ins, q_w, k_w, v_w, gate_w, up_w,
    q_grad, k_grad, v_grad, o_grad, gate_grad, up_grad, down_grad, sums,
):
    depth = q_w.shape[0]
    units, q_cols, kv_cols = dn.shape[3], q_w.shape[1] // 2, k_w.shape[1] // 2
    one = eye(depth)

    def weighted(w, g):
        return jnp.sum(w[...].astype(F32) * g[...], axis=1, keepdims=True)

    gate_grad[...] = jnp.concatenate(
        [gu[j // 2, j % 2, :, :units].astype(F32) for j in range(4)], axis=1
    )
    up_grad[...] = jnp.concatenate(
        [gu[j // 2, j % 2, :, units:].astype(F32) for j in range(4)], axis=1
    )
    for j in range(4):
        down_grad[j * units : (j + 1) * units, :] = dot(dn[j // 2, j % 2], one, ((0,), (0,)))
    for j in range(2):
        o_grad[j * q_cols : (j + 1) * q_cols, :] = dot(o[j], one, ((0,), (0,)))
    lo = 0
    for grad, cols in ((q_grad, q_cols), (k_grad, kv_cols), (v_grad, kv_cols)):
        grad[...] = jnp.concatenate(
            [ins[j, :, lo : lo + cols].astype(F32) for j in range(2)], axis=1
        )
        lo += cols
    first = weighted(q_w, q_grad) + weighted(k_w, k_grad) + weighted(v_w, v_grad)
    second = weighted(gate_w, gate_grad) + weighted(up_w, up_grad)
    lane = lax.broadcasted_iota(jnp.int32, sums.shape, 1)
    sums[...] = jnp.where(lane == 0, first, second)


def finish(gu, dn, o, ins, q_w, k_w, v_w, gate_w, up_w, o_shape, down_shape):
    shape = lambda dims: jax.ShapeDtypeStruct(dims, F32)
    return pl.pallas_call(
        finish_kernel,
        out_shape=(
            shape(q_w.shape), shape(k_w.shape), shape(v_w.shape), shape(o_shape),
            shape(gate_w.shape), shape(up_w.shape), shape(down_shape), shape((q_w.shape[0], LANES)),
        ),
        compiler_params=pltpu.CompilerParams(vmem_limit_bytes=VMEM_LIMIT),
        name="finish",
    )(gu, dn, o, ins, q_w, k_w, v_w, gate_w, up_w)


class TpGather:
    def __init__(self, links, at, out):
        self.links, self.at, self.out = links, at, out

    def own(self, src):
        at = self.at
        dst = self.out.at[at.t]
        self.x = self.links.send(src, dst, at.x)
        self.cores = [self.links.send(src, dst, at.core)]

    def second(self):
        at = self.at
        self.x.wait_recv()
        block = self.out.at[flip(at.t, 2)]
        self.cores.append(self.links.send(block, block, at.core))

    def last(self):
        for copy in self.cores:
            copy.wait_recv()


class GradFlow:
    def __init__(self, links, at, src, land, swap, out, passing, fetch=None):
        self.links, self.at, self.src, self.land = links, at, src, land
        self.swap, self.out, self.passing, self.fetch = swap, out, passing, fetch
        self.adds = [m for m in reversed(at.masks) if not (swap and m == at.n_z // 2)]
        self.slot = {}
        n = 0
        for m in self.adds:
            for rel in range(0, at.n_z, 2 * m):
                self.slot[m, rel] = n
                n += 1
        self.got = {}
        self.at_mask = {}

    def row(self, part):
        return self.at.y if part == 0 else 1 - self.at.y

    def own(self, rel, part):
        return self.src.at[flip_all(self.at.z, rel), self.row(part)]

    def held(self, rel, part):
        m = self.at_mask.get((rel, part))
        if m is None:
            return self.own(rel, part), True
        return self.land.at[self.slot[m, rel], part], False

    def send(self, m, rel, part):
        block, _ = self.held(rel, part)
        self.got[m, rel ^ m, part] = self.links.send(
            block, self.land.at[self.slot[m, rel ^ m], part], self.at.zz(m)
        )

    def first(self, parts=(1, 0)):
        m = self.adds[0]
        rels = [r for r in range(self.at.n_z) if r & m]
        for rel in sorted(rels, reverse=True):
            for part in parts:
                self.send(m, rel, part)

    def add(self, m, rel, part):
        block, is_first = self.held(rel, part)
        if is_first and self.fetch is not None:
            block = self.fetch(block)
        self.got[m, rel, part].wait_recv()
        slot = self.land.at[self.slot[m, rel], part]
        slot[...] = (block[...].astype(F32) + slot[...].astype(F32)).astype(BF16)
        self.at_mask[rel, part] = m

    def spread(self):
        at = self.at
        for i, m in enumerate(self.adds):
            left = range(0, at.n_z, 2 * m)
            nxt = self.adds[i + 1] if i + 1 < len(self.adds) else (2 * m if self.swap else None)
            for rel in sorted(left, key=lambda r: -(r & (nxt or 0))):
                for part in (1, 0):
                    self.add(m, rel, part)
                    if nxt is not None and rel & nxt:
                        if nxt in self.adds:
                            self.send(nxt, rel, part)
                        else:
                            self.exchange(nxt, rel, part)

    def column(self, mine):
        return self.at.zb if mine else 1 - self.at.zb

    def exchange(self, m, rel, part):
        block, _ = self.held(rel, part)
        if part == 0:
            dst = self.out.at[self.at.zb, self.at.y]
        else:
            dst = self.passing
        self.got[m, 0, part] = self.links.send(block, dst, self.at.zz(m))

    def cross(self):
        at = self.at
        block, _ = self.held(0, 1)
        dst = self.out.at[at.zb, at.y] if self.swap else self.out.at[at.y]
        self.ends = [self.links.send(block, dst, at.yy)]

    def cross_far(self):
        at = self.at
        self.got[at.n_z // 2, 0, 1].wait_recv()
        self.ends.append(self.links.send(self.passing, self.out.at[1 - at.zb, at.y], at.yy))
        self.ends.append(self.got[at.n_z // 2, 0, 0])

    def mine(self):
        at = self.at
        dst = self.out.at[at.zb, at.y] if self.swap else self.out.at[at.y]
        return self.held(0, 0)[0], dst

    def last(self):
        for copy in self.ends:
            copy.wait_recv()


def back_kernel(
    n_z, n_tp, scale, q_block, units, wide,
    x_here, dy_here, w3, d_gu, hidden, gu_src, dn_src, w_o, w_heads, norm_attn,
    mid, gains, rot, attn, stats, cos, sin, seg_col, seg_row, sel, spread,
    output, input_grad, gu_out, dn_out, o_out, in_out,
    w3_v, gu_v, hid_v,
    to_core_a, held_a, landed_a, total_a, free_a, to_core_b, held_b, landed_b, total_b, free_b,
    far_v, far_in, d_mid, row_v, d_proj, d_attn, d_qkv, dk_sum, dv_sum, o_v,
    gu_land, gu_pass, dn_land, dn_pass, fetch_gu, fetch_dn, o_land, in_land,
    send_sems, recv_sems, sems,
):
    at = Place(n_z, n_tp)
    links = Links(send_sems, recv_sems)
    z, y, t, me = at.z, at.y, at.t, at.me
    top = n_z // 2
    n_b, rows, width = 2 * n_tp, mid.shape[0], mid.shape[1]
    depth = gu_src.shape[2]
    full_len = rot.shape[0]
    h = rows // 2
    n_q = rot.shape[1] // LANES - 2
    local = []

    def move(src, dst):
        copy = pltpu.make_async_copy(src, dst, sems.at[len(local)])
        copy.start()
        local.append(copy)
        return copy

    load_w3 = move(w3, w3_v)
    load_gu, load_hid = move(d_gu, gu_v), move(hidden, hid_v)
    load_o = move(w_o, o_v)
    load_x = move(x_here.at[pl.ds(pl.multiple_of(t * rows, rows), rows)], row_v.at[0])
    load_dy = move(dy_here.at[pl.ds(pl.multiple_of(t * rows, rows), rows)], row_v.at[1])
    greet(at.peers())

    def fetch_with(buf):
        def fetch(block):
            move(block, buf).wait()
            return buf

        return fetch

    f_gu = GradFlow(links, at, gu_src, gu_land, True, gu_out, gu_pass, fetch_with(fetch_gu))
    f_dn = GradFlow(links, at, dn_src, dn_land, True, dn_out, dn_pass, fetch_with(fetch_dn))
    f_gu.first()

    def term(seq, lhs, lo, hi):
        def product(r, cols):
            return dot(lhs[seq, flip_all(me, r)], w3_v[cols, lo:hi], ((1,), (1,)))

        return product

    bufs_a = (to_core_a, held_a, landed_a, total_a, free_a)
    bufs_b = (to_core_b, held_b, landed_b, total_b, free_b)
    load_w3.wait()
    load_gu.wait()
    far = LayerSum(links, at, rows, bufs_a, term(1, gu_v, 0, 2 * units))
    own = LayerSum(links, at, rows, bufs_b, term(0, gu_v, 0, 2 * units))
    far.begin()
    far.middle()
    own.begin()

    def send_far(layer, i):
        sent = []
        for p, value in enumerate(layer.end()):
            far_v[i, pl.ds(p * h, h), :] = value.astype(BF16)
            sent.append(
                links.send(
                    half_rows(far_v.at[i], p, rows), half_rows(far_in.at[i], p, rows), at.zz(top),
                    kept=True,
                )
            )
        layer.release()
        return sent

    sent_far = send_far(far, 0)
    own.middle()
    heads_v = w3_v.at[:, : w_heads.shape[1]]
    load_heads = move(w_heads, heads_v)
    f_dn.first()
    load_hid.wait()
    ffn_far = LayerSum(links, at, rows, bufs_a, term(1, hid_v, wide, wide + units), far)
    ffn_own = LayerSum(links, at, rows, bufs_b, term(0, hid_v, wide, wide + units), own)
    ffn_far.begin()

    def norm_back(inputs, gain, d_normed):
        root = lax.rsqrt(jnp.mean(inputs * inputs, axis=1, keepdims=True) + NORM_EPS)
        scaled = d_normed * gain
        return root * scaled - inputs * (root * root * root) * jnp.mean(
            scaled * inputs, axis=1, keepdims=True
        )

    load_x.wait()
    load_dy.wait()
    gather = LayerGather(links, at, d_proj, rows)
    for p, value in enumerate(own.end()):
        r = slice(p * h, (p + 1) * h)
        sent_far[p].wait_recv()
        value = value + far_in[0, r, :].astype(F32)
        value = row_v[1, r, :].astype(F32) + norm_back(mid[r, :], gains[1:2, :], value)
        d_mid[r, :] = value
        d_proj[me, r, :] = value.astype(BF16)
        gather.own(p)
    own.release()
    gather.far_first()
    ffn_own.begin()
    f_gu.spread()
    gather.far_second()
    ffn_far.middle()
    f_dn.spread()
    gather.last()

    load_o.wait()
    w_o_all = o_v[...].reshape(width, o_v.shape[3])

    def d_attn_rows(b, carry):
        r = pl.ds(pl.multiple_of(b * rows, rows), rows)
        d_attn[r, :] = dot(d_proj[b], w_o_all).astype(BF16)
        return carry

    lax.fori_loop(0, n_b, d_attn_rows, 0)

    group = 1
    while 2 * depth * group % LANES:
        group *= 2
    span = 2 * depth * group

    def groups():
        rels = sorted(range(0, n_z, group), key=lambda r: (-(r & 1), -r))
        return [flip_all(z, r) // group for r in rels]

    def span_of(owner):
        return pl.ds(pl.multiple_of(owner * span, span), span)

    o_src = o_v
    f_o = GradFlow(links, at, o_src, o_land, False, o_out, None)
    for owner in groups():
        lhs = jnp.concatenate([d_proj[b, :, span_of(owner)] for b in range(n_b)], axis=0)
        value = dot(lhs, attn[...], ((0,), (0,))).astype(BF16)
        o_src[pl.ds(owner * group, group)] = value.reshape(group, 2, depth, value.shape[1])
    f_o.first()
    gather.drain()
    load_norm = move(norm_attn, d_proj)
    ffn_own.middle()
    dk_sum[...] = jnp.zeros_like(dk_sum)
    dv_sum[...] = jnp.zeros_like(dv_sum)
    for i in range(full_len // q_block):
        attend_back_rows(
            scale, q_block, i, rot, d_attn, stats, cos, sin, seg_col, seg_row, sel, d_qkv, dk_sum, dv_sum
        )
        if i == 0:
            f_gu.cross()
            f_dn.cross()
            sent_ffn = send_far(ffn_far, 1)
        if i == 1:
            f_o.spread()
            f_o.cross()
    attend_back_keys(scale, n_q, cos, sin, d_qkv, dk_sum, dv_sum)

    load_heads.wait()

    def d_term(r, cols):
        value = d_qkv[pl.ds(pl.multiple_of(flip_all(me, r) * rows, rows), rows), :]
        return dot(value, w3_v[cols, : w_heads.shape[1]], ((1,), (1,)))

    d_in = LayerSum(links, at, rows, bufs_a, d_term, ffn_far)
    d_in.begin()
    d_in.middle()
    in_cols = slice(w_heads.shape[1], w_heads.shape[1] + spread.shape[0])
    in_src = w3_v.reshape(n_z, 2, depth, w3_v.shape[1]).at[:, :, :, in_cols]
    f_in = GradFlow(links, at, in_src, in_land, False, in_out, None)
    packed = dot(d_qkv[...], spread[...], ((1,), (1,))).astype(BF16)
    load_norm.wait()
    for owner in groups():
        lhs = jnp.concatenate([d_proj[b, :, span_of(owner)] for b in range(n_b)], axis=0)
        w3_v[span_of(owner), in_cols] = dot(lhs, packed, ((0,), (0,))).astype(BF16)
    f_in.first()
    out_g, in_g = TpGather(links, at, output), TpGather(links, at, input_grad)
    stay = []
    for p, value in enumerate(d_in.end()):
        r = slice(p * h, (p + 1) * h)
        value = d_mid[r, :] + norm_back(row_v[0, r, :].astype(F32), gains[0:1, :], value)
        row_v[1, r, :] = value.astype(BF16)
    in_g.own(row_v.at[1])
    stay.append(move(row_v.at[1], input_grad.at[t]))
    for copy in sent_far:
        copy.wait_send()
    for p, value in enumerate(ffn_own.end()):
        r = slice(p * h, (p + 1) * h)
        sent_ffn[p].wait_recv()
        value = value + far_in[1, r, :].astype(F32)
        far_v[0, r, :] = (mid[r, :] + value).astype(BF16)
    out_g.own(far_v.at[0])
    stay.append(move(far_v.at[0], output.at[t]))
    f_in.spread()
    f_in.cross()
    f_gu.cross_far()
    f_dn.cross_far()
    for flow in (f_gu, f_dn, f_o, f_in):
        stay.append(move(*flow.mine()))
    in_g.second()
    out_g.second()
    for flow in (in_g, out_g, f_gu, f_dn, f_o, f_in):
        flow.last()
    for copy in stay:
        copy.wait()
    for copy in sent_ffn:
        copy.wait_send()
    links.finish(d_in, ffn_own)


def back(n_z, n_tp, scale, units, wide, *args):
    x_here, w_heads, spread, mid, sel = args[0], args[8], args[20], args[10], args[19]
    d_gu, hidden, gu_src, dn_src, w3, w_o, rot = args[3], args[4], args[5], args[6], args[2], args[7], args[12]
    half_len, width = x_here.shape
    rows = mid.shape[0]
    full_len = 2 * half_len
    depth = gu_src.shape[2]
    heads, compact = w_heads.shape[1], spread.shape[0]
    q_cols = sel.shape[1]
    any_, vmem = pl.BlockSpec(memory_space=pl.ANY), pl.BlockSpec(memory_space=pltpu.VMEM)
    shape = jax.ShapeDtypeStruct
    n_swap, n_add = max(1, n_z - 2), n_z - 1
    n_sems = 120 + 8 * n_z
    return pl.pallas_call(
        lambda *refs: back_kernel(n_z, n_tp, scale, min(256, full_len), units, wide, *refs),
        out_shape=(
            shape((n_tp, rows, width), BF16),
            shape((n_tp, rows, width), BF16),
            shape((2, 2, depth, 2 * units), BF16),
            shape((2, 2, depth, units), BF16),
            shape((2, depth, q_cols), BF16),
            shape((2, depth, compact), BF16),
        ),
        in_specs=[any_] * 10 + [vmem] * 11,
        out_specs=(any_,) * 6,
        scratch_shapes=[
            pltpu.VMEM(w3.shape, BF16),
            pltpu.VMEM(d_gu.shape, BF16),
            pltpu.VMEM(hidden.shape, BF16),
            *sum_scratch(rows, width),
            *sum_scratch(rows, width),
            pltpu.VMEM((2, rows, width), BF16),
            pltpu.VMEM((2, rows, width), BF16),
            pltpu.VMEM((rows, width), F32),
            pltpu.VMEM((2, rows, width), BF16),
            pltpu.VMEM((2 * n_tp, rows, width), BF16),
            pltpu.VMEM((full_len, q_cols), BF16),
            pltpu.VMEM((full_len, heads), BF16),
            pltpu.VMEM((full_len, LANES), F32),
            pltpu.VMEM((full_len, LANES), F32),
            pltpu.VMEM(w_o.shape, BF16),
            pltpu.VMEM((n_swap, 2, depth, 2 * units), BF16),
            pltpu.VMEM((depth, 2 * units), BF16),
            pltpu.VMEM((n_swap, 2, depth, units), BF16),
            pltpu.VMEM((depth, units), BF16),
            pltpu.VMEM((depth, 2 * units), BF16),
            pltpu.VMEM((depth, units), BF16),
            pltpu.VMEM((n_add, 2, depth, q_cols), BF16),
            pltpu.VMEM((n_add, 2, depth, compact), BF16),
            pltpu.SemaphoreType.DMA((n_sems,)),
            pltpu.SemaphoreType.DMA((n_sems,)),
            pltpu.SemaphoreType.DMA((24 + 6 * n_z,)),
        ],
        compiler_params=pltpu.CompilerParams(
            collective_id=2, has_side_effects=True, vmem_limit_bytes=BACK_LIMIT
        ),
        name="back",
    )(*args)


def body(
    tokens,
    segments,
    attn_gain,
    q_weight,
    k_weight,
    v_weight,
    o_weight,
    ffn_gain,
    gate_weight,
    up_weight,
    down_weight,
    cotangent,
):
    n_z = lax.axis_size("fsdp")
    n_tp = lax.axis_size("tp")
    _, half_len, width = tokens.shape
    full_len = segments.shape[1]
    rows = half_len // n_tp
    units = gate_weight.shape[1] // 4
    scale = HEAD_DIM ** (-0.5)

    extra = jnp.pad(jnp.stack([attn_gain, ffn_gain], axis=1), ((0, 0), (0, 30)))
    x_here = tokens.reshape(half_len, width)
    dy_here = cotangent.reshape(half_len, width)
    seg = segments.reshape(full_len)
    seg_col, seg_row = seg[:, None], seg[None, :]
    (
        w_heads, w_o, w3, gains, norm_attn, dy_all, norm_all, attn, rot, stats, mid, cos, sin, spread, sel,
    ) = front(
        n_z, n_tp, scale, x_here, dy_here,
        (q_weight, k_weight, v_weight, o_weight, gate_weight, up_weight, down_weight),
        extra, seg_col, seg_row,
    )
    w3 = w3.reshape(width, -1)
    norm_all = norm_all.reshape(4 * n_tp, rows, width)
    dy_all = dy_all.reshape(4 * n_tp, rows, width)
    d_gu, hidden = act(norm_all, dy_all, w3, units)
    gu_src, dn_src = terms(norm_all, dy_all, d_gu, hidden, n_z)
    output, input_grad, gu_four, dn_four, o_two, in_two = back(
        n_z, n_tp, scale, units, wide_of(units),
        x_here, dy_here, w3, d_gu.reshape(2, 2 * n_tp, rows, 2 * units),
        hidden.reshape(2, 2 * n_tp, rows, units), gu_src, dn_src, w_o, w_heads,
        norm_attn.reshape(2 * n_tp, rows, width),
        mid, gains, rot, attn, stats, cos, sin, seg_col, seg_row, sel, spread,
    )
    q_grad, k_grad, v_grad, o_grad, gate_grad, up_grad, down_grad, sums = finish(
        gu_four, dn_four, o_two, in_two, q_weight, k_weight, v_weight, gate_weight, up_weight,
        o_weight.shape, down_weight.shape,
    )
    gain_sums = sum_tp(sums[:, :2])
    attn_gain_grad = gain_sums[:, 0] / attn_gain.astype(F32)
    ffn_gain_grad = gain_sums[:, 1] / ffn_gain.astype(F32)

    return (
        output.reshape(tokens.shape),
        input_grad.reshape(tokens.shape),
        attn_gain_grad,
        q_grad,
        k_grad,
        v_grad,
        o_grad,
        ffn_gain_grad,
        gate_grad,
        up_grad,
        down_grad,
    )


def solution(mesh):
    specs = dict(
        tok=P("fsdp", "ctx", None),
        gain=P(("fsdp", "ctx")),
        row=P(("fsdp", "ctx"), "tp"),
        col=P("tp", ("fsdp", "ctx")),
    )
    tok, gain, row, col = specs["tok"], specs["gain"], specs["row"], specs["col"]
    return jax.shard_map(
        body,
        mesh=mesh,
        in_specs=(tok, P("fsdp", None), gain, row, row, row, col, gain, row, row, col, tok),
        out_specs=(tok, tok, gain, row, row, row, col, gain, row, row, col),
        check_vma=False,
    )
```

```python
import math

import jax
import jax.numpy as jnp
from jax import lax
from jax.experimental import pallas as pl
from jax.experimental.pallas import tpu as pltpu
from jax.sharding import PartitionSpec as P

HEAD_DIM = 80
HALF = HEAD_DIM // 2
LANES = 128
NORM_EPS = 1e-05
ROPE_BASE = 10000.0
MASK_FILL = -1000000000.0
F32 = jnp.float32
BF16 = jnp.bfloat16


def pp(value, axis, mask):
    size = lax.axis_size(axis)
    return lax.ppermute(value, axis, [(i, i ^ mask) for i in range(size)])


def dot(a, b, dims=((1,), (0,))):
    return lax.dot_general(a, b, (dims, ((), ())), preferred_element_type=F32)


def in_order(bit, mine, other, axis=0):
    return jnp.where(
        bit == 0, jnp.stack([mine, other], axis), jnp.stack([other, mine], axis)
    )


def pick(blocks, index):
    return lax.dynamic_index_in_dim(blocks, index, 0, keepdims=False)


def attend_rows(scale, block, i, rot, seg_col, seg_row, sel, attn, stats):
    n_q = rot.shape[1] // LANES - 2
    rows = slice(i * block, (i + 1) * block)
    keys = (i + 1) * block
    q_pos = i * block + lax.broadcasted_iota(jnp.int32, (block, keys), 0)
    k_pos = lax.broadcasted_iota(jnp.int32, (block, keys), 1)
    allowed = (seg_col[rows, :] == seg_row[:, :keys]) & (k_pos <= q_pos)
    k = rot[:keys, n_q * LANES : (n_q + 1) * LANES]
    v = rot[:keys, (n_q + 1) * LANES :]
    outs, maxes, totals = [], [], []
    for h in range(n_q):
        s = dot(rot[rows, h * LANES : (h + 1) * LANES], k, ((1,), (1,))) * scale
        s = jnp.where(allowed, s, MASK_FILL)
        top = jnp.max(s, axis=1, keepdims=True)
        e = jnp.exp(s - top)
        total = jnp.sum(e, axis=1, keepdims=True)
        outs.append(dot((e * (1.0 / total)).astype(BF16), v).astype(BF16))
        maxes.append(top)
        totals.append(total)
    attn[rows, :] = dot(jnp.concatenate(outs, axis=1), sel[...]).astype(BF16)
    stats[rows, :] = jnp.concatenate(maxes + totals, axis=1)


def turn_back(u, cos, sin, rows):
    return (u * cos[rows, :] - pltpu.roll(u, 64, 1) * sin[rows, :]).astype(BF16)


def attend_back_rows(
    scale, block, i, rot, d_attn, stats, cos, sin, seg_col, seg_row, sel, d_qkv, dk_sum, dv_sum
):
    n_q = rot.shape[1] // LANES - 2
    rows = slice(i * block, (i + 1) * block)
    keys = (i + 1) * block
    q_pos = i * block + lax.broadcasted_iota(jnp.int32, (block, keys), 0)
    k_pos = lax.broadcasted_iota(jnp.int32, (block, keys), 1)
    allowed = (seg_col[rows, :] == seg_row[:, :keys]) & (k_pos <= q_pos)
    k = rot[:keys, n_q * LANES : (n_q + 1) * LANES]
    v = rot[:keys, (n_q + 1) * LANES :]
    d_out = dot(d_attn[rows, :], sel[...], ((1,), (1,))).astype(BF16)
    stat = stats[rows, :]
    for h in range(n_q):
        q = rot[rows, h * LANES : (h + 1) * LANES]
        d_h = d_out[:, h * LANES : (h + 1) * LANES]
        s = dot(q, k, ((1,), (1,))) * scale
        s = jnp.where(allowed, s, MASK_FILL)
        p = jnp.exp(s - stat[:, h : h + 1]) * (1.0 / stat[:, n_q + h : n_q + h + 1])
        dv_sum[:keys, :] += dot(p.astype(BF16), d_h, ((0,), (0,)))
        d_p = dot(d_h, v, ((1,), (1,)))
        d_s = (p * (d_p - jnp.sum(p * d_p, axis=1, keepdims=True))).astype(BF16)
        d_q = (dot(d_s, k) * scale).astype(BF16).astype(F32)
        d_qkv[rows, h * LANES : (h + 1) * LANES] = turn_back(d_q, cos, sin, rows)
        dk_sum[:keys, :] += dot(d_s, q, ((0,), (0,)))


def attend_back_keys(scale, n_q, cos, sin, d_qkv, dk_sum, dv_sum):
    d_k = (dk_sum[...] * scale).astype(BF16).astype(F32)
    d_qkv[:, n_q * LANES : (n_q + 1) * LANES] = turn_back(d_k, cos, sin, slice(None))
    d_qkv[:, (n_q + 1) * LANES :] = dv_sum[...].astype(BF16)


VMEM_LIMIT = 56 * 1024 * 1024
BACK_LIMIT = 62 * 1024 * 1024


def sum_tp(value):
    others = [pp(value, "tp", mask) for mask in range(1, lax.axis_size("tp"))]
    return value, others


def below(top):
    masks = []
    while top > 1:
        top //= 2
        masks.append(top)
    return masks


def flip(index, mask):
    return index + mask * (1 - 2 * ((index // mask) % 2))


def flip_all(index, bits):
    mask = 1
    while mask <= bits:
        if bits & mask:
            index = flip(index, mask)
        mask *= 2
    return index


class Links:
    def __init__(self, send_sems, recv_sems):
        self.sems = (send_sems, recv_sems)
        self.copies = []
        self.count = 0

    def send(self, src, dst, peer, kept=False):
        k = self.count
        self.count += 1
        copy = pltpu.make_async_remote_copy(
            src_ref=src,
            dst_ref=dst,
            send_sem=self.sems[0].at[k],
            recv_sem=self.sems[1].at[k],
            device_id=peer,
            device_id_type=pl.DeviceIdType.MESH,
        )
        copy.start()
        if not kept:
            self.copies.append(copy)
        return copy

    def finish(self, *sums):
        for copy in self.copies:
            copy.wait_send()
        for layer in sums:
            layer.drain()


def greet(peers):
    barrier = pltpu.get_barrier_semaphore()
    for peer in peers:
        pl.semaphore_signal(barrier, inc=1, device_id=peer, device_id_type=pl.DeviceIdType.MESH)
    pl.semaphore_wait(barrier, len(peers))


class Place:
    def __init__(self, n_z, n_tp):
        self.n_z, self.n_tp = n_z, n_tp
        self.z, self.y, self.t = (lax.axis_index(a) for a in ("fsdp", "ctx", "tp"))
        self.me = self.y * n_tp + self.t
        self.core = {"tp": flip(self.t, 1)}
        self.x = {"tp": flip(self.t, 2)}
        self.yy = {"ctx": 1 - self.y}
        self.masks = below(n_z)
        self.zb = self.z // (n_z // 2)

    def zz(self, mask):
        return {"fsdp": flip(self.z, mask)}

    def peers(self):
        return [self.core, self.x, self.yy] + [self.zz(m) for m in self.masks]


class WeightFlow:
    def __init__(self, links, at, out, cross, first, second):
        self.links, self.at, self.out = links, at, out
        self.first, self.second = first, second
        self.got = {}
        self.y_copy = links.send(cross, second(None), at.yy)

    def own(self):
        at = self.at
        for m in at.masks:
            dst = self.out.at[at.z, at.y]
            self.got[m, 0] = self.links.send(self.first(m), dst, at.zz(m))

    def crossed(self):
        at = self.at
        self.y_copy.wait_recv()
        for m in at.masks:
            dst = self.out.at[at.z, 1 - at.y]
            self.got[m, 1] = self.links.send(self.second(m), dst, at.zz(m))

    def take(self, rel, part):
        at = self.at
        self.got[rel, part].wait_recv()
        low = rel & -rel
        row = at.y if part == 0 else 1 - at.y
        block = self.out.at[flip_all(at.z, rel), row]
        for m in at.masks:
            if m < low:
                self.got[rel ^ m, part] = self.links.send(block, block, at.zz(m))

    def order(self):
        rels = [r for r in range(1, self.at.n_z)]
        return sorted(rels, key=lambda r: (bin(r).count("1"), -(r & -r), r))


def half_rows(ref, part, rows):
    return ref.at[pl.ds(part * (rows // 2), rows // 2)]


class LayerGather:
    def __init__(self, links, at, out, rows):
        self.links, self.at, self.out, self.rows = links, at, out, rows
        self.cores = []
        self.sent = []

    def half(self, index, part):
        return half_rows(self.out.at[index], part, self.rows)

    def send(self, src, dst, peer):
        self.sent.append(self.links.send(src, dst, peer, kept=True))
        return self.sent[-1]

    def pass_on(self, index, part, peer):
        block = self.half(index, part)
        return self.send(block, block, peer)

    def own(self, part, src=None):
        at, me = self.at, self.at.me
        a = self.half(me, part)
        src = a if src is None else src
        send = lambda peer: self.send(src, a, peer)
        if part == 0:
            self.xa, self.ya = send(at.x), send(at.yy)
        else:
            self.yb, self.xb = send(at.yy), send(at.x)
        self.cores.append(send(at.core))

    def to_core(self, index, part):
        self.cores.append(self.pass_on(index, part, self.at.core))

    def far_first(self):
        at = self.at
        self.x_of, self.y_of = flip(at.me, 2), flip(at.me, at.n_tp)
        self.diag = flip(self.x_of, at.n_tp)
        self.xa.wait_recv()
        self.y_fwd = self.pass_on(self.x_of, 0, at.yy)
        self.to_core(self.x_of, 0)
        self.yb.wait_recv()
        self.x_fwd = self.pass_on(self.y_of, 1, at.x)
        self.to_core(self.y_of, 1)

    def far_second(self):
        self.ya.wait_recv()
        self.to_core(self.y_of, 0)
        self.xb.wait_recv()
        self.to_core(self.x_of, 1)
        self.y_fwd.wait_recv()
        self.to_core(self.diag, 0)
        self.x_fwd.wait_recv()
        self.to_core(self.diag, 1)

    def last(self):
        for copy in self.cores:
            copy.wait_recv()

    def drain(self):
        for copy in self.sent:
            copy.wait_send()


class LayerSum:
    def __init__(self, links, at, rows, bufs, product, after=None):
        self.links, self.at, self.rows = links, at, rows
        self.to_core, self.held, self.landed, self.total, self.free = bufs
        self.product = product
        self.after = after

    def peers(self):
        return (self.at.core, self.at.x, self.at.yy)

    def tiles(self, some):
        width = self.total.shape[1]
        tile = 512 if width % 512 == 0 else width

        def body(c, carry):
            some(pl.ds(pl.multiple_of(c * tile, tile), tile))
            return carry

        lax.fori_loop(0, width // tile, body, 0)

    def drain(self):
        for copy in self.sent:
            copy.wait_send()
        self.sent = []

    def release(self):
        self.drain()
        for i, peer in enumerate(self.peers()):
            pl.semaphore_signal(
                self.free.at[i], inc=1, device_id=peer, device_id_type=pl.DeviceIdType.MESH
            )

    def begin(self):
        self.core = {}
        if self.after is not None:
            self.after.drain()
            for i in range(3):
                pl.semaphore_wait(self.free.at[i], 1)
        sent = []
        for i, k in enumerate((3, 1, 2, 0)):
            if i >= 2:
                sent[i - 2].wait_send()


            def some(cols, i=i, k=k):
                self.to_core[i % 2, :, cols] = self.product(2 * k + 1, cols).astype(BF16)

            self.tiles(some)
            self.core[k] = self.links.send(
                self.to_core.at[i % 2], self.held.at[k], self.at.core, kept=True
            )
            sent.append(self.core[k])
        self.sent = sent[2:]

    def middle(self):
        at, rows, h = self.at, self.rows, self.rows // 2
        held, landed = self.held, self.landed
        a, b = slice(0, h), slice(h, rows)

        def level(k):
            self.core[k].wait_recv()

            def some(cols):
                value = self.product(2 * k, cols) + held[k, :, cols].astype(F32)
                if k == 0:
                    self.total[:, cols] = value
                else:
                    held[k, :, cols] = value.astype(BF16)

            self.tiles(some)

        def send(k, i, peer):
            copy = self.links.send(held.at[k, pl.ds((i % 2) * h, h)], landed.at[i], peer, kept=True)
            self.sent.append(copy)
            return copy

        level(3)
        x1 = send(3, 0, at.x)
        y1 = send(3, 1, at.yy)
        level(1)
        x2 = send(1, 2, at.x)
        level(2)
        y2 = send(2, 3, at.yy)
        level(0)
        x1.wait_recv()
        held[2, a] = (held[2, a].astype(F32) + landed[0].astype(F32)).astype(BF16)
        y3 = send(2, 4, at.yy)
        y1.wait_recv()
        held[1, b] = (held[1, b].astype(F32) + landed[1].astype(F32)).astype(BF16)
        x3 = send(1, 5, at.x)
        self.tail = (x2, y3, y2, x3)

    def end(self):
        h = self.rows // 2
        landed, total = self.landed, self.total
        for copy in self.tail:
            copy.wait_recv()
        top = total[:h, :] + landed[2].astype(F32) + landed[4].astype(F32)
        low = total[h:, :] + landed[3].astype(F32) + landed[5].astype(F32)
        return top, low


def sum_scratch(rows, width):
    return [
        pltpu.VMEM((2, rows, width), BF16),
        pltpu.VMEM((4, rows, width), BF16),
        pltpu.VMEM((6, rows // 2, width), BF16),
        pltpu.VMEM((rows, width), F32),
        pltpu.SemaphoreType.REGULAR((3,)),
    ]


def eye(n):
    shape = (n, n)
    same = lax.broadcasted_iota(jnp.int32, shape, 0) == lax.broadcasted_iota(jnp.int32, shape, 1)
    return same.astype(F32).astype(BF16)


def column(row):
    n = row.shape[1]
    same = lax.broadcasted_iota(jnp.int32, (n, n), 0) == lax.broadcasted_iota(jnp.int32, (n, n), 1)
    return jnp.sum(jnp.where(same, row.astype(F32), 0.0), axis=1, keepdims=True)


def head_spread(n_q, compact):
    shape = (compact, (n_q + 2) * LANES)
    col, lane = (lax.broadcasted_iota(jnp.int32, shape, d) for d in (0, 1))
    at, head = col % HEAD_DIM, col // HEAD_DIM
    spot = head * LANES + at + jnp.where((at >= HALF) & (head < n_q + 1), 64 - HALF, 0)
    return ((spot == lane) & (head < n_q + 2)).astype(F32).astype(BF16)


def head_select(n_q):
    shape = (n_q * LANES, n_q * HEAD_DIM)
    lane, col = (lax.broadcasted_iota(jnp.int32, shape, d) for d in (0, 1))
    return ((col // HEAD_DIM) * LANES + col % HEAD_DIM == lane).astype(F32).astype(BF16)


def front_kernel(
    n_z, n_tp, scale, q_block,
    x_here, dy_here, q_w, k_t, v_t, o_t, gate_w, up_w, down_t, gain_rows, seg_row,
    w_heads, w_o, w3, gains, norm_attn, dy_all, norm_all, attn, rot, stats, mid, cos, sin, spread, sel, seg_col,
    w_in, x_all, qkv, to_core, held, landed, total, free, in_cross, o_cross, w3_cross,
    heads_v, norm_v, own_v, root_v, o_v, in_send, o_send, w3_send, send_sems, recv_sems, sems,
):
    at = Place(n_z, n_tp)
    links = Links(send_sems, recv_sems)
    z, y, t, me = at.z, at.y, at.t, at.me
    zb = z // (n_z // 2)
    n_b, rows, width = 2 * n_tp, x_all.shape[0] // (2 * n_tp), x_all.shape[1]
    depth = in_send.shape[1]
    full_len = x_all.shape[0]
    local = []

    def move(src, dst):
        copy = pltpu.make_async_copy(src, dst, sems.at[len(local)])
        copy.start()
        local.append(copy)
        return copy

    def block_of(ref, index):
        return ref.at[pl.ds(pl.multiple_of(index * rows, rows), rows)]

    q_cols, kv_cols = q_w.shape[1] // 2, k_t.shape[0] // 2
    units = gate_w.shape[1] // 4
    wide = w3_send.shape[3] - units
    extra = jnp.concatenate(
        [column(gain_rows[i : i + 1, :]) for i in range(2)]
        + [jnp.zeros((depth, in_send.shape[2] - q_cols - 2 * kv_cols - 2), F32)],
        axis=1,
    ).astype(BF16)
    for j in range(2):
        kv = slice(j * kv_cols, (j + 1) * kv_cols)
        turned = [dot(w[kv, :], eye(kv_cols), ((0,), (0,))).astype(BF16) for w in (k_t, v_t)]
        in_send[j] = jnp.concatenate(
            [q_w[:, j * q_cols : (j + 1) * q_cols], *turned, extra], axis=1
        )
    greet(at.peers())
    f_in = WeightFlow(
        links, at, w_in, in_send.at[1 - y], lambda m: in_send.at[y], lambda m: in_cross
    )
    f_in.own()
    own_in = move(in_send.at[y], w_in.at[z, y])
    x_mine = block_of(x_here, t)
    tok_y = links.send(x_mine, block_of(x_all, me), at.yy)
    x_own = move(x_here, x_all.at[pl.ds(pl.multiple_of(y * (full_len // 2), full_len // 2), full_len // 2)])
    dy_mine = block_of(dy_here, t)
    dy_own = move(dy_here.reshape(n_tp, rows, width), dy_all.at[0, pl.ds(y * n_tp, n_tp)])

    for j in range(2):
        o_send[j] = o_t[:, j * q_cols : (j + 1) * q_cols]
    for j in range(4):
        cols = slice(j * units, (j + 1) * units)
        w3_send[j % 2, j // 2, :, : 2 * units] = jnp.concatenate(
            [gate_w[:, cols], up_w[:, cols]], axis=1
        )
        w3_send[j % 2, j // 2, :, wide:] = down_t[:, cols]
    f_in.crossed()
    cross_in = move(in_cross, w_in.at[z, 1 - y])
    f_o = WeightFlow(
        links, at, w_o, o_send.at[1 - y], lambda m: o_send.at[y], lambda m: o_cross
    )
    top = n_z // 2
    tok_y.wait_recv()
    f_3 = WeightFlow(
        links, at, w3, w3_send.at[1 - y],
        lambda m: w3_send.at[y, 1 - zb if m == top else zb],
        lambda m: w3_cross if m is None else w3_cross.at[1 - zb if m == top else zb],
    )
    dy_y = links.send(dy_mine, dy_all.at[0, me], at.yy)
    y_of, x_of = flip(me, n_tp), flip(me, 2)
    y_block = block_of(x_all, y_of)
    tok_x = links.send(y_block, y_block, at.x)
    tok_c = [links.send(y_block, y_block, at.core)]
    ins = [(rel, p) for rel in f_in.order() for p in (0, 1)]
    for rel, p in ins:
        if rel == top:
            f_in.take(rel, p)
    lane = lax.broadcasted_iota(jnp.int32, (1, LANES), 1)
    within = lane % 64
    frequency = jnp.where(
        within < HALF, jnp.exp(within.astype(F32) * (-2.0 * math.log(ROPE_BASE) / HEAD_DIM)), 0.0
    )
    sign = jnp.where(lane < 64, -1.0, 1.0)
    n_q = rot.shape[1] // LANES - 2
    spread[...] = head_spread(n_q, w_in.shape[3])
    sel[...] = head_select(n_q)
    step = min(256, full_len)

    def tables(c, carry):
        at_rows = pl.ds(pl.multiple_of(c * step, step), step)
        mine = jnp.concatenate(
            [
                column(seg_row[:, pl.ds(pl.multiple_of(c * step + i, LANES), LANES)])
                for i in range(0, step, LANES)
            ],
            axis=0,
        ).astype(jnp.int32)
        seg_col[at_rows, :] = mine
        before = jnp.where(seg_row[...] < mine, 1.0, 0.0)
        start = jnp.sum(before, axis=1, keepdims=True)
        position = (c * step + lax.broadcasted_iota(jnp.int32, (step, 1), 0)).astype(F32)
        angles = (position - start) * frequency
        cos[at_rows, :] = jnp.cos(angles)
        sin[at_rows, :] = jnp.sin(angles) * sign
        return carry

    lax.fori_loop(0, full_len // step, tables, 0)
    tok_x.wait_recv()
    diag = block_of(x_all, flip(y_of, 2))
    tok_c.append(links.send(diag, diag, at.core))
    x_own.wait()

    for copy in tok_c:
        copy.wait_recv()

    def find_root(c, carry):
        at_rows = pl.ds(pl.multiple_of(c * step, step), step)
        value = x_all[at_rows, :].astype(F32)
        root_v[at_rows, :] = lax.rsqrt(jnp.mean(value * value, axis=1, keepdims=True) + NORM_EPS)
        return carry

    lax.fori_loop(0, full_len // step, find_root, 0)
    own_in.wait()
    cross_in.wait()

    pick_gain = (
        lax.broadcasted_iota(jnp.int32, (8, w_in.shape[3]), 1)
        == sel.shape[1] // HEAD_DIM * HEAD_DIM + 2 * HEAD_DIM + lax.broadcasted_iota(jnp.int32, (8, w_in.shape[3]), 0)
    ).astype(F32).astype(BF16)

    group = 1
    while 2 * depth * group % LANES:
        group *= 2
    span = 2 * depth * group

    def project(rel, first):
        owner = flip_all(z, rel) // group
        cols = pl.ds(pl.multiple_of(owner * span, span), span)
        weights = w_in[pl.ds(owner * group, group)].reshape(span, w_in.shape[3])
        gain = dot(pick_gain, weights, ((1,), (1,)))
        gains[:, cols] = gain
        heads = dot(weights, spread[...]).astype(BF16)
        heads_v[cols, :] = heads

        def some_rows(c, carry):
            at_rows = pl.ds(pl.multiple_of(c * step, step), step)
            value = (x_all[at_rows, cols].astype(F32) * root_v[at_rows, :] * gain[0:1, :]).astype(BF16)
            norm_v[at_rows, cols] = value
            term = dot(value, heads)
            qkv[at_rows, :] = term if first else qkv[at_rows, :] + term
            return carry

        lax.fori_loop(0, full_len // step, some_rows, 0)

    f_o.own()
    f_o.crossed()
    if group == 1:
        project(0, True)
    rest = [rel for rel in f_in.order() if rel != top]
    for rel in [top] + rest:
        if rel != top:
            for p in (0, 1):
                f_in.take(rel, p)
        if rel == rest[-1]:
            f_3.own()
        if group == 1:
            project(rel, False)
    if group > 1:
        for rel in range(0, n_z, group):
            project(rel, rel == 0)
    heads_out = move(heads_v, w_heads)
    norm_out = move(norm_v, norm_attn)
    own_o = [move(o_send.at[y], w_o.at[z, y]), move(o_cross, w_o.at[z, 1 - y])]
    dy_y.wait_recv()
    dy_x = links.send(dy_all.at[0, y_of], dy_all.at[0, y_of], at.x)
    dy_c = [links.send(dy_all.at[0, y_of], dy_all.at[0, y_of], at.core)]
    for p in (0, 1):
        f_o.take(top, p)

    def turn(c, carry):
        r = pl.ds(pl.multiple_of(c * step, step), step)
        for h in range(n_q + 1):
            u = qkv[r, h * LANES : (h + 1) * LANES]
            rot[r, h * LANES : (h + 1) * LANES] = (
                u * cos[r, :] + pltpu.roll(u, 64, 1) * sin[r, :]
            ).astype(BF16)
        rot[r, (n_q + 1) * LANES :] = qkv[r, (n_q + 1) * LANES :].astype(BF16)
        return carry

    lax.fori_loop(0, full_len // step, turn, 0)
    dy_far = LayerGather(links, at, dy_all.at[1], rows)
    for i in range(full_len // q_block):
        attend_rows(scale, q_block, i, rot, seg_col, seg_row, sel, attn, stats)
        if i == 0:
            dy_x.wait_recv()
            d_of = flip(y_of, 2)
            dy_c.append(links.send(dy_all.at[0, d_of], dy_all.at[0, d_of], at.core))
        if i == 2:
            f_3.crossed()
            own_3 = [move(w3_send.at[y, zb], w3.at[z, y]), move(w3_cross.at[zb], w3.at[z, 1 - y])]
            dy_z = [
                links.send(
                    half_rows(dy_mine, p, rows), half_rows(dy_all.at[1, me], p, rows), at.zz(top)
                )
                for p in (0, 1)
            ]
    for rel in f_o.order():
        for p in (0, 1):
            if rel != top:
                f_o.take(rel, p)
    for copy in own_o:
        copy.wait()
    load_o = move(w_o.reshape(width, o_v.shape[1]), o_v)
    load_o.wait()

    def product(r, cols):
        lhs = attn[pl.ds(pl.multiple_of(flip_all(me, r) * rows, rows), rows), :]
        return dot(lhs, o_v[cols, :], ((1,), (1,)))

    layer = LayerSum(links, at, rows, (to_core, held, landed, total, free), product)
    layer.begin()
    layer.middle()
    norm_own = LayerGather(links, at, norm_all.at[0], rows)
    norm_far = LayerGather(links, at, norm_all.at[1], rows)
    far = []
    h = rows // 2
    load_x = move(x_mine, own_v)
    load_x.wait()
    for p, value in enumerate(layer.end()):
        r = slice(p * h, (p + 1) * h)
        value = value + own_v[r, :].astype(F32)
        mid[r, :] = value
        root = lax.rsqrt(jnp.mean(value * value, axis=1, keepdims=True) + NORM_EPS)
        own_v[r, :] = (value * root * gains[1:2, :]).astype(BF16)
        src = own_v.at[pl.ds(p * h, h)]
        far.append(links.send(src, half_rows(norm_all.at[1, me], p, rows), at.zz(top)))
        norm_own.own(p, src)
    keep = move(own_v, norm_all.at[0, me])
    norm_own.far_first()
    norm_own.far_second()
    for p in (0, 1):
        dy_z[p].wait_recv()
        dy_far.own(p)
    dy_far.far_first()
    for p in (0, 1):
        f_3.take(top, p)
    dy_far.far_second()
    for p in (0, 1):
        far[p].wait_recv()
        norm_far.own(p)
    norm_far.far_first()
    norm_far.far_second()
    for rel in f_3.order():
        for p in (0, 1):
            if rel != top:
                f_3.take(rel, p)
    for gather in (norm_own, dy_far, norm_far):
        gather.last()
        gather.drain()
    for copy in dy_c:
        copy.wait_recv()
    for copy in [dy_own, heads_out, norm_out, keep] + own_3:
        copy.wait()
    links.finish(layer)


def front(n_z, n_tp, scale, x_here, dy_here, weights, gain_rows, seg_row):
    q_w, k_t, _, _, gate_w, _, _ = weights
    half_len, width = x_here.shape
    full_len = 2 * half_len
    rows = half_len // n_tp
    depth, q_cols = q_w.shape[0], q_w.shape[1] // 2
    n_q = q_cols // HEAD_DIM
    heads = (n_q + 2) * LANES
    compact = q_cols + k_t.shape[0] + 32
    units = gate_w.shape[1] // 4
    w3_cols = wide_of(units) + units
    any_, vmem = pl.BlockSpec(memory_space=pl.ANY), pl.BlockSpec(memory_space=pltpu.VMEM)
    n_sems = 80 + 6 * n_z + 32
    shape = jax.ShapeDtypeStruct
    return pl.pallas_call(
        lambda *refs: front_kernel(n_z, n_tp, scale, min(256, full_len), *refs),
        out_shape=(
            shape((width, heads), BF16),
            shape((n_z, 2, depth, q_cols), BF16),
            shape((n_z, 2, depth, w3_cols), BF16),
            shape((8, width), F32),
            shape((full_len, width), BF16),
            shape((2, 2 * n_tp, rows, width), BF16),
            shape((2, 2 * n_tp, rows, width), BF16),
            shape((full_len, q_cols), BF16),
            shape((full_len, heads), BF16),
            shape((full_len, 2 * n_q), F32),
            shape((rows, width), F32),
            shape((full_len, LANES), F32),
            shape((full_len, LANES), F32),
            shape((compact, heads), BF16),
            shape((n_q * LANES, q_cols), BF16),
            shape((full_len, 1), jnp.int32),
        ),
        in_specs=[any_] * 2 + [vmem] * 9,
        out_specs=(any_, any_, any_, vmem, any_, any_, any_) + (vmem,) * 9,
        scratch_shapes=[
            pltpu.VMEM((n_z, 2, depth, compact), BF16),
            pltpu.VMEM((full_len, width), BF16),
            pltpu.VMEM((full_len, heads), F32),
            *sum_scratch(rows, width),
            pltpu.VMEM((depth, compact), BF16),
            pltpu.VMEM((depth, q_cols), BF16),
            pltpu.VMEM((2, depth, w3_cols), BF16),
            pltpu.VMEM((width, heads), BF16),
            pltpu.VMEM((full_len, width), BF16),
            pltpu.VMEM((rows, width), BF16),
            pltpu.VMEM((full_len, 1), F32),
            pltpu.VMEM((width, q_cols), BF16),
            pltpu.VMEM((2, depth, compact), BF16),
            pltpu.VMEM((2, depth, q_cols), BF16),
            pltpu.VMEM((2, 2, depth, w3_cols), BF16),
            pltpu.SemaphoreType.DMA((n_sems,)),
            pltpu.SemaphoreType.DMA((n_sems,)),
            pltpu.SemaphoreType.DMA((16,)),
        ],
        compiler_params=pltpu.CompilerParams(
            collective_id=1, has_side_effects=True, vmem_limit_bytes=VMEM_LIMIT
        ),
        name="front",
    )(x_here, dy_here, *weights, gain_rows, seg_row)


def wide_of(units):
    return -(-2 * units // LANES) * LANES


def act_kernel(norm, dy, w3, d_gu, hidden):
    units = hidden.shape[2]
    n = norm.shape[0] * norm.shape[1]
    wide = w3.shape[1] - units
    gate_up = dot(norm[...].reshape(n, norm.shape[2]), w3[:, : 2 * units])
    d_hidden = dot(dy[...].reshape(n, dy.shape[2]), w3[:, wide:])
    gate, up = gate_up[:, :units], gate_up[:, units:]
    sig = 1.0 / (1.0 + jnp.exp(-gate))
    silu = gate * sig
    hidden[...] = (silu * up).astype(BF16).reshape(hidden.shape)
    d_up = (d_hidden * silu).astype(BF16)
    d_gate = (d_hidden * up * sig * (1.0 + gate * (1.0 - sig))).astype(BF16)
    d_gu[...] = jnp.concatenate([d_gate, d_up], axis=1).reshape(d_gu.shape)


def act(norm, dy, w3, units):
    blocks, rows, width = norm.shape
    per = max(1, 512 // rows)
    one = lambda cols: pl.BlockSpec((per, rows, cols), lambda i: (i, 0, 0))
    return pl.pallas_call(
        act_kernel,
        grid=(blocks // per,),
        out_shape=(
            jax.ShapeDtypeStruct((blocks, rows, 2 * units), BF16),
            jax.ShapeDtypeStruct((blocks, rows, units), BF16),
        ),
        in_specs=[one(width), one(width), pl.BlockSpec(w3.shape, lambda i: (0, 0))],
        out_specs=(one(2 * units), one(units)),
        compiler_params=pltpu.CompilerParams(vmem_limit_bytes=VMEM_LIMIT),
        name="act",
    )(norm, dy, w3)


def terms_kernel(norm, dy, d_gu, hidden, gu, dn):
    def term(lhs, rhs, out):
        n = lhs.shape[0] * lhs.shape[1]
        value = dot(lhs[...].reshape(n, lhs.shape[2]), rhs[...].reshape(n, rhs.shape[2]), ((0,), (0,)))
        out[...] = value.astype(BF16).reshape(out.shape)

    term(norm, d_gu, gu)
    term(dy, hidden, dn)


def terms(norm, dy, d_gu, hidden, n_z):
    blocks, rows, width = norm.shape
    depth, units = width // n_z // 2, hidden.shape[2]
    group = 1
    while 2 * depth * group % LANES:
        group *= 2
    cols = pl.BlockSpec((blocks, rows, 2 * depth * group), lambda i: (0, 0, i))
    whole = lambda a: pl.BlockSpec(a.shape, lambda i: (0, 0, 0))
    out = lambda c: pl.BlockSpec((group, 2, depth, c), lambda i: (i, 0, 0, 0))
    return pl.pallas_call(
        terms_kernel,
        grid=(n_z // group,),
        out_shape=(
            jax.ShapeDtypeStruct((n_z, 2, depth, 2 * units), BF16),
            jax.ShapeDtypeStruct((n_z, 2, depth, units), BF16),
        ),
        in_specs=[cols, cols, whole(d_gu), whole(hidden)],
        out_specs=(out(2 * units), out(units)),
        compiler_params=pltpu.CompilerParams(vmem_limit_bytes=VMEM_LIMIT),
        name="terms",
    )(norm, dy, d_gu, hidden)


def finish_in_kernel(gu, ins, q_w, k_t, v_t, gate_w, up_w, q_grad, k_grad, v_grad, sums):
    depth = q_w.shape[0]
    units, q_cols, kv_cols = gu.shape[3] // 2, q_w.shape[1] // 2, k_t.shape[0] // 2
    one = eye(depth)
    q_grad[...] = jnp.concatenate([ins[j, :, :q_cols].astype(F32) for j in range(2)], axis=1)
    first = jnp.sum(q_w[...].astype(F32) * q_grad[...], axis=1, keepdims=True)
    lo = q_cols
    for w, grad in ((k_t, k_grad), (v_t, v_grad)):
        for j in range(2):
            grad[j * kv_cols : (j + 1) * kv_cols, :] = dot(
                ins[j, :, lo : lo + kv_cols], one, ((0,), (0,))
            )
        lo += kv_cols
        first += column(jnp.sum(w[...].astype(F32) * grad[...], axis=0, keepdims=True))
    second = jnp.zeros((depth, 1), F32)
    for j in range(4):
        cols = slice(j * units, (j + 1) * units)
        weights = jnp.concatenate([gate_w[:, cols], up_w[:, cols]], axis=1).astype(F32)
        second += jnp.sum(weights * gu[j // 2, j % 2].astype(F32), axis=1, keepdims=True)
    lane = lax.broadcasted_iota(jnp.int32, sums.shape, 1)
    sums[...] = jnp.where(lane == 0, first, second)


def finish_in(gu, ins, q_w, k_t, v_t, gate_w, up_w):
    shape = lambda dims: jax.ShapeDtypeStruct(dims, F32)
    return pl.pallas_call(
        finish_in_kernel,
        out_shape=(
            shape(q_w.shape), shape(k_t.shape), shape(v_t.shape), shape((q_w.shape[0], LANES)),
        ),
        compiler_params=pltpu.CompilerParams(vmem_limit_bytes=VMEM_LIMIT),
        name="finish_in",
    )(gu, ins, q_w, k_t, v_t, gate_w, up_w)


def finish_kernel(gu, dn, o, rows_a, rows_b, gate_grad, up_grad, down_grad, o_grad, out_a, out_b, sems):
    copies = [
        pltpu.make_async_copy(src, dst, sems.at[i])
        for i, (src, dst) in enumerate(((rows_a, out_a), (rows_b, out_b)))
    ]
    for copy in copies:
        copy.start()
    units = dn.shape[3]
    for grad, part in ((gate_grad, slice(0, units)), (up_grad, slice(units, 2 * units))):
        grad[...] = jnp.concatenate(
            [gu[j // 2, j % 2, :, part].astype(F32) for j in range(4)], axis=1
        )
    down_grad[...] = jnp.concatenate([dn[j // 2, j % 2].astype(F32) for j in range(4)], axis=1)
    o_grad[...] = jnp.concatenate([o[j].astype(F32) for j in range(2)], axis=1)
    for copy in copies:
        copy.wait()


def finish(gu, dn, o, rows_a, rows_b):
    depth, units, q_cols = dn.shape[2], dn.shape[3], o.shape[2]
    shape = lambda cols: jax.ShapeDtypeStruct((depth, cols), F32)
    like = lambda a: jax.ShapeDtypeStruct(a.shape, a.dtype)
    any_, vmem = pl.BlockSpec(memory_space=pl.ANY), pl.BlockSpec(memory_space=pltpu.VMEM)
    return pl.pallas_call(
        finish_kernel,
        out_shape=(
            shape(4 * units), shape(4 * units), shape(4 * units), shape(2 * q_cols),
            like(rows_a), like(rows_b),
        ),
        in_specs=[vmem] * 3 + [any_] * 2,
        out_specs=(vmem,) * 4 + (any_,) * 2,
        scratch_shapes=[pltpu.SemaphoreType.DMA((2,))],
        compiler_params=pltpu.CompilerParams(vmem_limit_bytes=VMEM_LIMIT),
        cost_estimate=pl.CostEstimate(flops=0, bytes_accessed=20 * 2**20, transcendentals=0),
        name="finish",
    )(gu, dn, o, rows_a, rows_b)


class TpGather:
    def __init__(self, links, at, out):
        self.links, self.at, self.out = links, at, out

    def own(self, src):
        at = self.at
        dst = self.out.at[at.t]
        self.x = self.links.send(src, dst, at.x)
        self.cores = [self.links.send(src, dst, at.core)]

    def second(self):
        at = self.at
        self.x.wait_recv()
        block = self.out.at[flip(at.t, 2)]
        self.cores.append(self.links.send(block, block, at.core))

    def last(self):
        for copy in self.cores:
            copy.wait_recv()


class GradFlow:
    def __init__(self, links, at, src, land, swap, out, passing, fetch=None):
        self.links, self.at, self.src, self.land = links, at, src, land
        self.swap, self.out, self.passing, self.fetch = swap, out, passing, fetch
        self.adds = [m for m in reversed(at.masks) if not (swap and m == at.n_z // 2)]
        self.slot = {}
        n = 0
        for m in self.adds:
            for rel in range(0, at.n_z, 2 * m):
                self.slot[m, rel] = n
                n += 1
        self.got = {}
        self.at_mask = {}

    def row(self, part):
        return self.at.y if part == 0 else 1 - self.at.y

    def own(self, rel, part):
        return self.src.at[flip_all(self.at.z, rel), self.row(part)]

    def held(self, rel, part):
        m = self.at_mask.get((rel, part))
        if m is None:
            return self.own(rel, part), True
        return self.land.at[self.slot[m, rel], part], False

    def send(self, m, rel, part):
        block, _ = self.held(rel, part)
        self.got[m, rel ^ m, part] = self.links.send(
            block, self.land.at[self.slot[m, rel ^ m], part], self.at.zz(m)
        )

    def first(self, parts=(1, 0)):
        m = self.adds[0]
        rels = [r for r in range(self.at.n_z) if r & m]
        for rel in sorted(rels, reverse=True):
            for part in parts:
                self.send(m, rel, part)

    def add(self, m, rel, part):
        block, is_first = self.held(rel, part)
        if is_first and self.fetch is not None:
            block = self.fetch(block)
        self.got[m, rel, part].wait_recv()
        slot = self.land.at[self.slot[m, rel], part]
        slot[...] = (block[...].astype(F32) + slot[...].astype(F32)).astype(BF16)
        self.at_mask[rel, part] = m

    def spread(self):
        at = self.at
        for i, m in enumerate(self.adds):
            left = range(0, at.n_z, 2 * m)
            nxt = self.adds[i + 1] if i + 1 < len(self.adds) else (2 * m if self.swap else None)
            for rel in sorted(left, key=lambda r: -(r & (nxt or 0))):
                for part in (1, 0):
                    self.add(m, rel, part)
                    if nxt is not None and rel & nxt:
                        if nxt in self.adds:
                            self.send(nxt, rel, part)
                        else:
                            self.exchange(nxt, rel, part)

    def column(self, mine):
        return self.at.zb if mine else 1 - self.at.zb

    def exchange(self, m, rel, part):
        block, _ = self.held(rel, part)
        if part == 0:
            dst = self.out.at[self.at.zb, self.at.y]
        else:
            dst = self.passing
        self.got[m, 0, part] = self.links.send(block, dst, self.at.zz(m))

    def cross(self):
        at = self.at
        block, _ = self.held(0, 1)
        dst = self.out.at[at.zb, at.y] if self.swap else self.out.at[at.y]
        self.ends = [self.links.send(block, dst, at.yy)]

    def cross_far(self):
        at = self.at
        self.got[at.n_z // 2, 0, 1].wait_recv()
        self.ends.append(self.links.send(self.passing, self.out.at[1 - at.zb, at.y], at.yy))
        self.ends.append(self.got[at.n_z // 2, 0, 0])

    def mine(self):
        at = self.at
        dst = self.out.at[at.zb, at.y] if self.swap else self.out.at[at.y]
        return self.held(0, 0)[0], dst

    def last(self):
        for copy in self.ends:
            copy.wait_recv()


def back_kernel(
    n_z, n_tp, scale, q_block, units, wide,
    x_here, dy_here, w3, d_gu, hidden, gu_src, dn_src, w_o, w_heads, norm_attn,
    mid, gains, rot, attn, stats, cos, sin, seg_col, seg_row, sel, spread,
    output, input_grad, gu_out, dn_out, o_out, in_out,
    w3_v, gu_v, hid_v,
    to_core_a, held_a, landed_a, total_a, free_a, to_core_b, held_b, landed_b, total_b, free_b,
    far_v, far_in, d_mid, row_v, d_proj, d_attn, d_qkv, dk_sum, dv_sum, o_v,
    gu_land, gu_pass, dn_land, dn_pass, fetch_gu, fetch_dn, o_land, in_land,
    send_sems, recv_sems, sems,
):
    at = Place(n_z, n_tp)
    links = Links(send_sems, recv_sems)
    z, y, t, me = at.z, at.y, at.t, at.me
    top = n_z // 2
    n_b, rows, width = 2 * n_tp, mid.shape[0], mid.shape[1]
    depth = gu_src.shape[2]
    full_len = rot.shape[0]
    h = rows // 2
    n_q = rot.shape[1] // LANES - 2
    local = []

    def move(src, dst):
        copy = pltpu.make_async_copy(src, dst, sems.at[len(local)])
        copy.start()
        local.append(copy)
        return copy

    load_w3 = move(w3, w3_v)
    load_gu, load_hid = move(d_gu, gu_v), move(hidden, hid_v)
    load_o = move(w_o, o_v)
    load_x = move(x_here.at[pl.ds(pl.multiple_of(t * rows, rows), rows)], row_v.at[0])
    load_dy = move(dy_here.at[pl.ds(pl.multiple_of(t * rows, rows), rows)], row_v.at[1])
    greet(at.peers())

    def fetch_with(buf):
        def fetch(block):
            move(block, buf).wait()
            return buf

        return fetch

    f_gu = GradFlow(links, at, gu_src, gu_land, True, gu_out, gu_pass, fetch_with(fetch_gu))
    f_dn = GradFlow(links, at, dn_src, dn_land, True, dn_out, dn_pass, fetch_with(fetch_dn))
    f_gu.first()
    f_dn.first()

    def term(seq, lhs, lo, hi):
        def product(r, cols):
            return dot(lhs[seq, flip_all(me, r)], w3_v[cols, lo:hi], ((1,), (1,)))

        return product

    bufs_a = (to_core_a, held_a, landed_a, total_a, free_a)
    bufs_b = (to_core_b, held_b, landed_b, total_b, free_b)
    load_w3.wait()
    load_gu.wait()
    far = LayerSum(links, at, rows, bufs_a, term(1, gu_v, 0, 2 * units))
    own = LayerSum(links, at, rows, bufs_b, term(0, gu_v, 0, 2 * units))
    far.begin()
    far.middle()
    own.begin()

    def send_far(layer, i):
        sent = []
        for p, value in enumerate(layer.end()):
            far_v[i, pl.ds(p * h, h), :] = value.astype(BF16)
            sent.append(
                links.send(
                    half_rows(far_v.at[i], p, rows), half_rows(far_in.at[i], p, rows), at.zz(top),
                    kept=True,
                )
            )
        layer.release()
        return sent

    sent_far = send_far(far, 0)
    own.middle()
    heads_v = w3_v.at[:, : w_heads.shape[1]]
    load_heads = move(w_heads, heads_v)
    load_hid.wait()
    ffn_far = LayerSum(links, at, rows, bufs_a, term(1, hid_v, wide, wide + units), far)
    ffn_own = LayerSum(links, at, rows, bufs_b, term(0, hid_v, wide, wide + units), own)
    ffn_far.begin()

    def norm_back(inputs, gain, d_normed):
        root = lax.rsqrt(jnp.mean(inputs * inputs, axis=1, keepdims=True) + NORM_EPS)
        scaled = d_normed * gain
        return root * scaled - inputs * (root * root * root) * jnp.mean(
            scaled * inputs, axis=1, keepdims=True
        )

    load_x.wait()
    load_dy.wait()
    gather = LayerGather(links, at, d_proj, rows)
    for p, value in enumerate(own.end()):
        r = slice(p * h, (p + 1) * h)
        sent_far[p].wait_recv()
        value = value + far_in[0, r, :].astype(F32)
        value = row_v[1, r, :].astype(F32) + norm_back(mid[r, :], gains[1:2, :], value)
        d_mid[r, :] = value
        d_proj[me, r, :] = value.astype(BF16)
        gather.own(p)
    own.release()
    gather.far_first()
    ffn_own.begin()
    f_gu.spread()
    gather.far_second()
    ffn_far.middle()
    gather.last()

    load_o.wait()
    w_o_all = o_v[...].reshape(width, o_v.shape[3])

    def d_attn_rows(b, carry):
        r = pl.ds(pl.multiple_of(b * rows, rows), rows)
        d_attn[r, :] = dot(d_proj[b], w_o_all).astype(BF16)
        return carry

    lax.fori_loop(0, n_b, d_attn_rows, 0)

    group = 1
    while 2 * depth * group % LANES:
        group *= 2
    span = 2 * depth * group

    def groups():
        rels = sorted(range(0, n_z, group), key=lambda r: (-(r & 1), -r))
        return [flip_all(z, r) // group for r in rels]

    def span_of(owner):
        return pl.ds(pl.multiple_of(owner * span, span), span)

    o_src = o_v
    f_o = GradFlow(links, at, o_src, o_land, False, o_out, None)
    for owner in groups():
        lhs = jnp.concatenate([d_proj[b, :, span_of(owner)] for b in range(n_b)], axis=0)
        value = dot(lhs, attn[...], ((0,), (0,))).astype(BF16)
        o_src[pl.ds(owner * group, group)] = value.reshape(group, 2, depth, value.shape[1])
    f_o.first()
    gather.drain()
    load_norm = move(norm_attn, d_proj)
    f_dn.spread()
    ffn_own.middle()
    dk_sum[...] = jnp.zeros_like(dk_sum)
    dv_sum[...] = jnp.zeros_like(dv_sum)
    for i in range(full_len // q_block):
        attend_back_rows(
            scale, q_block, i, rot, d_attn, stats, cos, sin, seg_col, seg_row, sel, d_qkv, dk_sum, dv_sum
        )
        if i == 0:
            f_gu.cross()
            f_dn.cross()
            sent_ffn = send_far(ffn_far, 1)
    attend_back_keys(scale, n_q, cos, sin, d_qkv, dk_sum, dv_sum)

    load_heads.wait()

    def d_term(r, cols):
        value = d_qkv[pl.ds(pl.multiple_of(flip_all(me, r) * rows, rows), rows), :]
        return dot(value, w3_v[cols, : w_heads.shape[1]], ((1,), (1,)))

    in_cols = slice(w_heads.shape[1], w_heads.shape[1] + spread.shape[0])
    in_src = w3_v.reshape(n_z, 2, depth, w3_v.shape[1]).at[:, :, :, in_cols]
    f_in = GradFlow(links, at, in_src, in_land, False, in_out, None)
    packed = dot(d_qkv[...], spread[...], ((1,), (1,))).astype(BF16)
    load_norm.wait()
    for owner in groups():
        lhs = jnp.concatenate([d_proj[b, :, span_of(owner)] for b in range(n_b)], axis=0)
        w3_v[span_of(owner), in_cols] = dot(lhs, packed, ((0,), (0,))).astype(BF16)
    f_in.first()
    d_in = LayerSum(links, at, rows, bufs_a, d_term, ffn_far)
    d_in.begin()
    d_in.middle()
    f_o.spread()
    f_o.cross()
    out_g, in_g = TpGather(links, at, output), TpGather(links, at, input_grad)
    stay = []
    for p, value in enumerate(d_in.end()):
        r = slice(p * h, (p + 1) * h)
        value = d_mid[r, :] + norm_back(row_v[0, r, :].astype(F32), gains[0:1, :], value)
        row_v[1, r, :] = value.astype(BF16)
    in_g.own(row_v.at[1])
    stay.append(move(row_v.at[1], input_grad.at[t]))
    for copy in sent_far:
        copy.wait_send()
    for p, value in enumerate(ffn_own.end()):
        r = slice(p * h, (p + 1) * h)
        sent_ffn[p].wait_recv()
        value = value + far_in[1, r, :].astype(F32)
        far_v[0, r, :] = (mid[r, :] + value).astype(BF16)
    out_g.own(far_v.at[0])
    stay.append(move(far_v.at[0], output.at[t]))
    f_in.spread()
    f_in.cross()
    f_gu.cross_far()
    f_dn.cross_far()
    for flow in (f_gu, f_dn, f_o, f_in):
        stay.append(move(*flow.mine()))
    in_g.second()
    out_g.second()
    for flow in (in_g, out_g, f_gu, f_dn, f_o, f_in):
        flow.last()
    for copy in stay:
        copy.wait()
    for copy in sent_ffn:
        copy.wait_send()
    links.finish(d_in, ffn_own)


def back(n_z, n_tp, scale, units, wide, *args):
    x_here, w_heads, spread, mid, sel = args[0], args[8], args[20], args[10], args[19]
    d_gu, hidden, gu_src, dn_src, w3, w_o, rot = args[3], args[4], args[5], args[6], args[2], args[7], args[12]
    half_len, width = x_here.shape
    rows = mid.shape[0]
    full_len = 2 * half_len
    depth = gu_src.shape[2]
    heads, compact = w_heads.shape[1], spread.shape[0]
    q_cols = sel.shape[1]
    any_, vmem = pl.BlockSpec(memory_space=pl.ANY), pl.BlockSpec(memory_space=pltpu.VMEM)
    shape = jax.ShapeDtypeStruct
    n_swap, n_add = max(1, n_z - 2), n_z - 1
    n_sems = 120 + 8 * n_z
    return pl.pallas_call(
        lambda *refs: back_kernel(n_z, n_tp, scale, min(256, full_len), units, wide, *refs),
        out_shape=(
            shape((n_tp, rows, width), BF16),
            shape((n_tp, rows, width), BF16),
            shape((2, 2, depth, 2 * units), BF16),
            shape((2, 2, depth, units), BF16),
            shape((2, depth, q_cols), BF16),
            shape((2, depth, compact), BF16),
        ),
        in_specs=[any_] * 10 + [vmem] * 11,
        out_specs=(any_,) * 6,
        scratch_shapes=[
            pltpu.VMEM(w3.shape, BF16),
            pltpu.VMEM(d_gu.shape, BF16),
            pltpu.VMEM(hidden.shape, BF16),
            *sum_scratch(rows, width),
            *sum_scratch(rows, width),
            pltpu.VMEM((2, rows, width), BF16),
            pltpu.VMEM((2, rows, width), BF16),
            pltpu.VMEM((rows, width), F32),
            pltpu.VMEM((2, rows, width), BF16),
            pltpu.VMEM((2 * n_tp, rows, width), BF16),
            pltpu.VMEM((full_len, q_cols), BF16),
            pltpu.VMEM((full_len, heads), BF16),
            pltpu.VMEM((full_len, LANES), F32),
            pltpu.VMEM((full_len, LANES), F32),
            pltpu.VMEM(w_o.shape, BF16),
            pltpu.VMEM((n_swap, 2, depth, 2 * units), BF16),
            pltpu.VMEM((depth, 2 * units), BF16),
            pltpu.VMEM((n_swap, 2, depth, units), BF16),
            pltpu.VMEM((depth, units), BF16),
            pltpu.VMEM((depth, 2 * units), BF16),
            pltpu.VMEM((depth, units), BF16),
            pltpu.VMEM((n_add, 2, depth, q_cols), BF16),
            pltpu.VMEM((n_add, 2, depth, compact), BF16),
            pltpu.SemaphoreType.DMA((n_sems,)),
            pltpu.SemaphoreType.DMA((n_sems,)),
            pltpu.SemaphoreType.DMA((24 + 6 * n_z,)),
        ],
        compiler_params=pltpu.CompilerParams(
            collective_id=2, has_side_effects=True, vmem_limit_bytes=BACK_LIMIT
        ),
        name="back",
    )(*args)


def body(
    tokens,
    segments,
    attn_gain,
    q_weight,
    k_weight,
    v_weight,
    o_weight,
    ffn_gain,
    gate_weight,
    up_weight,
    down_weight,
    cotangent,
):
    n_z = lax.axis_size("fsdp")
    n_tp = lax.axis_size("tp")
    _, half_len, width = tokens.shape
    full_len = segments.shape[1]
    rows = half_len // n_tp
    units = gate_weight.shape[1] // 4
    scale = HEAD_DIM ** (-0.5)

    x_here = tokens.reshape(half_len, width)
    dy_here = cotangent.reshape(half_len, width)
    k_t, v_t, o_t, down_t = k_weight.T, v_weight.T, o_weight.T, down_weight.T
    (
        w_heads, w_o, w3, gains, norm_attn, dy_all, norm_all, attn, rot, stats, mid, cos, sin, spread, sel,
        seg_col,
    ) = front(
        n_z, n_tp, scale, x_here, dy_here,
        (q_weight, k_t, v_t, o_t, gate_weight, up_weight, down_t),
        jnp.stack([attn_gain, ffn_gain]), segments,
    )
    w3 = w3.reshape(width, -1)
    norm_all = norm_all.reshape(4 * n_tp, rows, width)
    dy_all = dy_all.reshape(4 * n_tp, rows, width)
    d_gu, hidden = act(norm_all, dy_all, w3, units)
    gu_src, dn_src = terms(norm_all, dy_all, d_gu, hidden, n_z)
    output, input_grad, gu_four, dn_four, o_two, in_two = back(
        n_z, n_tp, scale, units, wide_of(units),
        x_here, dy_here, w3, d_gu.reshape(2, 2 * n_tp, rows, 2 * units),
        hidden.reshape(2, 2 * n_tp, rows, units), gu_src, dn_src, w_o, w_heads,
        norm_attn.reshape(2 * n_tp, rows, width),
        mid, gains, rot, attn, stats, cos, sin, seg_col, segments, sel, spread,
    )
    q_grad, k_grad, v_grad, sums = finish_in(
        gu_four, in_two, q_weight, k_t, v_t, gate_weight, up_weight
    )
    here, others = sum_tp(sums[:, :2].T)
    gate_grad, up_grad, down_grad, o_grad, output, input_grad = finish(
        gu_four, dn_four, o_two, output, input_grad
    )
    gain_sums = sum(others, here)
    attn_gain_grad = gain_sums[0] / attn_gain.astype(F32)
    ffn_gain_grad = gain_sums[1] / ffn_gain.astype(F32)

    return (
        output.reshape(tokens.shape),
        input_grad.reshape(tokens.shape),
        attn_gain_grad,
        q_grad,
        k_grad.T,
        v_grad.T,
        o_grad.T,
        ffn_gain_grad,
        gate_grad,
        up_grad,
        down_grad.T,
    )


def solution(mesh):
    specs = dict(
        tok=P("fsdp", "ctx", None),
        gain=P(("fsdp", "ctx")),
        row=P(("fsdp", "ctx"), "tp"),
        col=P("tp", ("fsdp", "ctx")),
    )
    tok, gain, row, col = specs["tok"], specs["gain"], specs["row"], specs["col"]
    return jax.shard_map(
        body,
        mesh=mesh,
        in_specs=(tok, P("fsdp", None), gain, row, row, row, col, gain, row, row, col, tok),
        out_specs=(tok, tok, gain, row, row, row, col, gain, row, row, col),
        check_vma=False,
    )
```

```python
import math

import jax
import jax.numpy as jnp
from jax import lax
from jax.experimental import pallas as pl
from jax.experimental.pallas import tpu as pltpu
from jax.sharding import PartitionSpec as P

HEAD_DIM = 80
HALF = HEAD_DIM // 2
LANES = 128
NORM_EPS = 1e-05
ROPE_BASE = 10000.0
MASK_FILL = -1000000000.0
F32 = jnp.float32
BF16 = jnp.bfloat16


def pp(value, axis, mask):
    size = lax.axis_size(axis)
    return lax.ppermute(value, axis, [(i, i ^ mask) for i in range(size)])


def dot(a, b, dims=((1,), (0,))):
    return lax.dot_general(a, b, (dims, ((), ())), preferred_element_type=F32)


def in_order(bit, mine, other, axis=0):
    return jnp.where(
        bit == 0, jnp.stack([mine, other], axis), jnp.stack([other, mine], axis)
    )


def pick(blocks, index):
    return lax.dynamic_index_in_dim(blocks, index, 0, keepdims=False)


def attend_rows(scale, block, i, rot, seg_col, seg_row, sel, attn, stats):
    n_q = rot.shape[1] // LANES - 2
    rows = slice(i * block, (i + 1) * block)
    keys = (i + 1) * block
    q_pos = i * block + lax.broadcasted_iota(jnp.int32, (block, keys), 0)
    k_pos = lax.broadcasted_iota(jnp.int32, (block, keys), 1)
    allowed = (seg_col[rows, :] == seg_row[:, :keys]) & (k_pos <= q_pos)
    k = rot[:keys, n_q * LANES : (n_q + 1) * LANES]
    v = rot[:keys, (n_q + 1) * LANES :]
    outs, maxes, totals = [], [], []
    for h in range(n_q):
        s = dot(rot[rows, h * LANES : (h + 1) * LANES], k, ((1,), (1,))) * scale
        s = jnp.where(allowed, s, MASK_FILL)
        top = jnp.max(s, axis=1, keepdims=True)
        e = jnp.exp(s - top)
        total = jnp.sum(e, axis=1, keepdims=True)
        outs.append(dot((e * (1.0 / total)).astype(BF16), v).astype(BF16))
        maxes.append(top)
        totals.append(total)
    attn[rows, :] = dot(jnp.concatenate(outs, axis=1), sel[...]).astype(BF16)
    stats[rows, :] = jnp.concatenate(maxes + totals, axis=1)


def turn_back(u, cos, sin, rows):
    return (u * cos[rows, :] - pltpu.roll(u, 64, 1) * sin[rows, :]).astype(BF16)


def attend_back_rows(
    scale, block, i, rot, d_attn, stats, cos, sin, seg_col, seg_row, sel, d_qkv, dk_sum, dv_sum
):
    n_q = rot.shape[1] // LANES - 2
    rows = slice(i * block, (i + 1) * block)
    keys = (i + 1) * block
    q_pos = i * block + lax.broadcasted_iota(jnp.int32, (block, keys), 0)
    k_pos = lax.broadcasted_iota(jnp.int32, (block, keys), 1)
    allowed = (seg_col[rows, :] == seg_row[:, :keys]) & (k_pos <= q_pos)
    k = rot[:keys, n_q * LANES : (n_q + 1) * LANES]
    v = rot[:keys, (n_q + 1) * LANES :]
    d_out = dot(d_attn[rows, :], sel[...], ((1,), (1,))).astype(BF16)
    stat = stats[rows, :]
    for h in range(n_q):
        q = rot[rows, h * LANES : (h + 1) * LANES]
        d_h = d_out[:, h * LANES : (h + 1) * LANES]
        s = dot(q, k, ((1,), (1,))) * scale
        s = jnp.where(allowed, s, MASK_FILL)
        p = jnp.exp(s - stat[:, h : h + 1]) * (1.0 / stat[:, n_q + h : n_q + h + 1])
        dv_sum[:keys, :] += dot(p.astype(BF16), d_h, ((0,), (0,)))
        d_p = dot(d_h, v, ((1,), (1,)))
        d_s = (p * (d_p - jnp.sum(p * d_p, axis=1, keepdims=True))).astype(BF16)
        d_q = (dot(d_s, k) * scale).astype(BF16).astype(F32)
        d_qkv[rows, h * LANES : (h + 1) * LANES] = turn_back(d_q, cos, sin, rows)
        dk_sum[:keys, :] += dot(d_s, q, ((0,), (0,)))


def attend_back_keys(scale, n_q, cos, sin, d_qkv, dk_sum, dv_sum):
    d_k = (dk_sum[...] * scale).astype(BF16).astype(F32)
    d_qkv[:, n_q * LANES : (n_q + 1) * LANES] = turn_back(d_k, cos, sin, slice(None))
    d_qkv[:, (n_q + 1) * LANES :] = dv_sum[...].astype(BF16)


VMEM_LIMIT = 56 * 1024 * 1024
BACK_LIMIT = 62 * 1024 * 1024


def sum_tp(value):
    others = [pp(value, "tp", mask) for mask in range(1, lax.axis_size("tp"))]
    return value, others


def below(top):
    masks = []
    while top > 1:
        top //= 2
        masks.append(top)
    return masks


def flip(index, mask):
    return index + mask * (1 - 2 * ((index // mask) % 2))


def flip_all(index, bits):
    mask = 1
    while mask <= bits:
        if bits & mask:
            index = flip(index, mask)
        mask *= 2
    return index


class Links:
    def __init__(self, send_sems, recv_sems):
        self.sems = (send_sems, recv_sems)
        self.copies = []
        self.count = 0

    def send(self, src, dst, peer, kept=False):
        k = self.count
        self.count += 1
        copy = pltpu.make_async_remote_copy(
            src_ref=src,
            dst_ref=dst,
            send_sem=self.sems[0].at[k],
            recv_sem=self.sems[1].at[k],
            device_id=peer,
            device_id_type=pl.DeviceIdType.MESH,
        )
        copy.start()
        if not kept:
            self.copies.append(copy)
        return copy

    def finish(self, *sums):
        for copy in self.copies:
            copy.wait_send()
        for layer in sums:
            layer.drain()


def greet(peers):
    barrier = pltpu.get_barrier_semaphore()
    for peer in peers:
        pl.semaphore_signal(barrier, inc=1, device_id=peer, device_id_type=pl.DeviceIdType.MESH)
    pl.semaphore_wait(barrier, len(peers))


class Place:
    def __init__(self, n_z, n_tp):
        self.n_z, self.n_tp = n_z, n_tp
        self.z, self.y, self.t = (lax.axis_index(a) for a in ("fsdp", "ctx", "tp"))
        self.me = self.y * n_tp + self.t
        self.core = {"tp": flip(self.t, 1)}
        self.x = {"tp": flip(self.t, 2)}
        self.yy = {"ctx": 1 - self.y}
        self.masks = below(n_z)
        self.zb = self.z // (n_z // 2)

    def zz(self, mask):
        return {"fsdp": flip(self.z, mask)}

    def peers(self):
        return [self.core, self.x, self.yy] + [self.zz(m) for m in self.masks]


class WeightFlow:
    def __init__(self, links, at, out, cross, first, second):
        self.links, self.at, self.out = links, at, out
        self.first, self.second = first, second
        self.got = {}
        self.y_copy = links.send(cross, second(None), at.yy)

    def own(self, masks=None):
        at = self.at
        for m in at.masks if masks is None else masks:
            dst = self.out.at[at.z, at.y]
            self.got[m, 0] = self.links.send(self.first(m), dst, at.zz(m))

    def arrived(self):
        self.y_copy.wait_recv()

    def crossed(self, masks=None):
        at = self.at
        for m in at.masks if masks is None else masks:
            dst = self.out.at[at.z, 1 - at.y]
            self.got[m, 1] = self.links.send(self.second(m), dst, at.zz(m))

    def take(self, rel, part):
        at = self.at
        self.got[rel, part].wait_recv()
        low = rel & -rel
        row = at.y if part == 0 else 1 - at.y
        block = self.out.at[flip_all(at.z, rel), row]
        for m in at.masks:
            if m < low:
                self.got[rel ^ m, part] = self.links.send(block, block, at.zz(m))

    def order(self):
        rels = [r for r in range(1, self.at.n_z)]
        return sorted(rels, key=lambda r: (bin(r).count("1"), -(r & -r), r))


def half_rows(ref, part, rows):
    return ref.at[pl.ds(part * (rows // 2), rows // 2)]


class LayerGather:
    def __init__(self, links, at, out, rows):
        self.links, self.at, self.out, self.rows = links, at, out, rows
        self.cores = []
        self.sent = []

    def half(self, index, part):
        return half_rows(self.out.at[index], part, self.rows)

    def send(self, src, dst, peer):
        self.sent.append(self.links.send(src, dst, peer, kept=True))
        return self.sent[-1]

    def pass_on(self, index, part, peer):
        block = self.half(index, part)
        return self.send(block, block, peer)

    def own(self, part, src=None):
        at, me = self.at, self.at.me
        a = self.half(me, part)
        src = a if src is None else src
        send = lambda peer: self.send(src, a, peer)
        if part == 0:
            self.xa, self.ya = send(at.x), send(at.yy)
        else:
            self.yb, self.xb = send(at.yy), send(at.x)
        self.cores.append(send(at.core))

    def to_core(self, index, part):
        self.cores.append(self.pass_on(index, part, self.at.core))

    def far_first(self):
        at = self.at
        self.x_of, self.y_of = flip(at.me, 2), flip(at.me, at.n_tp)
        self.diag = flip(self.x_of, at.n_tp)
        self.xa.wait_recv()
        self.y_fwd = self.pass_on(self.x_of, 0, at.yy)
        self.to_core(self.x_of, 0)
        self.yb.wait_recv()
        self.x_fwd = self.pass_on(self.y_of, 1, at.x)
        self.to_core(self.y_of, 1)

    def far_second(self):
        self.ya.wait_recv()
        self.to_core(self.y_of, 0)
        self.xb.wait_recv()
        self.to_core(self.x_of, 1)
        self.y_fwd.wait_recv()
        self.to_core(self.diag, 0)
        self.x_fwd.wait_recv()
        self.to_core(self.diag, 1)

    def last(self):
        for copy in self.cores:
            copy.wait_recv()

    def drain(self):
        for copy in self.sent:
            copy.wait_send()


class LayerSum:
    def __init__(self, links, at, rows, bufs, product, after=None):
        self.links, self.at, self.rows = links, at, rows
        self.to_core, self.held, self.landed, self.total, self.free = bufs
        self.product = product
        self.after = after

    def peers(self):
        return (self.at.core, self.at.x, self.at.yy)

    def tiles(self, some):
        width = self.total.shape[1]
        tile = 512 if width % 512 == 0 else width

        def body(c, carry):
            some(pl.ds(pl.multiple_of(c * tile, tile), tile))
            return carry

        lax.fori_loop(0, width // tile, body, 0)

    def drain(self):
        for copy in self.sent:
            copy.wait_send()
        self.sent = []

    def release(self):
        self.drain()
        for i, peer in enumerate(self.peers()):
            pl.semaphore_signal(
                self.free.at[i], inc=1, device_id=peer, device_id_type=pl.DeviceIdType.MESH
            )

    def begin(self):
        self.core = {}
        if self.after is not None:
            self.after.drain()
            for i in range(3):
                pl.semaphore_wait(self.free.at[i], 1)
        sent = []
        for i, k in enumerate((3, 1, 2, 0)):
            if i >= 2:
                sent[i - 2].wait_send()


            def some(cols, i=i, k=k):
                self.to_core[i % 2, :, cols] = self.product(2 * k + 1, cols).astype(BF16)

            self.tiles(some)
            self.core[k] = self.links.send(
                self.to_core.at[i % 2], self.held.at[k], self.at.core, kept=True
            )
            sent.append(self.core[k])
        self.sent = sent[2:]

    def middle(self):
        at, rows, h = self.at, self.rows, self.rows // 2
        held, landed = self.held, self.landed
        a, b = slice(0, h), slice(h, rows)

        def level(k):
            self.core[k].wait_recv()

            def some(cols):
                value = self.product(2 * k, cols) + held[k, :, cols].astype(F32)
                if k == 0:
                    self.total[:, cols] = value
                else:
                    held[k, :, cols] = value.astype(BF16)

            self.tiles(some)

        def send(k, i, peer):
            copy = self.links.send(held.at[k, pl.ds((i % 2) * h, h)], landed.at[i], peer, kept=True)
            self.sent.append(copy)
            return copy

        level(3)
        self.x1 = send(3, 0, at.x)
        self.y1 = send(3, 1, at.yy)
        level(1)
        x2 = send(1, 2, at.x)
        level(2)
        y2 = send(2, 3, at.yy)
        level(0)
        self.send, self.tail = send, (x2, y2)

    def second(self):
        at, h = self.at, self.rows // 2
        held, landed = self.held, self.landed
        a, b = slice(0, h), slice(h, self.rows)
        self.x1.wait_recv()
        held[2, a] = (held[2, a].astype(F32) + landed[0].astype(F32)).astype(BF16)
        y3 = self.send(2, 4, at.yy)
        self.y1.wait_recv()
        held[1, b] = (held[1, b].astype(F32) + landed[1].astype(F32)).astype(BF16)
        x3 = self.send(1, 5, at.x)
        self.tail += (y3, x3)

    def end(self):
        h = self.rows // 2
        landed, total = self.landed, self.total
        for copy in self.tail:
            copy.wait_recv()
        top = total[:h, :] + landed[2].astype(F32) + landed[4].astype(F32)
        low = total[h:, :] + landed[3].astype(F32) + landed[5].astype(F32)
        return top, low


def sum_scratch(rows, width):
    return [
        pltpu.VMEM((2, rows, width), BF16),
        pltpu.VMEM((4, rows, width), BF16),
        pltpu.VMEM((6, rows // 2, width), BF16),
        pltpu.VMEM((rows, width), F32),
        pltpu.SemaphoreType.REGULAR((3,)),
    ]


def eye(n):
    shape = (n, n)
    same = lax.broadcasted_iota(jnp.int32, shape, 0) == lax.broadcasted_iota(jnp.int32, shape, 1)
    return same.astype(F32).astype(BF16)


def column(row):
    n = row.shape[1]
    same = lax.broadcasted_iota(jnp.int32, (n, n), 0) == lax.broadcasted_iota(jnp.int32, (n, n), 1)
    return jnp.sum(jnp.where(same, row.astype(F32), 0.0), axis=1, keepdims=True)


def head_spread(n_q, compact):
    shape = (compact, (n_q + 2) * LANES)
    col, lane = (lax.broadcasted_iota(jnp.int32, shape, d) for d in (0, 1))
    at, head = col % HEAD_DIM, col // HEAD_DIM
    spot = head * LANES + at + jnp.where((at >= HALF) & (head < n_q + 1), 64 - HALF, 0)
    return ((spot == lane) & (head < n_q + 2)).astype(F32).astype(BF16)


def head_select(n_q):
    shape = (n_q * LANES, n_q * HEAD_DIM)
    lane, col = (lax.broadcasted_iota(jnp.int32, shape, d) for d in (0, 1))
    return ((col // HEAD_DIM) * LANES + col % HEAD_DIM == lane).astype(F32).astype(BF16)


def front_kernel(
    n_z, n_tp, scale, q_block,
    x_here, dy_here, q_w, k_t, v_t, o_t, gate_w, up_w, down_t, gain_rows, seg_row,
    w_heads, w_o, w3, gains, norm_attn, dy_all, norm_all, attn, rot, stats, mid, cos, sin, spread, sel, seg_col,
    w_in, x_all, qkv, to_core, held, landed, total, free, in_cross, o_cross, w3_cross,
    heads_v, norm_v, own_v, root_v, o_v, in_send, o_send, w3_send, send_sems, recv_sems, sems,
):
    at = Place(n_z, n_tp)
    links = Links(send_sems, recv_sems)
    z, y, t, me = at.z, at.y, at.t, at.me
    zb = z // (n_z // 2)
    n_b, rows, width = 2 * n_tp, x_all.shape[0] // (2 * n_tp), x_all.shape[1]
    depth = in_send.shape[1]
    full_len = x_all.shape[0]
    local = []

    def move(src, dst):
        copy = pltpu.make_async_copy(src, dst, sems.at[len(local)])
        copy.start()
        local.append(copy)
        return copy

    def block_of(ref, index):
        return ref.at[pl.ds(pl.multiple_of(index * rows, rows), rows)]

    q_cols, kv_cols = q_w.shape[1] // 2, k_t.shape[0] // 2
    units = gate_w.shape[1] // 4
    wide = w3_send.shape[3] - units
    extra = jnp.concatenate(
        [column(gain_rows[i : i + 1, :]) for i in range(2)]
        + [jnp.zeros((depth, in_send.shape[2] - q_cols - 2 * kv_cols - 2), F32)],
        axis=1,
    ).astype(BF16)
    for j in range(2):
        kv = slice(j * kv_cols, (j + 1) * kv_cols)
        turned = [dot(w[kv, :], eye(kv_cols), ((0,), (0,))).astype(BF16) for w in (k_t, v_t)]
        in_send[j] = jnp.concatenate(
            [q_w[:, j * q_cols : (j + 1) * q_cols], *turned, extra], axis=1
        )
    greet(at.peers())
    f_in = WeightFlow(
        links, at, w_in, in_send.at[1 - y], lambda m: in_send.at[y], lambda m: in_cross
    )
    f_in.own()
    own_in = move(in_send.at[y], w_in.at[z, y])
    x_mine = block_of(x_here, t)
    tok_y = links.send(x_mine, block_of(x_all, me), at.yy)
    x_own = move(x_here, x_all.at[pl.ds(pl.multiple_of(y * (full_len // 2), full_len // 2), full_len // 2)])
    dy_mine = block_of(dy_here, t)
    dy_in = move(dy_here, norm_v.at[pl.ds(0, full_len // 2)])

    for j in range(2):
        o_send[j] = o_t[:, j * q_cols : (j + 1) * q_cols]
    for j in range(4):
        cols = slice(j * units, (j + 1) * units)
        w3_send[j % 2, j // 2, :, : 2 * units] = jnp.concatenate(
            [gate_w[:, cols], up_w[:, cols]], axis=1
        )
        w3_send[j % 2, j // 2, :, wide:] = down_t[:, cols]
    f_in.arrived()
    f_in.crossed()
    cross_in = move(in_cross, w_in.at[z, 1 - y])
    f_o = WeightFlow(
        links, at, w_o, o_send.at[1 - y], lambda m: o_send.at[y], lambda m: o_cross
    )
    top = n_z // 2
    tok_y.wait_recv()
    f_3 = WeightFlow(
        links, at, w3, w3_send.at[1 - y],
        lambda m: w3_send.at[y, 1 - zb if m == top else zb],
        lambda m: w3_cross if m is None else w3_cross.at[1 - zb if m == top else zb],
    )
    dy_y = links.send(dy_mine, dy_all.at[0, me], at.yy)
    dy_in.wait()
    dy_own = move(
        norm_v.at[pl.ds(0, full_len // 2)].reshape(n_tp, rows, width),
        dy_all.at[0, pl.ds(y * n_tp, n_tp)],
    )
    y_of, x_of = flip(me, n_tp), flip(me, 2)
    y_block = block_of(x_all, y_of)
    tok_x = links.send(y_block, y_block, at.x)
    tok_c = [links.send(y_block, y_block, at.core)]
    ins = [(rel, p) for rel in f_in.order() for p in (0, 1)]
    for rel, p in ins:
        if rel == top:
            f_in.take(rel, p)
    lane = lax.broadcasted_iota(jnp.int32, (1, LANES), 1)
    within = lane % 64
    frequency = jnp.where(
        within < HALF, jnp.exp(within.astype(F32) * (-2.0 * math.log(ROPE_BASE) / HEAD_DIM)), 0.0
    )
    sign = jnp.where(lane < 64, -1.0, 1.0)
    n_q = rot.shape[1] // LANES - 2
    spread[...] = head_spread(n_q, w_in.shape[3])
    sel[...] = head_select(n_q)
    step = min(256, full_len)

    def tables(c, carry):
        at_rows = pl.ds(pl.multiple_of(c * step, step), step)
        mine = jnp.concatenate(
            [
                column(seg_row[:, pl.ds(pl.multiple_of(c * step + i, LANES), LANES)])
                for i in range(0, step, LANES)
            ],
            axis=0,
        ).astype(jnp.int32)
        seg_col[at_rows, :] = mine
        before = jnp.where(seg_row[...] < mine, 1.0, 0.0)
        start = jnp.sum(before, axis=1, keepdims=True)
        position = (c * step + lax.broadcasted_iota(jnp.int32, (step, 1), 0)).astype(F32)
        angles = (position - start) * frequency
        cos[at_rows, :] = jnp.cos(angles)
        sin[at_rows, :] = jnp.sin(angles) * sign
        return carry

    lax.fori_loop(0, full_len // step, tables, 0)
    tok_x.wait_recv()
    diag = block_of(x_all, flip(y_of, 2))
    tok_c.append(links.send(diag, diag, at.core))
    x_own.wait()

    for copy in tok_c:
        copy.wait_recv()

    def find_root(c, carry):
        at_rows = pl.ds(pl.multiple_of(c * step, step), step)
        value = x_all[at_rows, :].astype(F32)
        root_v[at_rows, :] = lax.rsqrt(jnp.mean(value * value, axis=1, keepdims=True) + NORM_EPS)
        return carry

    lax.fori_loop(0, full_len // step, find_root, 0)
    own_in.wait()
    cross_in.wait()
    dy_own.wait()

    pick_gain = (
        lax.broadcasted_iota(jnp.int32, (8, w_in.shape[3]), 1)
        == sel.shape[1] // HEAD_DIM * HEAD_DIM + 2 * HEAD_DIM + lax.broadcasted_iota(jnp.int32, (8, w_in.shape[3]), 0)
    ).astype(F32).astype(BF16)

    group = 1
    while 2 * depth * group % LANES:
        group *= 2
    span = 2 * depth * group

    def project(rel, first):
        owner = flip_all(z, rel) // group
        cols = pl.ds(pl.multiple_of(owner * span, span), span)
        weights = w_in[pl.ds(owner * group, group)].reshape(span, w_in.shape[3])
        gain = dot(pick_gain, weights, ((1,), (1,)))
        gains[:, cols] = gain
        heads = dot(weights, spread[...]).astype(BF16)
        heads_v[cols, :] = heads

        def some_rows(c, carry):
            at_rows = pl.ds(pl.multiple_of(c * step, step), step)
            value = (x_all[at_rows, cols].astype(F32) * root_v[at_rows, :] * gain[0:1, :]).astype(BF16)
            norm_v[at_rows, cols] = value
            term = dot(value, heads)
            qkv[at_rows, :] = term if first else qkv[at_rows, :] + term
            return carry

        lax.fori_loop(0, full_len // step, some_rows, 0)

    f_o.own()
    f_o.arrived()
    f_o.crossed()
    if group == 1:
        project(0, True)
    rest = [rel for rel in f_in.order() if rel != top]
    for rel in [top] + rest:
        if rel != top:
            for p in (0, 1):
                f_in.take(rel, p)
        if group == 1:
            project(rel, False)
    if group > 1:
        for rel in range(0, n_z, group):
            project(rel, rel == 0)
    heads_out = move(heads_v, w_heads)
    norm_out = move(norm_v, norm_attn)
    own_o = [move(o_send.at[y], w_o.at[z, y]), move(o_cross, w_o.at[z, 1 - y])]
    dy_y.wait_recv()
    dy_x = links.send(dy_all.at[0, y_of], dy_all.at[0, y_of], at.x)
    dy_c = [links.send(dy_all.at[0, y_of], dy_all.at[0, y_of], at.core)]
    lower = at.masks[1:]
    dy_z = [
        links.send(half_rows(dy_mine, p, rows), half_rows(dy_all.at[1, me], p, rows), at.zz(top))
        for p in (0, 1)
    ]
    f_3.own([top])
    for p in (0, 1):
        f_o.take(top, p)
    f_3.own(lower)

    def turn(c, carry):
        r = pl.ds(pl.multiple_of(c * step, step), step)
        for h in range(n_q + 1):
            u = qkv[r, h * LANES : (h + 1) * LANES]
            rot[r, h * LANES : (h + 1) * LANES] = (
                u * cos[r, :] + pltpu.roll(u, 64, 1) * sin[r, :]
            ).astype(BF16)
        rot[r, (n_q + 1) * LANES :] = qkv[r, (n_q + 1) * LANES :].astype(BF16)
        return carry

    lax.fori_loop(0, full_len // step, turn, 0)
    dy_far = LayerGather(links, at, dy_all.at[1], rows)
    for i in range(full_len // q_block):
        attend_rows(scale, q_block, i, rot, seg_col, seg_row, sel, attn, stats)
        if i == 0:
            dy_x.wait_recv()
            d_of = flip(y_of, 2)
            dy_c.append(links.send(dy_all.at[0, d_of], dy_all.at[0, d_of], at.core))
        if i == 2:
            f_3.arrived()
            f_3.crossed()
            own_3 = [move(w3_send.at[y, zb], w3.at[z, y]), move(w3_cross.at[zb], w3.at[z, 1 - y])]
    for rel in f_o.order():
        for p in (0, 1):
            if rel != top:
                f_o.take(rel, p)
    for copy in own_o:
        copy.wait()
    load_o = move(w_o.reshape(width, o_v.shape[1]), o_v)
    load_o.wait()

    def product(r, cols):
        lhs = attn[pl.ds(pl.multiple_of(flip_all(me, r) * rows, rows), rows), :]
        return dot(lhs, o_v[cols, :], ((1,), (1,)))

    layer = LayerSum(links, at, rows, (to_core, held, landed, total, free), product)
    layer.begin()
    layer.middle()
    layer.second()
    norm_own = LayerGather(links, at, norm_all.at[0], rows)
    norm_far = LayerGather(links, at, norm_all.at[1], rows)
    far = []
    h = rows // 2
    load_x = move(x_mine, own_v)
    load_x.wait()
    for p, value in enumerate(layer.end()):
        r = slice(p * h, (p + 1) * h)
        value = value + own_v[r, :].astype(F32)
        mid[r, :] = value
        root = lax.rsqrt(jnp.mean(value * value, axis=1, keepdims=True) + NORM_EPS)
        own_v[r, :] = (value * root * gains[1:2, :]).astype(BF16)
        src = own_v.at[pl.ds(p * h, h)]
        far.append(links.send(src, half_rows(norm_all.at[1, me], p, rows), at.zz(top)))
        norm_own.own(p, src)
    keep = move(own_v, norm_all.at[0, me])
    f_3.take(top, 0)
    norm_own.far_first()
    for p in (0, 1):
        dy_z[p].wait_recv()
        dy_far.own(p)
    norm_own.far_second()
    dy_far.far_first()
    for p in (0, 1):
        far[p].wait_recv()
        norm_far.own(p)
    dy_far.far_second()
    f_3.take(top, 1)
    norm_far.far_first()
    norm_far.far_second()
    for rel in f_3.order():
        for p in (0, 1):
            if rel != top:
                f_3.take(rel, p)
    for gather in (norm_own, dy_far, norm_far):
        gather.last()
        gather.drain()
    for copy in dy_c:
        copy.wait_recv()
    for copy in [heads_out, norm_out, keep] + own_3:
        copy.wait()
    links.finish(layer)


def front(n_z, n_tp, scale, x_here, dy_here, weights, gain_rows, seg_row):
    q_w, k_t, _, _, gate_w, _, _ = weights
    half_len, width = x_here.shape
    full_len = 2 * half_len
    rows = half_len // n_tp
    depth, q_cols = q_w.shape[0], q_w.shape[1] // 2
    n_q = q_cols // HEAD_DIM
    heads = (n_q + 2) * LANES
    compact = q_cols + k_t.shape[0] + 32
    units = gate_w.shape[1] // 4
    w3_cols = wide_of(units) + units
    any_, vmem = pl.BlockSpec(memory_space=pl.ANY), pl.BlockSpec(memory_space=pltpu.VMEM)
    n_sems = 80 + 6 * n_z + 32
    shape = jax.ShapeDtypeStruct
    return pl.pallas_call(
        lambda *refs: front_kernel(n_z, n_tp, scale, min(256, full_len), *refs),
        out_shape=(
            shape((width, heads), BF16),
            shape((n_z, 2, depth, q_cols), BF16),
            shape((n_z, 2, depth, w3_cols), BF16),
            shape((8, width), F32),
            shape((full_len, width), BF16),
            shape((2, 2 * n_tp, rows, width), BF16),
            shape((2, 2 * n_tp, rows, width), BF16),
            shape((full_len, q_cols), BF16),
            shape((full_len, heads), BF16),
            shape((full_len, 2 * n_q), F32),
            shape((rows, width), F32),
            shape((full_len, LANES), F32),
            shape((full_len, LANES), F32),
            shape((compact, heads), BF16),
            shape((n_q * LANES, q_cols), BF16),
            shape((full_len, 1), jnp.int32),
        ),
        in_specs=[any_] * 2 + [vmem] * 9,
        out_specs=(any_, any_, any_, vmem, any_, any_, any_) + (vmem,) * 9,
        scratch_shapes=[
            pltpu.VMEM((n_z, 2, depth, compact), BF16),
            pltpu.VMEM((full_len, width), BF16),
            pltpu.VMEM((full_len, heads), F32),
            *sum_scratch(rows, width),
            pltpu.VMEM((depth, compact), BF16),
            pltpu.VMEM((depth, q_cols), BF16),
            pltpu.VMEM((2, depth, w3_cols), BF16),
            pltpu.VMEM((width, heads), BF16),
            pltpu.VMEM((full_len, width), BF16),
            pltpu.VMEM((rows, width), BF16),
            pltpu.VMEM((full_len, 1), F32),
            pltpu.VMEM((width, q_cols), BF16),
            pltpu.VMEM((2, depth, compact), BF16),
            pltpu.VMEM((2, depth, q_cols), BF16),
            pltpu.VMEM((2, 2, depth, w3_cols), BF16),
            pltpu.SemaphoreType.DMA((n_sems,)),
            pltpu.SemaphoreType.DMA((n_sems,)),
            pltpu.SemaphoreType.DMA((16,)),
        ],
        compiler_params=pltpu.CompilerParams(
            collective_id=1, has_side_effects=True, vmem_limit_bytes=VMEM_LIMIT
        ),
        name="front",
    )(x_here, dy_here, *weights, gain_rows, seg_row)


def wide_of(units):
    return -(-2 * units // LANES) * LANES


def act_kernel(norm, dy, w3, d_gu, hidden):
    units = hidden.shape[2]
    n = norm.shape[0] * norm.shape[1]
    wide = w3.shape[1] - units
    gate_up = dot(norm[...].reshape(n, norm.shape[2]), w3[:, : 2 * units])
    d_hidden = dot(dy[...].reshape(n, dy.shape[2]), w3[:, wide:])
    gate, up = gate_up[:, :units], gate_up[:, units:]
    sig = 1.0 / (1.0 + jnp.exp(-gate))
    silu = gate * sig
    hidden[...] = (silu * up).astype(BF16).reshape(hidden.shape)
    d_up = (d_hidden * silu).astype(BF16)
    d_gate = (d_hidden * up * sig * (1.0 + gate * (1.0 - sig))).astype(BF16)
    d_gu[...] = jnp.concatenate([d_gate, d_up], axis=1).reshape(d_gu.shape)


def act(norm, dy, w3, units):
    blocks, rows, width = norm.shape
    per = max(1, 512 // rows)
    one = lambda cols: pl.BlockSpec((per, rows, cols), lambda i: (i, 0, 0))
    return pl.pallas_call(
        act_kernel,
        grid=(blocks // per,),
        out_shape=(
            jax.ShapeDtypeStruct((blocks, rows, 2 * units), BF16),
            jax.ShapeDtypeStruct((blocks, rows, units), BF16),
        ),
        in_specs=[one(width), one(width), pl.BlockSpec(w3.shape, lambda i: (0, 0))],
        out_specs=(one(2 * units), one(units)),
        compiler_params=pltpu.CompilerParams(vmem_limit_bytes=VMEM_LIMIT),
        name="act",
    )(norm, dy, w3)


def terms_kernel(norm, dy, d_gu, hidden, gu, dn):
    def term(lhs, rhs, out):
        n = lhs.shape[0] * lhs.shape[1]
        value = dot(lhs[...].reshape(n, lhs.shape[2]), rhs[...].reshape(n, rhs.shape[2]), ((0,), (0,)))
        out[...] = value.astype(BF16).reshape(out.shape)

    term(norm, d_gu, gu)
    term(dy, hidden, dn)


def terms(norm, dy, d_gu, hidden, n_z):
    blocks, rows, width = norm.shape
    depth, units = width // n_z // 2, hidden.shape[2]
    group = 1
    while 2 * depth * group % LANES:
        group *= 2
    cols = pl.BlockSpec((blocks, rows, 2 * depth * group), lambda i: (0, 0, i))
    whole = lambda a: pl.BlockSpec(a.shape, lambda i: (0, 0, 0))
    out = lambda c: pl.BlockSpec((group, 2, depth, c), lambda i: (i, 0, 0, 0))
    return pl.pallas_call(
        terms_kernel,
        grid=(n_z // group,),
        out_shape=(
            jax.ShapeDtypeStruct((n_z, 2, depth, 2 * units), BF16),
            jax.ShapeDtypeStruct((n_z, 2, depth, units), BF16),
        ),
        in_specs=[cols, cols, whole(d_gu), whole(hidden)],
        out_specs=(out(2 * units), out(units)),
        compiler_params=pltpu.CompilerParams(vmem_limit_bytes=VMEM_LIMIT),
        name="terms",
    )(norm, dy, d_gu, hidden)


def finish_in_kernel(gu, ins, q_w, k_t, v_t, gate_w, up_w, q_grad, k_grad, v_grad, sums):
    depth = q_w.shape[0]
    units, q_cols, kv_cols = gu.shape[3] // 2, q_w.shape[1] // 2, k_t.shape[0] // 2
    one = eye(depth)
    q_grad[...] = jnp.concatenate([ins[j, :, :q_cols].astype(F32) for j in range(2)], axis=1)
    first = jnp.sum(q_w[...].astype(F32) * q_grad[...], axis=1, keepdims=True)
    lo = q_cols
    for w, grad in ((k_t, k_grad), (v_t, v_grad)):
        for j in range(2):
            grad[j * kv_cols : (j + 1) * kv_cols, :] = dot(
                ins[j, :, lo : lo + kv_cols], one, ((0,), (0,))
            )
        lo += kv_cols
        first += column(jnp.sum(w[...].astype(F32) * grad[...], axis=0, keepdims=True))
    second = jnp.zeros((depth, 1), F32)
    for j in range(4):
        cols = slice(j * units, (j + 1) * units)
        weights = jnp.concatenate([gate_w[:, cols], up_w[:, cols]], axis=1).astype(F32)
        second += jnp.sum(weights * gu[j // 2, j % 2].astype(F32), axis=1, keepdims=True)
    lane = lax.broadcasted_iota(jnp.int32, sums.shape, 1)
    sums[...] = jnp.where(lane == 0, first, second)


def finish_in(gu, ins, q_w, k_t, v_t, gate_w, up_w):
    shape = lambda dims: jax.ShapeDtypeStruct(dims, F32)
    return pl.pallas_call(
        finish_in_kernel,
        out_shape=(
            shape(q_w.shape), shape(k_t.shape), shape(v_t.shape), shape((q_w.shape[0], LANES)),
        ),
        compiler_params=pltpu.CompilerParams(vmem_limit_bytes=VMEM_LIMIT),
        name="finish_in",
    )(gu, ins, q_w, k_t, v_t, gate_w, up_w)


def finish_kernel(gu, dn, o, rows_a, rows_b, gate_grad, up_grad, down_grad, o_grad, out_a, out_b):
    out_a[...] = rows_a[...]
    out_b[...] = rows_b[...]
    units = dn.shape[3]
    for grad, part in ((gate_grad, slice(0, units)), (up_grad, slice(units, 2 * units))):
        grad[...] = jnp.concatenate(
            [gu[j // 2, j % 2, :, part].astype(F32) for j in range(4)], axis=1
        )
    down_grad[...] = jnp.concatenate([dn[j // 2, j % 2].astype(F32) for j in range(4)], axis=1)
    o_grad[...] = jnp.concatenate([o[j].astype(F32) for j in range(2)], axis=1)


def finish(gu, dn, o, rows_a, rows_b):
    depth, units, q_cols = dn.shape[2], dn.shape[3], o.shape[2]
    shape = lambda cols: jax.ShapeDtypeStruct((depth, cols), F32)
    like = lambda a: jax.ShapeDtypeStruct(a.shape, a.dtype)
    return pl.pallas_call(
        finish_kernel,
        out_shape=(
            shape(4 * units), shape(4 * units), shape(4 * units), shape(2 * q_cols),
            like(rows_a), like(rows_b),
        ),
        compiler_params=pltpu.CompilerParams(vmem_limit_bytes=VMEM_LIMIT),
        cost_estimate=pl.CostEstimate(flops=0, bytes_accessed=20 * 2**20, transcendentals=0),
        name="finish",
    )(gu, dn, o, rows_a, rows_b)


class TpGather:
    def __init__(self, links, at, out):
        self.links, self.at, self.out = links, at, out

    def own(self, src):
        at = self.at
        dst = self.out.at[at.t]
        self.x = self.links.send(src, dst, at.x)
        self.cores = [self.links.send(src, dst, at.core)]

    def second(self):
        at = self.at
        self.x.wait_recv()
        block = self.out.at[flip(at.t, 2)]
        self.cores.append(self.links.send(block, block, at.core))

    def last(self):
        for copy in self.cores:
            copy.wait_recv()


class GradFlow:
    def __init__(self, links, at, src, land, swap, out, passing, fetch=None):
        self.links, self.at, self.src, self.land = links, at, src, land
        self.swap, self.out, self.passing, self.fetch = swap, out, passing, fetch
        self.adds = [m for m in reversed(at.masks) if not (swap and m == at.n_z // 2)]
        self.slot = {}
        n = 0
        for m in self.adds:
            for rel in range(0, at.n_z, 2 * m):
                self.slot[m, rel] = n
                n += 1
        self.got = {}
        self.at_mask = {}
        self.steps = None

    def row(self, part):
        return self.at.y if part == 0 else 1 - self.at.y

    def own(self, rel, part):
        return self.src.at[flip_all(self.at.z, rel), self.row(part)]

    def held(self, rel, part):
        m = self.at_mask.get((rel, part))
        if m is None:
            return self.own(rel, part), True
        return self.land.at[self.slot[m, rel], part], False

    def send(self, m, rel, part):
        block, _ = self.held(rel, part)
        self.got[m, rel ^ m, part] = self.links.send(
            block, self.land.at[self.slot[m, rel ^ m], part], self.at.zz(m)
        )

    def first(self, rel=None):
        m = self.adds[0]
        rels = [r for r in range(self.at.n_z) if r & m] if rel is None else [rel] if rel & m else []
        for rel in sorted(rels, reverse=True):
            for part in (1, 0):
                self.send(m, rel, part)

    def add(self, m, rel, part):
        block, is_first = self.held(rel, part)
        if is_first and self.fetch is not None:
            block = self.fetch(block)
        self.got[m, rel, part].wait_recv()
        slot = self.land.at[self.slot[m, rel], part]
        slot[...] = (block[...].astype(F32) + slot[...].astype(F32)).astype(BF16)
        self.at_mask[rel, part] = m

    def plan(self):
        steps = []
        for i, m in enumerate(self.adds):
            left = range(0, self.at.n_z, 2 * m)
            nxt = self.adds[i + 1] if i + 1 < len(self.adds) else (2 * m if self.swap else None)
            for rel in sorted(left, key=lambda r: -(r & (nxt or 0))):
                steps += [(m, nxt, rel, part) for part in (1, 0)]
        return steps

    def go(self, count=None):
        if self.steps is None:
            self.steps = self.plan()
        count = len(self.steps) if count is None else count
        for m, nxt, rel, part in self.steps[:count]:
            self.add(m, rel, part)
            if nxt is not None and rel & nxt:
                if nxt in self.adds:
                    self.send(nxt, rel, part)
                else:
                    self.exchange(nxt, rel, part)
        self.steps = self.steps[count:]

    def exchange(self, m, rel, part):
        block, _ = self.held(rel, part)
        if part == 0:
            dst = self.out.at[self.at.zb, self.at.y]
        else:
            dst = self.passing
        self.got[m, 0, part] = self.links.send(block, dst, self.at.zz(m))

    def cross(self):
        at = self.at
        block, _ = self.held(0, 1)
        dst = self.out.at[at.zb, at.y] if self.swap else self.out.at[at.y]
        self.ends = [self.links.send(block, dst, at.yy)]

    def cross_far(self):
        at = self.at
        self.got[at.n_z // 2, 0, 1].wait_recv()
        self.ends.append(self.links.send(self.passing, self.out.at[1 - at.zb, at.y], at.yy))
        self.ends.append(self.got[at.n_z // 2, 0, 0])

    def mine(self):
        at = self.at
        dst = self.out.at[at.zb, at.y] if self.swap else self.out.at[at.y]
        return self.held(0, 0)[0], dst

    def last(self):
        for copy in self.ends:
            copy.wait_recv()


def back_kernel(
    n_z, n_tp, scale, q_block, units, wide,
    x_here, dy_here, w3, d_gu, hidden, gu_src, dn_src, w_o, w_heads, norm_attn,
    mid, gains, rot, attn, stats, cos, sin, seg_col, seg_row, sel, spread,
    output, input_grad, gu_out, dn_out, o_out, in_out,
    w3_v, gu_v, hid_v,
    to_core_a, held_a, landed_a, total_a, free_a, to_core_b, held_b, landed_b, total_b, free_b,
    far_v, far_in, d_mid, row_v, d_proj, d_attn, d_qkv, dk_sum, dv_sum, o_v,
    gu_land, gu_pass, dn_land, dn_pass, fetch_gu, fetch_dn, o_land, in_land,
    send_sems, recv_sems, sems,
):
    at = Place(n_z, n_tp)
    links = Links(send_sems, recv_sems)
    z, y, t, me = at.z, at.y, at.t, at.me
    top = n_z // 2
    n_b, rows, width = 2 * n_tp, mid.shape[0], mid.shape[1]
    depth = gu_src.shape[2]
    full_len = rot.shape[0]
    h = rows // 2
    n_q = rot.shape[1] // LANES - 2
    local = []

    def move(src, dst):
        copy = pltpu.make_async_copy(src, dst, sems.at[len(local)])
        copy.start()
        local.append(copy)
        return copy

    load_w3 = move(w3, w3_v)
    load_gu, load_hid = move(d_gu, gu_v), move(hidden, hid_v)
    load_o = move(w_o, o_v)
    load_x = move(x_here.at[pl.ds(pl.multiple_of(t * rows, rows), rows)], row_v.at[0])
    load_dy = move(dy_here.at[pl.ds(pl.multiple_of(t * rows, rows), rows)], row_v.at[1])
    greet(at.peers())

    def fetch_with(buf):
        def fetch(block):
            move(block, buf).wait()
            return buf

        return fetch

    f_gu = GradFlow(links, at, gu_src, gu_land, True, gu_out, gu_pass, fetch_with(fetch_gu))
    f_dn = GradFlow(links, at, dn_src, dn_land, True, dn_out, dn_pass, fetch_with(fetch_dn))
    f_gu.first()
    f_dn.first()

    def term(seq, lhs, lo, hi):
        def product(r, cols):
            return dot(lhs[seq, flip_all(me, r)], w3_v[cols, lo:hi], ((1,), (1,)))

        return product

    bufs_a = (to_core_a, held_a, landed_a, total_a, free_a)
    bufs_b = (to_core_b, held_b, landed_b, total_b, free_b)
    load_w3.wait()
    load_gu.wait()
    far = LayerSum(links, at, rows, bufs_a, term(1, gu_v, 0, 2 * units))
    own = LayerSum(links, at, rows, bufs_b, term(0, gu_v, 0, 2 * units))
    far.begin()
    far.middle()
    own.begin()
    far.second()
    f_gu.go(1)

    def send_far(layer, i):
        sent = []
        for p, value in enumerate(layer.end()):
            far_v[i, pl.ds(p * h, h), :] = value.astype(BF16)
            sent.append(
                links.send(
                    half_rows(far_v.at[i], p, rows), half_rows(far_in.at[i], p, rows), at.zz(top),
                    kept=True,
                )
            )
        layer.release()
        return sent

    own.middle()
    sent_far = send_far(far, 0)
    own.second()
    f_gu.go(1)
    heads_v = w3_v.at[:, : w_heads.shape[1]]
    load_heads = move(w_heads, heads_v)
    load_hid.wait()
    ffn_far = LayerSum(links, at, rows, bufs_a, term(1, hid_v, wide, wide + units), far)
    ffn_own = LayerSum(links, at, rows, bufs_b, term(0, hid_v, wide, wide + units), own)
    ffn_far.begin()

    def norm_back(inputs, gain, d_normed):
        root = lax.rsqrt(jnp.mean(inputs * inputs, axis=1, keepdims=True) + NORM_EPS)
        scaled = d_normed * gain
        return root * scaled - inputs * (root * root * root) * jnp.mean(
            scaled * inputs, axis=1, keepdims=True
        )

    load_x.wait()
    load_dy.wait()
    gather = LayerGather(links, at, d_proj, rows)
    for p, value in enumerate(own.end()):
        r = slice(p * h, (p + 1) * h)
        sent_far[p].wait_recv()
        value = value + far_in[0, r, :].astype(F32)
        value = row_v[1, r, :].astype(F32) + norm_back(mid[r, :], gains[1:2, :], value)
        d_mid[r, :] = value
        d_proj[me, r, :] = value.astype(BF16)
        gather.own(p)
    own.release()
    f_dn.go(2)
    gather.far_first()
    ffn_own.begin()
    f_gu.go()
    gather.far_second()
    f_dn.go()
    gather.last()

    load_o.wait()
    w_o_all = o_v[...].reshape(width, o_v.shape[3])

    n_part = 4

    def d_attn_rows(c, carry):
        per = n_b // n_part
        r = pl.ds(pl.multiple_of(c * (per * rows), per * rows), per * rows)
        value = d_proj[pl.ds(c * per, per)].reshape(per * rows, width)
        d_attn[r, :] = dot(value, w_o_all).astype(BF16)
        return carry

    lax.fori_loop(0, n_part, d_attn_rows, 0)

    group = 1
    while 2 * depth * group % LANES:
        group *= 2
    span = 2 * depth * group

    def groups():
        rels = sorted(range(0, n_z, group), key=lambda r: (-(r & 1), -r))
        return [(r, flip_all(z, r) // group) for r in rels]

    def span_of(owner):
        return pl.ds(pl.multiple_of(owner * span, span), span)

    o_src = o_v
    f_o = GradFlow(links, at, o_src, o_land, False, o_out, None)
    for rel, owner in groups():
        lhs = jnp.concatenate([d_proj[b, :, span_of(owner)] for b in range(n_b)], axis=0)
        value = dot(lhs, attn[...], ((0,), (0,))).astype(BF16)
        o_src[pl.ds(owner * group, group)] = value.reshape(group, 2, depth, value.shape[1])
    f_o.first()
    ffn_far.middle()
    ffn_own.middle()
    gather.drain()
    load_norm = move(norm_attn, d_proj)
    dk_sum[...] = jnp.zeros_like(dk_sum)
    dv_sum[...] = jnp.zeros_like(dv_sum)
    for i in range(full_len // q_block):
        attend_back_rows(
            scale, q_block, i, rot, d_attn, stats, cos, sin, seg_col, seg_row, sel, d_qkv, dk_sum, dv_sum
        )
        if i == 0:
            ffn_far.second()
            ffn_own.second()
            f_gu.cross()
            f_dn.cross()
    attend_back_keys(scale, n_q, cos, sin, d_qkv, dk_sum, dv_sum)
    sent_ffn = send_far(ffn_far, 1)

    load_heads.wait()

    def d_term(r, cols):
        value = d_qkv[pl.ds(pl.multiple_of(flip_all(me, r) * rows, rows), rows), :]
        return dot(value, w3_v[cols, : w_heads.shape[1]], ((1,), (1,)))

    in_cols = slice(w_heads.shape[1], w_heads.shape[1] + spread.shape[0])
    in_src = w3_v.reshape(n_z, 2, depth, w3_v.shape[1]).at[:, :, :, in_cols]
    f_in = GradFlow(links, at, in_src, in_land, False, in_out, None)
    packed = dot(d_qkv[...], spread[...], ((1,), (1,))).astype(BF16)
    load_norm.wait()
    for rel, owner in groups():
        lhs = jnp.concatenate([d_proj[b, :, span_of(owner)] for b in range(n_b)], axis=0)
        w3_v[span_of(owner), in_cols] = dot(lhs, packed, ((0,), (0,))).astype(BF16)
        if group == 1:
            f_in.first(rel)
    if group > 1:
        f_in.first()
    d_in = LayerSum(links, at, rows, bufs_a, d_term, ffn_far)
    d_in.begin()
    f_o.go(2)
    d_in.middle()
    f_in.go(2)
    d_in.second()
    f_in.go(2)
    f_o.go()
    f_o.cross()
    out_g, in_g = TpGather(links, at, output), TpGather(links, at, input_grad)
    stay = []
    for p, value in enumerate(d_in.end()):
        r = slice(p * h, (p + 1) * h)
        value = d_mid[r, :] + norm_back(row_v[0, r, :].astype(F32), gains[0:1, :], value)
        row_v[1, r, :] = value.astype(BF16)
    in_g.own(row_v.at[1])
    stay.append(move(row_v.at[1], input_grad.at[t]))
    for copy in sent_far:
        copy.wait_send()
    for p, value in enumerate(ffn_own.end()):
        r = slice(p * h, (p + 1) * h)
        sent_ffn[p].wait_recv()
        value = value + far_in[1, r, :].astype(F32)
        far_v[0, r, :] = (mid[r, :] + value).astype(BF16)
    out_g.own(far_v.at[0])
    stay.append(move(far_v.at[0], output.at[t]))
    f_in.go()
    f_in.cross()
    f_gu.cross_far()
    f_dn.cross_far()
    for flow in (f_gu, f_dn, f_o, f_in):
        stay.append(move(*flow.mine()))
    in_g.second()
    out_g.second()
    for flow in (in_g, out_g, f_gu, f_dn, f_o, f_in):
        flow.last()
    for copy in stay:
        copy.wait()
    for copy in sent_ffn:
        copy.wait_send()
    links.finish(d_in, ffn_own)


def back(n_z, n_tp, scale, units, wide, *args):
    x_here, w_heads, spread, mid, sel = args[0], args[8], args[20], args[10], args[19]
    d_gu, hidden, gu_src, dn_src, w3, w_o, rot = args[3], args[4], args[5], args[6], args[2], args[7], args[12]
    half_len, width = x_here.shape
    rows = mid.shape[0]
    full_len = 2 * half_len
    depth = gu_src.shape[2]
    heads, compact = w_heads.shape[1], spread.shape[0]
    q_cols = sel.shape[1]
    any_, vmem = pl.BlockSpec(memory_space=pl.ANY), pl.BlockSpec(memory_space=pltpu.VMEM)
    shape = jax.ShapeDtypeStruct
    n_swap, n_add = max(1, n_z - 2), n_z - 1
    n_sems = 120 + 8 * n_z
    return pl.pallas_call(
        lambda *refs: back_kernel(n_z, n_tp, scale, min(256, full_len), units, wide, *refs),
        out_shape=(
            shape((n_tp, rows, width), BF16),
            shape((n_tp, rows, width), BF16),
            shape((2, 2, depth, 2 * units), BF16),
            shape((2, 2, depth, units), BF16),
            shape((2, depth, q_cols), BF16),
            shape((2, depth, compact), BF16),
        ),
        in_specs=[any_] * 10 + [vmem] * 11,
        out_specs=(any_,) * 6,
        scratch_shapes=[
            pltpu.VMEM(w3.shape, BF16),
            pltpu.VMEM(d_gu.shape, BF16),
            pltpu.VMEM(hidden.shape, BF16),
            *sum_scratch(rows, width),
            *sum_scratch(rows, width),
            pltpu.VMEM((2, rows, width), BF16),
            pltpu.VMEM((2, rows, width), BF16),
            pltpu.VMEM((rows, width), F32),
            pltpu.VMEM((2, rows, width), BF16),
            pltpu.VMEM((2 * n_tp, rows, width), BF16),
            pltpu.VMEM((full_len, q_cols), BF16),
            pltpu.VMEM((full_len, heads), BF16),
            pltpu.VMEM((full_len, LANES), F32),
            pltpu.VMEM((full_len, LANES), F32),
            pltpu.VMEM(w_o.shape, BF16),
            pltpu.VMEM((n_swap, 2, depth, 2 * units), BF16),
            pltpu.VMEM((depth, 2 * units), BF16),
            pltpu.VMEM((n_swap, 2, depth, units), BF16),
            pltpu.VMEM((depth, units), BF16),
            pltpu.VMEM((depth, 2 * units), BF16),
            pltpu.VMEM((depth, units), BF16),
            pltpu.VMEM((n_add, 2, depth, q_cols), BF16),
            pltpu.VMEM((n_add, 2, depth, compact), BF16),
            pltpu.SemaphoreType.DMA((n_sems,)),
            pltpu.SemaphoreType.DMA((n_sems,)),
            pltpu.SemaphoreType.DMA((24 + 6 * n_z,)),
        ],
        compiler_params=pltpu.CompilerParams(
            collective_id=2, has_side_effects=True, vmem_limit_bytes=BACK_LIMIT
        ),
        name="back",
    )(*args)


def body(
    tokens,
    segments,
    attn_gain,
    q_weight,
    k_weight,
    v_weight,
    o_weight,
    ffn_gain,
    gate_weight,
    up_weight,
    down_weight,
    cotangent,
):
    n_z = lax.axis_size("fsdp")
    n_tp = lax.axis_size("tp")
    _, half_len, width = tokens.shape
    full_len = segments.shape[1]
    rows = half_len // n_tp
    units = gate_weight.shape[1] // 4
    scale = HEAD_DIM ** (-0.5)

    x_here = tokens.reshape(half_len, width)
    dy_here = cotangent.reshape(half_len, width)
    k_t, v_t, o_t, down_t = k_weight.T, v_weight.T, o_weight.T, down_weight.T
    (
        w_heads, w_o, w3, gains, norm_attn, dy_all, norm_all, attn, rot, stats, mid, cos, sin, spread, sel,
        seg_col,
    ) = front(
        n_z, n_tp, scale, x_here, dy_here,
        (q_weight, k_t, v_t, o_t, gate_weight, up_weight, down_t),
        jnp.stack([attn_gain, ffn_gain]), segments,
    )
    w3 = w3.reshape(width, -1)
    norm_all = norm_all.reshape(4 * n_tp, rows, width)
    dy_all = dy_all.reshape(4 * n_tp, rows, width)
    d_gu, hidden = act(norm_all, dy_all, w3, units)
    gu_src, dn_src = terms(norm_all, dy_all, d_gu, hidden, n_z)
    output, input_grad, gu_four, dn_four, o_two, in_two = back(
        n_z, n_tp, scale, units, wide_of(units),
        x_here, dy_here, w3, d_gu.reshape(2, 2 * n_tp, rows, 2 * units),
        hidden.reshape(2, 2 * n_tp, rows, units), gu_src, dn_src, w_o, w_heads,
        norm_attn.reshape(2 * n_tp, rows, width),
        mid, gains, rot, attn, stats, cos, sin, seg_col, segments, sel, spread,
    )
    q_grad, k_grad, v_grad, sums = finish_in(
        gu_four, in_two, q_weight, k_t, v_t, gate_weight, up_weight
    )
    here, others = sum_tp(sums[:, :2].T)
    gate_grad, up_grad, down_grad, o_grad, output, input_grad = finish(
        gu_four, dn_four, o_two, output, input_grad
    )
    gain_sums = sum(others, here)
    attn_gain_grad = gain_sums[0] / attn_gain.astype(F32)
    ffn_gain_grad = gain_sums[1] / ffn_gain.astype(F32)

    return (
        output.reshape(tokens.shape),
        input_grad.reshape(tokens.shape),
        attn_gain_grad,
        q_grad,
        k_grad.T,
        v_grad.T,
        o_grad.T,
        ffn_gain_grad,
        gate_grad,
        up_grad,
        down_grad.T,
    )


def solution(mesh):
    specs = dict(
        tok=P("fsdp", "ctx", None),
        gain=P(("fsdp", "ctx")),
        row=P(("fsdp", "ctx"), "tp"),
        col=P("tp", ("fsdp", "ctx")),
    )
    tok, gain, row, col = specs["tok"], specs["gain"], specs["row"], specs["col"]
    return jax.shard_map(
        body,
        mesh=mesh,
        in_specs=(tok, P("fsdp", None), gain, row, row, row, col, gain, row, row, col, tok),
        out_specs=(tok, tok, gain, row, row, row, col, gain, row, row, col),
        check_vma=False,
    )
```

```python
import math

import jax
import jax.numpy as jnp
from jax import lax
from jax.experimental import pallas as pl
from jax.experimental.pallas import tpu as pltpu
from jax.sharding import PartitionSpec as P

HEAD_DIM = 80
HALF = HEAD_DIM // 2
LANES = 128
NORM_EPS = 1e-05
ROPE_BASE = 10000.0
MASK_FILL = -1000000000.0
F32 = jnp.float32
BF16 = jnp.bfloat16


def pp(value, axis, mask):
    size = lax.axis_size(axis)
    return lax.ppermute(value, axis, [(i, i ^ mask) for i in range(size)])


def dot(a, b, dims=((1,), (0,))):
    return lax.dot_general(a, b, (dims, ((), ())), preferred_element_type=F32)


def in_order(bit, mine, other, axis=0):
    return jnp.where(
        bit == 0, jnp.stack([mine, other], axis), jnp.stack([other, mine], axis)
    )


def pick(blocks, index):
    return lax.dynamic_index_in_dim(blocks, index, 0, keepdims=False)


def attend_rows(scale, block, i, rot, seg_col, seg_row, sel, attn, stats):
    n_q = rot.shape[1] // LANES - 2
    rows = slice(i * block, (i + 1) * block)
    keys = (i + 1) * block
    q_pos = i * block + lax.broadcasted_iota(jnp.int32, (block, keys), 0)
    k_pos = lax.broadcasted_iota(jnp.int32, (block, keys), 1)
    allowed = (seg_col[rows, :] == seg_row[:, :keys]) & (k_pos <= q_pos)
    k = rot[:keys, n_q * LANES : (n_q + 1) * LANES]
    v = rot[:keys, (n_q + 1) * LANES :]
    outs, maxes, totals = [], [], []
    for h in range(n_q):
        s = dot(rot[rows, h * LANES : (h + 1) * LANES], k, ((1,), (1,))) * scale
        s = jnp.where(allowed, s, MASK_FILL)
        top = jnp.max(s, axis=1, keepdims=True)
        e = jnp.exp(s - top)
        total = jnp.sum(e, axis=1, keepdims=True)
        outs.append(dot((e * (1.0 / total)).astype(BF16), v).astype(BF16))
        maxes.append(top)
        totals.append(total)
    attn[rows, :] = dot(jnp.concatenate(outs, axis=1), sel[...]).astype(BF16)
    stats[rows, :] = jnp.concatenate(maxes + totals, axis=1)


def turn_back(u, cos, sin, rows):
    return (u * cos[rows, :] - pltpu.roll(u, 64, 1) * sin[rows, :]).astype(BF16)


def attend_back_rows(
    scale, block, i, rot, d_attn, stats, cos, sin, seg_col, seg_row, sel, d_qkv, dk_sum, dv_sum
):
    n_q = rot.shape[1] // LANES - 2
    rows = slice(i * block, (i + 1) * block)
    keys = (i + 1) * block
    q_pos = i * block + lax.broadcasted_iota(jnp.int32, (block, keys), 0)
    k_pos = lax.broadcasted_iota(jnp.int32, (block, keys), 1)
    allowed = (seg_col[rows, :] == seg_row[:, :keys]) & (k_pos <= q_pos)
    k = rot[:keys, n_q * LANES : (n_q + 1) * LANES]
    v = rot[:keys, (n_q + 1) * LANES :]
    d_out = dot(d_attn[rows, :], sel[...], ((1,), (1,))).astype(BF16)
    stat = stats[rows, :]
    for h in range(n_q):
        q = rot[rows, h * LANES : (h + 1) * LANES]
        d_h = d_out[:, h * LANES : (h + 1) * LANES]
        s = dot(q, k, ((1,), (1,))) * scale
        s = jnp.where(allowed, s, MASK_FILL)
        p = jnp.exp(s - stat[:, h : h + 1]) * (1.0 / stat[:, n_q + h : n_q + h + 1])
        dv_sum[:keys, :] += dot(p.astype(BF16), d_h, ((0,), (0,)))
        d_p = dot(d_h, v, ((1,), (1,)))
        d_s = (p * (d_p - jnp.sum(p * d_p, axis=1, keepdims=True))).astype(BF16)
        d_q = (dot(d_s, k) * scale).astype(BF16).astype(F32)
        d_qkv[rows, h * LANES : (h + 1) * LANES] = turn_back(d_q, cos, sin, rows)
        dk_sum[:keys, :] += dot(d_s, q, ((0,), (0,)))


def attend_back_keys(scale, n_q, cos, sin, d_qkv, dk_sum, dv_sum):
    d_k = (dk_sum[...] * scale).astype(BF16).astype(F32)
    d_qkv[:, n_q * LANES : (n_q + 1) * LANES] = turn_back(d_k, cos, sin, slice(None))
    d_qkv[:, (n_q + 1) * LANES :] = dv_sum[...].astype(BF16)


VMEM_LIMIT = 56 * 1024 * 1024
BACK_LIMIT = 63 * 1024 * 1024


def sum_tp(value):
    others = [pp(value, "tp", mask) for mask in range(1, lax.axis_size("tp"))]
    return value, others


def below(top):
    masks = []
    while top > 1:
        top //= 2
        masks.append(top)
    return masks


def flip(index, mask):
    return index + mask * (1 - 2 * ((index // mask) % 2))


def flip_all(index, bits):
    mask = 1
    while mask <= bits:
        if bits & mask:
            index = flip(index, mask)
        mask *= 2
    return index


class Links:
    def __init__(self, send_sems, recv_sems):
        self.sems = (send_sems, recv_sems)
        self.copies = []
        self.count = 0

    def send(self, src, dst, peer, kept=False):
        k = self.count
        self.count += 1
        copy = pltpu.make_async_remote_copy(
            src_ref=src,
            dst_ref=dst,
            send_sem=self.sems[0].at[k],
            recv_sem=self.sems[1].at[k],
            device_id=peer,
            device_id_type=pl.DeviceIdType.MESH,
        )
        copy.start()
        if not kept:
            self.copies.append(copy)
        return copy

    def finish(self, *sums):
        for copy in self.copies:
            copy.wait_send()
        for layer in sums:
            layer.drain()


def greet(peers):
    barrier = pltpu.get_barrier_semaphore()
    for peer in peers:
        pl.semaphore_signal(barrier, inc=1, device_id=peer, device_id_type=pl.DeviceIdType.MESH)
    pl.semaphore_wait(barrier, len(peers))


class Place:
    def __init__(self, n_z, n_tp):
        self.n_z, self.n_tp = n_z, n_tp
        self.z, self.y, self.t = (lax.axis_index(a) for a in ("fsdp", "ctx", "tp"))
        self.me = self.y * n_tp + self.t
        self.core = {"tp": flip(self.t, 1)}
        self.x = {"tp": flip(self.t, 2)}
        self.yy = {"ctx": 1 - self.y}
        self.masks = below(n_z)
        self.zb = self.z // (n_z // 2)

    def zz(self, mask):
        return {"fsdp": flip(self.z, mask)}

    def peers(self):
        return [self.core, self.x, self.yy] + [self.zz(m) for m in self.masks]


class WeightFlow:
    def __init__(self, links, at, out, cross, first, second):
        self.links, self.at, self.out = links, at, out
        self.first, self.second = first, second
        self.got = {}
        self.y_copy = links.send(cross, second(None), at.yy)

    def own(self, masks=None):
        at = self.at
        for m in at.masks if masks is None else masks:
            dst = self.out.at[at.z, at.y]
            self.got[m, 0] = self.links.send(self.first(m), dst, at.zz(m))

    def arrived(self):
        self.y_copy.wait_recv()

    def crossed(self, masks=None):
        at = self.at
        for m in at.masks if masks is None else masks:
            dst = self.out.at[at.z, 1 - at.y]
            self.got[m, 1] = self.links.send(self.second(m), dst, at.zz(m))

    def take(self, rel, part):
        at = self.at
        self.got[rel, part].wait_recv()
        low = rel & -rel
        row = at.y if part == 0 else 1 - at.y
        block = self.out.at[flip_all(at.z, rel), row]
        for m in at.masks:
            if m < low:
                self.got[rel ^ m, part] = self.links.send(block, block, at.zz(m))

    def order(self):
        rels = [r for r in range(1, self.at.n_z)]
        return sorted(rels, key=lambda r: (bin(r).count("1"), -(r & -r), r))


def half_rows(ref, part, rows):
    return ref.at[pl.ds(part * (rows // 2), rows // 2)]


class LayerGather:
    def __init__(self, links, at, out, rows):
        self.links, self.at, self.out, self.rows = links, at, out, rows
        self.cores = []
        self.sent = []

    def half(self, index, part):
        return half_rows(self.out.at[index], part, self.rows)

    def send(self, src, dst, peer):
        self.sent.append(self.links.send(src, dst, peer, kept=True))
        return self.sent[-1]

    def pass_on(self, index, part, peer):
        block = self.half(index, part)
        return self.send(block, block, peer)

    def own(self, part, src=None):
        at, me = self.at, self.at.me
        a = self.half(me, part)
        src = a if src is None else src
        send = lambda peer: self.send(src, a, peer)
        if part == 0:
            self.xa, self.ya = send(at.x), send(at.yy)
        else:
            self.yb, self.xb = send(at.yy), send(at.x)
        self.cores.append(send(at.core))

    def to_core(self, index, part):
        self.cores.append(self.pass_on(index, part, self.at.core))

    def far_first(self):
        at = self.at
        self.x_of, self.y_of = flip(at.me, 2), flip(at.me, at.n_tp)
        self.diag = flip(self.x_of, at.n_tp)
        self.xa.wait_recv()
        self.y_fwd = self.pass_on(self.x_of, 0, at.yy)
        self.to_core(self.x_of, 0)
        self.yb.wait_recv()
        self.x_fwd = self.pass_on(self.y_of, 1, at.x)
        self.to_core(self.y_of, 1)

    def far_second(self):
        self.ya.wait_recv()
        self.to_core(self.y_of, 0)
        self.xb.wait_recv()
        self.to_core(self.x_of, 1)
        self.y_fwd.wait_recv()
        self.to_core(self.diag, 0)
        self.x_fwd.wait_recv()
        self.to_core(self.diag, 1)

    def last(self):
        for copy in self.cores:
            copy.wait_recv()

    def drain(self):
        for copy in self.sent:
            copy.wait_send()


class LayerSum:
    def __init__(self, links, at, rows, bufs, product, after=None):
        self.links, self.at, self.rows = links, at, rows
        self.to_core, self.held, self.landed, self.total, self.free = bufs
        self.product = product
        self.after = after

    def peers(self):
        return (self.at.core, self.at.x, self.at.yy)

    def tiles(self, some):
        width = self.total.shape[1]
        tile = 512 if width % 512 == 0 else width

        def body(c, carry):
            some(pl.ds(pl.multiple_of(c * tile, tile), tile))
            return carry

        lax.fori_loop(0, width // tile, body, 0)

    def drain(self):
        for copy in self.sent:
            copy.wait_send()
        self.sent = []

    def release(self):
        self.drain()
        for i, peer in enumerate(self.peers()):
            pl.semaphore_signal(
                self.free.at[i], inc=1, device_id=peer, device_id_type=pl.DeviceIdType.MESH
            )

    def begin(self):
        self.core = {}
        if self.after is not None:
            self.after.drain()
            for i in range(3):
                pl.semaphore_wait(self.free.at[i], 1)
        sent = []
        for i, k in enumerate((3, 1, 2, 0)):
            if i >= 2:
                sent[i - 2].wait_send()


            def some(cols, i=i, k=k):
                self.to_core[i % 2, :, cols] = self.product(2 * k + 1, cols).astype(BF16)

            self.tiles(some)
            self.core[k] = self.links.send(
                self.to_core.at[i % 2], self.held.at[k], self.at.core, kept=True
            )
            sent.append(self.core[k])
        self.sent = sent[2:]

    def middle(self):
        at, rows, h = self.at, self.rows, self.rows // 2
        held, landed = self.held, self.landed
        a, b = slice(0, h), slice(h, rows)

        def level(k):
            self.core[k].wait_recv()

            def some(cols):
                value = self.product(2 * k, cols) + held[k, :, cols].astype(F32)
                if k == 0:
                    self.total[:, cols] = value
                else:
                    held[k, :, cols] = value.astype(BF16)

            self.tiles(some)

        def send(k, i, peer):
            copy = self.links.send(held.at[k, pl.ds((i % 2) * h, h)], landed.at[i], peer, kept=True)
            self.sent.append(copy)
            return copy

        level(3)
        self.x1 = send(3, 0, at.x)
        self.y1 = send(3, 1, at.yy)
        level(1)
        x2 = send(1, 2, at.x)
        level(2)
        y2 = send(2, 3, at.yy)
        level(0)
        self.send, self.tail = send, (x2, y2)

    def second(self):
        at, h = self.at, self.rows // 2
        held, landed = self.held, self.landed
        a, b = slice(0, h), slice(h, self.rows)
        self.x1.wait_recv()
        held[2, a] = (held[2, a].astype(F32) + landed[0].astype(F32)).astype(BF16)
        y3 = self.send(2, 4, at.yy)
        self.y1.wait_recv()
        held[1, b] = (held[1, b].astype(F32) + landed[1].astype(F32)).astype(BF16)
        x3 = self.send(1, 5, at.x)
        self.tail += (y3, x3)

    def end(self):
        h = self.rows // 2
        landed, total = self.landed, self.total
        for copy in self.tail:
            copy.wait_recv()
        top = total[:h, :] + landed[2].astype(F32) + landed[4].astype(F32)
        low = total[h:, :] + landed[3].astype(F32) + landed[5].astype(F32)
        return top, low


def sum_scratch(rows, width):
    return [
        pltpu.VMEM((2, rows, width), BF16),
        pltpu.VMEM((4, rows, width), BF16),
        pltpu.VMEM((6, rows // 2, width), BF16),
        pltpu.VMEM((rows, width), F32),
        pltpu.SemaphoreType.REGULAR((3,)),
    ]


def eye(n):
    shape = (n, n)
    same = lax.broadcasted_iota(jnp.int32, shape, 0) == lax.broadcasted_iota(jnp.int32, shape, 1)
    return same.astype(F32).astype(BF16)


def column(row):
    n = row.shape[1]
    same = lax.broadcasted_iota(jnp.int32, (n, n), 0) == lax.broadcasted_iota(jnp.int32, (n, n), 1)
    return jnp.sum(jnp.where(same, row.astype(F32), 0.0), axis=1, keepdims=True)


def head_spread(n_q, compact):
    shape = (compact, (n_q + 2) * LANES)
    col, lane = (lax.broadcasted_iota(jnp.int32, shape, d) for d in (0, 1))
    at, head = col % HEAD_DIM, col // HEAD_DIM
    spot = head * LANES + at + jnp.where((at >= HALF) & (head < n_q + 1), 64 - HALF, 0)
    return ((spot == lane) & (head < n_q + 2)).astype(F32).astype(BF16)


def head_select(n_q):
    shape = (n_q * LANES, n_q * HEAD_DIM)
    lane, col = (lax.broadcasted_iota(jnp.int32, shape, d) for d in (0, 1))
    return ((col // HEAD_DIM) * LANES + col % HEAD_DIM == lane).astype(F32).astype(BF16)


def front_kernel(
    n_z, n_tp, scale, q_block,
    x_here, dy_here, q_w, k_t, v_t, o_t, gate_w, up_w, down_t, gain_rows, seg_row,
    w_heads, w_o, w3, gains, norm_attn, dy_all, norm_all, attn, rot, stats, mid, cos, sin, spread, sel, seg_col,
    w_in, x_all, qkv, to_core, held, landed, total, free, in_cross, o_cross, w3_cross,
    heads_v, norm_v, own_v, root_v, o_v, in_send, o_send, w3_send, send_sems, recv_sems, sems,
):
    at = Place(n_z, n_tp)
    links = Links(send_sems, recv_sems)
    z, y, t, me = at.z, at.y, at.t, at.me
    zb = z // (n_z // 2)
    n_b, rows, width = 2 * n_tp, x_all.shape[0] // (2 * n_tp), x_all.shape[1]
    depth = in_send.shape[1]
    full_len = x_all.shape[0]
    local = []

    def move(src, dst):
        copy = pltpu.make_async_copy(src, dst, sems.at[len(local)])
        copy.start()
        local.append(copy)
        return copy

    def block_of(ref, index):
        return ref.at[pl.ds(pl.multiple_of(index * rows, rows), rows)]

    q_cols, kv_cols = q_w.shape[1] // 2, k_t.shape[0] // 2
    units = gate_w.shape[1] // 4
    wide = w3_send.shape[3] - units
    extra = jnp.concatenate(
        [column(gain_rows[i : i + 1, :]) for i in range(2)]
        + [jnp.zeros((depth, in_send.shape[2] - q_cols - 2 * kv_cols - 2), F32)],
        axis=1,
    ).astype(BF16)
    for j in range(2):
        kv = slice(j * kv_cols, (j + 1) * kv_cols)
        turned = [dot(w[kv, :], eye(kv_cols), ((0,), (0,))).astype(BF16) for w in (k_t, v_t)]
        in_send[j] = jnp.concatenate(
            [q_w[:, j * q_cols : (j + 1) * q_cols], *turned, extra], axis=1
        )
    greet(at.peers())
    f_in = WeightFlow(
        links, at, w_in, in_send.at[1 - y], lambda m: in_send.at[y], lambda m: in_cross
    )
    f_in.own()
    own_in = move(in_send.at[y], w_in.at[z, y])
    x_mine = block_of(x_here, t)
    tok_y = links.send(x_mine, block_of(x_all, me), at.yy)
    x_own = move(x_here, x_all.at[pl.ds(pl.multiple_of(y * (full_len // 2), full_len // 2), full_len // 2)])
    dy_mine = block_of(dy_here, t)
    dy_in = move(dy_here, norm_v.at[pl.ds(0, full_len // 2)])

    for j in range(2):
        o_send[j] = o_t[:, j * q_cols : (j + 1) * q_cols]
    for j in range(4):
        cols = slice(j * units, (j + 1) * units)
        w3_send[j % 2, j // 2, :, : 2 * units] = jnp.concatenate(
            [gate_w[:, cols], up_w[:, cols]], axis=1
        )
        w3_send[j % 2, j // 2, :, wide:] = down_t[:, cols]
    f_in.arrived()
    f_in.crossed()
    cross_in = move(in_cross, w_in.at[z, 1 - y])
    f_o = WeightFlow(
        links, at, w_o, o_send.at[1 - y], lambda m: o_send.at[y], lambda m: o_cross
    )
    top = n_z // 2
    tok_y.wait_recv()
    f_3 = WeightFlow(
        links, at, w3, w3_send.at[1 - y],
        lambda m: w3_send.at[y, 1 - zb if m == top else zb],
        lambda m: w3_cross if m is None else w3_cross.at[1 - zb if m == top else zb],
    )
    dy_y = links.send(dy_mine, dy_all.at[0, me], at.yy)
    dy_in.wait()
    dy_own = move(
        norm_v.at[pl.ds(0, full_len // 2)].reshape(n_tp, rows, width),
        dy_all.at[0, pl.ds(y * n_tp, n_tp)],
    )
    y_of, x_of = flip(me, n_tp), flip(me, 2)
    y_block = block_of(x_all, y_of)
    tok_x = links.send(y_block, y_block, at.x)
    tok_c = [links.send(y_block, y_block, at.core)]
    ins = [(rel, p) for rel in f_in.order() for p in (0, 1)]
    for rel, p in ins:
        if rel == top:
            f_in.take(rel, p)
    lane = lax.broadcasted_iota(jnp.int32, (1, LANES), 1)
    within = lane % 64
    frequency = jnp.where(
        within < HALF, jnp.exp(within.astype(F32) * (-2.0 * math.log(ROPE_BASE) / HEAD_DIM)), 0.0
    )
    sign = jnp.where(lane < 64, -1.0, 1.0)
    n_q = rot.shape[1] // LANES - 2
    spread[...] = head_spread(n_q, w_in.shape[3])
    sel[...] = head_select(n_q)
    step = min(256, full_len)

    def tables(c, carry):
        at_rows = pl.ds(pl.multiple_of(c * step, step), step)
        mine = jnp.concatenate(
            [
                column(seg_row[:, pl.ds(pl.multiple_of(c * step + i, LANES), LANES)])
                for i in range(0, step, LANES)
            ],
            axis=0,
        ).astype(jnp.int32)
        seg_col[at_rows, :] = mine
        before = jnp.where(seg_row[...] < mine, 1.0, 0.0)
        start = jnp.sum(before, axis=1, keepdims=True)
        position = (c * step + lax.broadcasted_iota(jnp.int32, (step, 1), 0)).astype(F32)
        angles = (position - start) * frequency
        cos[at_rows, :] = jnp.cos(angles)
        sin[at_rows, :] = jnp.sin(angles) * sign
        return carry

    lax.fori_loop(0, full_len // step, tables, 0)
    tok_x.wait_recv()
    diag = block_of(x_all, flip(y_of, 2))
    tok_c.append(links.send(diag, diag, at.core))
    x_own.wait()

    for copy in tok_c:
        copy.wait_recv()

    def find_root(c, carry):
        at_rows = pl.ds(pl.multiple_of(c * step, step), step)
        value = x_all[at_rows, :].astype(F32)
        root_v[at_rows, :] = lax.rsqrt(jnp.mean(value * value, axis=1, keepdims=True) + NORM_EPS)
        return carry

    lax.fori_loop(0, full_len // step, find_root, 0)
    own_in.wait()
    cross_in.wait()
    dy_own.wait()

    pick_gain = (
        lax.broadcasted_iota(jnp.int32, (8, w_in.shape[3]), 1)
        == sel.shape[1] // HEAD_DIM * HEAD_DIM + 2 * HEAD_DIM + lax.broadcasted_iota(jnp.int32, (8, w_in.shape[3]), 0)
    ).astype(F32).astype(BF16)

    group = 1
    while 2 * depth * group % LANES:
        group *= 2
    span = 2 * depth * group

    def project(rel, first):
        owner = flip_all(z, rel) // group
        cols = pl.ds(pl.multiple_of(owner * span, span), span)
        weights = w_in[pl.ds(owner * group, group)].reshape(span, w_in.shape[3])
        gain = dot(pick_gain, weights, ((1,), (1,)))
        gains[:, cols] = gain
        heads = dot(weights, spread[...]).astype(BF16)
        heads_v[cols, :] = heads

        def some_rows(c, carry):
            at_rows = pl.ds(pl.multiple_of(c * step, step), step)
            value = (x_all[at_rows, cols].astype(F32) * root_v[at_rows, :] * gain[0:1, :]).astype(BF16)
            norm_v[at_rows, cols] = value
            term = dot(value, heads)
            qkv[at_rows, :] = term if first else qkv[at_rows, :] + term
            return carry

        lax.fori_loop(0, full_len // step, some_rows, 0)

    f_o.own()
    f_o.arrived()
    f_o.crossed()
    if group == 1:
        project(0, True)
    rest = [rel for rel in f_in.order() if rel != top]
    for rel in [top] + rest:
        if rel != top:
            for p in (0, 1):
                f_in.take(rel, p)
        if group == 1:
            project(rel, False)
    if group > 1:
        for rel in range(0, n_z, group):
            project(rel, rel == 0)
    heads_out = move(heads_v, w_heads)
    norm_out = move(norm_v, norm_attn)
    own_o = [move(o_send.at[y], w_o.at[z, y]), move(o_cross, w_o.at[z, 1 - y])]
    dy_y.wait_recv()
    dy_x = links.send(dy_all.at[0, y_of], dy_all.at[0, y_of], at.x)
    dy_c = [links.send(dy_all.at[0, y_of], dy_all.at[0, y_of], at.core)]
    lower = at.masks[1:]
    dy_z = [
        links.send(half_rows(dy_mine, p, rows), half_rows(dy_all.at[1, me], p, rows), at.zz(top))
        for p in (0, 1)
    ]
    f_3.own([top])
    for p in (0, 1):
        f_o.take(top, p)
    f_3.own(lower)

    def turn(c, carry):
        r = pl.ds(pl.multiple_of(c * step, step), step)
        for h in range(n_q + 1):
            u = qkv[r, h * LANES : (h + 1) * LANES]
            rot[r, h * LANES : (h + 1) * LANES] = (
                u * cos[r, :] + pltpu.roll(u, 64, 1) * sin[r, :]
            ).astype(BF16)
        rot[r, (n_q + 1) * LANES :] = qkv[r, (n_q + 1) * LANES :].astype(BF16)
        return carry

    lax.fori_loop(0, full_len // step, turn, 0)
    dy_far = LayerGather(links, at, dy_all.at[1], rows)
    for i in range(full_len // q_block):
        attend_rows(scale, q_block, i, rot, seg_col, seg_row, sel, attn, stats)
        if i == 0:
            dy_x.wait_recv()
            d_of = flip(y_of, 2)
            dy_c.append(links.send(dy_all.at[0, d_of], dy_all.at[0, d_of], at.core))
        if i == 2:
            f_3.arrived()
            f_3.crossed()
            own_3 = [move(w3_send.at[y, zb], w3.at[z, y]), move(w3_cross.at[zb], w3.at[z, 1 - y])]
    for rel in f_o.order():
        for p in (0, 1):
            if rel != top:
                f_o.take(rel, p)
    for copy in own_o:
        copy.wait()
    load_o = move(w_o.reshape(width, o_v.shape[1]), o_v)
    load_o.wait()

    def product(r, cols):
        lhs = attn[pl.ds(pl.multiple_of(flip_all(me, r) * rows, rows), rows), :]
        return dot(lhs, o_v[cols, :], ((1,), (1,)))

    layer = LayerSum(links, at, rows, (to_core, held, landed, total, free), product)
    layer.begin()
    layer.middle()
    layer.second()
    norm_own = LayerGather(links, at, norm_all.at[0], rows)
    norm_far = LayerGather(links, at, norm_all.at[1], rows)
    far = []
    h = rows // 2
    load_x = move(x_mine, own_v)
    load_x.wait()
    for p, value in enumerate(layer.end()):
        r = slice(p * h, (p + 1) * h)
        value = value + own_v[r, :].astype(F32)
        mid[r, :] = value
        root = lax.rsqrt(jnp.mean(value * value, axis=1, keepdims=True) + NORM_EPS)
        own_v[r, :] = (value * root * gains[1:2, :]).astype(BF16)
        src = own_v.at[pl.ds(p * h, h)]
        far.append(links.send(src, half_rows(norm_all.at[1, me], p, rows), at.zz(top)))
        norm_own.own(p, src)
    keep = move(own_v, norm_all.at[0, me])
    f_3.take(top, 0)
    norm_own.far_first()
    for p in (0, 1):
        dy_z[p].wait_recv()
        dy_far.own(p)
    norm_own.far_second()
    dy_far.far_first()
    for p in (0, 1):
        far[p].wait_recv()
        norm_far.own(p)
    dy_far.far_second()
    f_3.take(top, 1)
    norm_far.far_first()
    norm_far.far_second()
    for rel in f_3.order():
        for p in (0, 1):
            if rel != top:
                f_3.take(rel, p)
    for gather in (norm_own, dy_far, norm_far):
        gather.last()
        gather.drain()
    for copy in dy_c:
        copy.wait_recv()
    for copy in [heads_out, norm_out, keep] + own_3:
        copy.wait()
    links.finish(layer)


def front(n_z, n_tp, scale, x_here, dy_here, weights, gain_rows, seg_row):
    q_w, k_t, _, _, gate_w, _, _ = weights
    half_len, width = x_here.shape
    full_len = 2 * half_len
    rows = half_len // n_tp
    depth, q_cols = q_w.shape[0], q_w.shape[1] // 2
    n_q = q_cols // HEAD_DIM
    heads = (n_q + 2) * LANES
    compact = q_cols + k_t.shape[0] + 32
    units = gate_w.shape[1] // 4
    w3_cols = wide_of(units) + units
    any_, vmem = pl.BlockSpec(memory_space=pl.ANY), pl.BlockSpec(memory_space=pltpu.VMEM)
    n_sems = 80 + 6 * n_z + 32
    shape = jax.ShapeDtypeStruct
    return pl.pallas_call(
        lambda *refs: front_kernel(n_z, n_tp, scale, min(256, full_len), *refs),
        out_shape=(
            shape((width, heads), BF16),
            shape((n_z, 2, depth, q_cols), BF16),
            shape((n_z, 2, depth, w3_cols), BF16),
            shape((8, width), F32),
            shape((full_len, width), BF16),
            shape((2, 2 * n_tp, rows, width), BF16),
            shape((2, 2 * n_tp, rows, width), BF16),
            shape((full_len, q_cols), BF16),
            shape((full_len, heads), BF16),
            shape((full_len, 2 * n_q), F32),
            shape((rows, width), F32),
            shape((full_len, LANES), F32),
            shape((full_len, LANES), F32),
            shape((compact, heads), BF16),
            shape((n_q * LANES, q_cols), BF16),
            shape((full_len, 1), jnp.int32),
        ),
        in_specs=[any_] * 2 + [vmem] * 9,
        out_specs=(any_, any_, any_, vmem, any_, any_, any_) + (vmem,) * 9,
        scratch_shapes=[
            pltpu.VMEM((n_z, 2, depth, compact), BF16),
            pltpu.VMEM((full_len, width), BF16),
            pltpu.VMEM((full_len, heads), F32),
            *sum_scratch(rows, width),
            pltpu.VMEM((depth, compact), BF16),
            pltpu.VMEM((depth, q_cols), BF16),
            pltpu.VMEM((2, depth, w3_cols), BF16),
            pltpu.VMEM((width, heads), BF16),
            pltpu.VMEM((full_len, width), BF16),
            pltpu.VMEM((rows, width), BF16),
            pltpu.VMEM((full_len, 1), F32),
            pltpu.VMEM((width, q_cols), BF16),
            pltpu.VMEM((2, depth, compact), BF16),
            pltpu.VMEM((2, depth, q_cols), BF16),
            pltpu.VMEM((2, 2, depth, w3_cols), BF16),
            pltpu.SemaphoreType.DMA((n_sems,)),
            pltpu.SemaphoreType.DMA((n_sems,)),
            pltpu.SemaphoreType.DMA((16,)),
        ],
        compiler_params=pltpu.CompilerParams(
            collective_id=1, has_side_effects=True, vmem_limit_bytes=VMEM_LIMIT
        ),
        name="front",
    )(x_here, dy_here, *weights, gain_rows, seg_row)


def wide_of(units):
    return -(-2 * units // LANES) * LANES


def act_kernel(norm, dy, w3, d_gu, hidden):
    units = hidden.shape[2]
    n = norm.shape[0] * norm.shape[1]
    wide = w3.shape[1] - units
    gate_up = dot(norm[...].reshape(n, norm.shape[2]), w3[:, : 2 * units])
    d_hidden = dot(dy[...].reshape(n, dy.shape[2]), w3[:, wide:])
    gate, up = gate_up[:, :units], gate_up[:, units:]
    sig = 1.0 / (1.0 + jnp.exp(-gate))
    silu = gate * sig
    hidden[...] = (silu * up).astype(BF16).reshape(hidden.shape)
    d_up = (d_hidden * silu).astype(BF16)
    d_gate = (d_hidden * up * sig * (1.0 + gate * (1.0 - sig))).astype(BF16)
    d_gu[...] = jnp.concatenate([d_gate, d_up], axis=1).reshape(d_gu.shape)


def act(norm, dy, w3, units):
    blocks, rows, width = norm.shape
    per = max(1, 512 // rows)
    one = lambda cols: pl.BlockSpec((per, rows, cols), lambda i: (i, 0, 0))
    return pl.pallas_call(
        act_kernel,
        grid=(blocks // per,),
        out_shape=(
            jax.ShapeDtypeStruct((blocks, rows, 2 * units), BF16),
            jax.ShapeDtypeStruct((blocks, rows, units), BF16),
        ),
        in_specs=[one(width), one(width), pl.BlockSpec(w3.shape, lambda i: (0, 0))],
        out_specs=(one(2 * units), one(units)),
        compiler_params=pltpu.CompilerParams(vmem_limit_bytes=VMEM_LIMIT),
        name="act",
    )(norm, dy, w3)


def terms_kernel(norm, dy, d_gu, hidden, gu, dn):
    def term(lhs, rhs, out):
        n = lhs.shape[0] * lhs.shape[1]
        value = dot(lhs[...].reshape(n, lhs.shape[2]), rhs[...].reshape(n, rhs.shape[2]), ((0,), (0,)))
        out[...] = value.astype(BF16).reshape(out.shape)

    term(norm, d_gu, gu)
    term(dy, hidden, dn)


def terms(norm, dy, d_gu, hidden, n_z):
    blocks, rows, width = norm.shape
    depth, units = width // n_z // 2, hidden.shape[2]
    group = 1
    while 2 * depth * group % LANES:
        group *= 2
    cols = pl.BlockSpec((blocks, rows, 2 * depth * group), lambda i: (0, 0, i))
    whole = lambda a: pl.BlockSpec(a.shape, lambda i: (0, 0, 0))
    out = lambda c: pl.BlockSpec((group, 2, depth, c), lambda i: (i, 0, 0, 0))
    return pl.pallas_call(
        terms_kernel,
        grid=(n_z // group,),
        out_shape=(
            jax.ShapeDtypeStruct((n_z, 2, depth, 2 * units), BF16),
            jax.ShapeDtypeStruct((n_z, 2, depth, units), BF16),
        ),
        in_specs=[cols, cols, whole(d_gu), whole(hidden)],
        out_specs=(out(2 * units), out(units)),
        compiler_params=pltpu.CompilerParams(vmem_limit_bytes=VMEM_LIMIT),
        name="terms",
    )(norm, dy, d_gu, hidden)


def finish_in_kernel(gu, ins, q_w, k_t, v_t, gate_w, up_w, q_grad, k_grad, v_grad, sums):
    depth = q_w.shape[0]
    units, q_cols, kv_cols = gu.shape[3] // 2, q_w.shape[1] // 2, k_t.shape[0] // 2
    one = eye(depth)
    q_grad[...] = jnp.concatenate([ins[j, :, :q_cols].astype(F32) for j in range(2)], axis=1)
    first = jnp.sum(q_w[...].astype(F32) * q_grad[...], axis=1, keepdims=True)
    lo = q_cols
    for w, grad in ((k_t, k_grad), (v_t, v_grad)):
        for j in range(2):
            grad[j * kv_cols : (j + 1) * kv_cols, :] = dot(
                ins[j, :, lo : lo + kv_cols], one, ((0,), (0,))
            )
        lo += kv_cols
        first += column(jnp.sum(w[...].astype(F32) * grad[...], axis=0, keepdims=True))
    second = jnp.zeros((depth, 1), F32)
    for j in range(4):
        cols = slice(j * units, (j + 1) * units)
        weights = jnp.concatenate([gate_w[:, cols], up_w[:, cols]], axis=1).astype(F32)
        second += jnp.sum(weights * gu[j // 2, j % 2].astype(F32), axis=1, keepdims=True)
    lane = lax.broadcasted_iota(jnp.int32, sums.shape, 1)
    sums[...] = jnp.where(lane == 0, first, second)


def finish_in(gu, ins, q_w, k_t, v_t, gate_w, up_w):
    shape = lambda dims: jax.ShapeDtypeStruct(dims, F32)
    return pl.pallas_call(
        finish_in_kernel,
        out_shape=(
            shape(q_w.shape), shape(k_t.shape), shape(v_t.shape), shape((q_w.shape[0], LANES)),
        ),
        compiler_params=pltpu.CompilerParams(vmem_limit_bytes=VMEM_LIMIT),
        name="finish_in",
    )(gu, ins, q_w, k_t, v_t, gate_w, up_w)


def finish_kernel(gu, dn, o, rows_a, rows_b, gate_grad, up_grad, down_grad, o_grad, out_a, out_b):
    out_a[...] = rows_a[...]
    out_b[...] = rows_b[...]
    units = dn.shape[3]
    for grad, part in ((gate_grad, slice(0, units)), (up_grad, slice(units, 2 * units))):
        grad[...] = jnp.concatenate(
            [gu[j // 2, j % 2, :, part].astype(F32) for j in range(4)], axis=1
        )
    down_grad[...] = jnp.concatenate([dn[j // 2, j % 2].astype(F32) for j in range(4)], axis=1)
    o_grad[...] = jnp.concatenate([o[j].astype(F32) for j in range(2)], axis=1)


def finish(gu, dn, o, rows_a, rows_b):
    depth, units, q_cols = dn.shape[2], dn.shape[3], o.shape[2]
    shape = lambda cols: jax.ShapeDtypeStruct((depth, cols), F32)
    like = lambda a: jax.ShapeDtypeStruct(a.shape, a.dtype)
    return pl.pallas_call(
        finish_kernel,
        out_shape=(
            shape(4 * units), shape(4 * units), shape(4 * units), shape(2 * q_cols),
            like(rows_a), like(rows_b),
        ),
        compiler_params=pltpu.CompilerParams(vmem_limit_bytes=VMEM_LIMIT),
        cost_estimate=pl.CostEstimate(flops=0, bytes_accessed=20 * 2**20, transcendentals=0),
        name="finish",
    )(gu, dn, o, rows_a, rows_b)


class TpGather:
    def __init__(self, links, at, out):
        self.links, self.at, self.out = links, at, out

    def own(self, src):
        at = self.at
        dst = self.out.at[at.t]
        self.x = self.links.send(src, dst, at.x)
        self.cores = [self.links.send(src, dst, at.core)]

    def second(self):
        at = self.at
        self.x.wait_recv()
        block = self.out.at[flip(at.t, 2)]
        self.cores.append(self.links.send(block, block, at.core))

    def last(self):
        for copy in self.cores:
            copy.wait_recv()


class GradFlow:
    def __init__(self, links, at, src, land, swap, out, passing, fetch=None):
        self.links, self.at, self.src, self.land = links, at, src, land
        self.swap, self.out, self.passing, self.fetch = swap, out, passing, fetch
        self.adds = [m for m in reversed(at.masks) if not (swap and m == at.n_z // 2)]
        self.slot = {}
        n = 0
        for m in self.adds:
            for rel in range(0, at.n_z, 2 * m):
                self.slot[m, rel] = n
                n += 1
        self.got = {}
        self.at_mask = {}
        self.steps = None

    def row(self, part):
        return self.at.y if part == 0 else 1 - self.at.y

    def own(self, rel, part):
        return self.src.at[flip_all(self.at.z, rel), self.row(part)]

    def held(self, rel, part):
        m = self.at_mask.get((rel, part))
        if m is None:
            return self.own(rel, part), True
        return self.land.at[self.slot[m, rel], part], False

    def send(self, m, rel, part):
        block, _ = self.held(rel, part)
        self.got[m, rel ^ m, part] = self.links.send(
            block, self.land.at[self.slot[m, rel ^ m], part], self.at.zz(m)
        )

    def first(self, rel=None):
        m = self.adds[0]
        rels = [r for r in range(self.at.n_z) if r & m] if rel is None else [rel] if rel & m else []
        for rel in sorted(rels, reverse=True):
            for part in (1, 0):
                self.send(m, rel, part)

    def add(self, m, rel, part):
        block, is_first = self.held(rel, part)
        if is_first and self.fetch is not None:
            block = self.fetch(block)
        self.got[m, rel, part].wait_recv()
        slot = self.land.at[self.slot[m, rel], part]
        slot[...] = (block[...].astype(F32) + slot[...].astype(F32)).astype(BF16)
        self.at_mask[rel, part] = m

    def plan(self):
        steps = []
        for i, m in enumerate(self.adds):
            left = range(0, self.at.n_z, 2 * m)
            nxt = self.adds[i + 1] if i + 1 < len(self.adds) else (2 * m if self.swap else None)
            for rel in sorted(left, key=lambda r: -(r & (nxt or 0))):
                steps += [(m, nxt, rel, part) for part in (1, 0)]
        return steps

    def go(self, count=None):
        if self.steps is None:
            self.steps = self.plan()
        count = len(self.steps) if count is None else count
        for m, nxt, rel, part in self.steps[:count]:
            self.add(m, rel, part)
            if nxt is not None and rel & nxt:
                if nxt in self.adds:
                    self.send(nxt, rel, part)
                else:
                    self.exchange(nxt, rel, part)
        self.steps = self.steps[count:]

    def exchange(self, m, rel, part):
        block, _ = self.held(rel, part)
        if part == 0:
            dst = self.out.at[self.at.zb, self.at.y]
        else:
            dst = self.passing
        self.got[m, 0, part] = self.links.send(block, dst, self.at.zz(m))

    def cross(self):
        at = self.at
        block, _ = self.held(0, 1)
        dst = self.out.at[at.zb, at.y] if self.swap else self.out.at[at.y]
        self.ends = [self.links.send(block, dst, at.yy)]

    def cross_far(self):
        at = self.at
        self.got[at.n_z // 2, 0, 1].wait_recv()
        self.ends.append(self.links.send(self.passing, self.out.at[1 - at.zb, at.y], at.yy))
        self.ends.append(self.got[at.n_z // 2, 0, 0])

    def mine(self):
        at = self.at
        dst = self.out.at[at.zb, at.y] if self.swap else self.out.at[at.y]
        return self.held(0, 0)[0], dst

    def last(self):
        for copy in self.ends:
            copy.wait_recv()


def back_kernel(
    n_z, n_tp, scale, q_block, units, wide,
    x_here, dy_here, w3, d_gu, hidden, gu_src, dn_src, w_o, w_heads, norm_attn,
    mid, gains, rot, attn, stats, cos, sin, seg_col, seg_row, sel, spread,
    output, input_grad, gu_out, dn_out, o_out, in_out,
    w3_v, gu_v, hid_v,
    to_core_a, held_a, landed_a, total_a, free_a, to_core_b, held_b, landed_b, total_b, free_b,
    far_v, far_in, d_mid, row_v, d_proj, d_attn, d_qkv, dk_sum, dv_sum, o_v,
    gu_land, gu_pass, dn_land, dn_pass, fetch_gu, fetch_dn, o_land, in_land,
    send_sems, recv_sems, sems,
):
    at = Place(n_z, n_tp)
    links = Links(send_sems, recv_sems)
    z, y, t, me = at.z, at.y, at.t, at.me
    top = n_z // 2
    n_b, rows, width = 2 * n_tp, mid.shape[0], mid.shape[1]
    depth = gu_src.shape[2]
    full_len = rot.shape[0]
    h = rows // 2
    n_q = rot.shape[1] // LANES - 2
    local = []

    def move(src, dst):
        copy = pltpu.make_async_copy(src, dst, sems.at[len(local)])
        copy.start()
        local.append(copy)
        return copy

    load_w3 = move(w3, w3_v)
    load_gu, load_hid = move(d_gu, gu_v), move(hidden, hid_v)
    load_o = move(w_o, o_v)
    load_x = move(x_here.at[pl.ds(pl.multiple_of(t * rows, rows), rows)], row_v.at[0])
    load_dy = move(dy_here.at[pl.ds(pl.multiple_of(t * rows, rows), rows)], row_v.at[1])
    greet(at.peers())

    def fetch_with(buf):
        def fetch(block):
            move(block, buf).wait()
            return buf

        return fetch

    f_gu = GradFlow(links, at, gu_src, gu_land, True, gu_out, gu_pass, fetch_with(fetch_gu))
    f_dn = GradFlow(links, at, dn_src, dn_land, True, dn_out, dn_pass, fetch_with(fetch_dn))
    for rel in reversed(range(1, n_z, 2)):
        f_gu.first(rel)
        f_dn.first(rel)

    def term(seq, lhs, lo, hi):
        def product(r, cols):
            return dot(lhs[seq, flip_all(me, r)], w3_v[cols, lo:hi], ((1,), (1,)))

        return product

    bufs_a = (to_core_a, held_a, landed_a, total_a, free_a)
    bufs_b = (to_core_b, held_b, landed_b, total_b, free_b)
    load_w3.wait()
    load_gu.wait()
    far = LayerSum(links, at, rows, bufs_a, term(1, gu_v, 0, 2 * units))
    own = LayerSum(links, at, rows, bufs_b, term(0, gu_v, 0, 2 * units))
    far.begin()
    far.middle()
    own.begin()
    far.second()
    f_gu.go(1)

    def send_far(layer, i):
        sent = []
        for p, value in enumerate(layer.end()):
            far_v[i, pl.ds(p * h, h), :] = value.astype(BF16)
            sent.append(
                links.send(
                    half_rows(far_v.at[i], p, rows), half_rows(far_in.at[i], p, rows), at.zz(top),
                    kept=True,
                )
            )
        layer.release()
        return sent

    own.middle()
    sent_far = send_far(far, 0)
    own.second()
    f_gu.go(1)
    heads_v = w3_v.at[:, : w_heads.shape[1]]
    load_heads = move(w_heads, heads_v)
    load_hid.wait()
    ffn_far = LayerSum(links, at, rows, bufs_a, term(1, hid_v, wide, wide + units), far)
    ffn_own = LayerSum(links, at, rows, bufs_b, term(0, hid_v, wide, wide + units), own)
    ffn_far.begin()
    ffn_far.middle()

    def norm_back(inputs, gain, d_normed):
        root = lax.rsqrt(jnp.mean(inputs * inputs, axis=1, keepdims=True) + NORM_EPS)
        scaled = d_normed * gain
        return root * scaled - inputs * (root * root * root) * jnp.mean(
            scaled * inputs, axis=1, keepdims=True
        )

    load_x.wait()
    load_dy.wait()
    gather = LayerGather(links, at, d_proj, rows)
    for p, value in enumerate(own.end()):
        r = slice(p * h, (p + 1) * h)
        sent_far[p].wait_recv()
        value = value + far_in[0, r, :].astype(F32)
        value = row_v[1, r, :].astype(F32) + norm_back(mid[r, :], gains[1:2, :], value)
        d_mid[r, :] = value
        d_proj[me, r, :] = value.astype(BF16)
        gather.own(p)
    own.release()
    f_dn.go(2)
    gather.far_first()
    ffn_far.second()
    ffn_own.begin()
    gather.far_second()
    sent_ffn = send_far(ffn_far, 1)
    gather.last()

    load_o.wait()
    w_o_all = o_v[...].reshape(width, o_v.shape[3])

    n_part = 4

    def d_attn_rows(c, carry):
        per = n_b // n_part
        r = pl.ds(pl.multiple_of(c * (per * rows), per * rows), per * rows)
        value = d_proj[pl.ds(c * per, per)].reshape(per * rows, width)
        d_attn[r, :] = dot(value, w_o_all).astype(BF16)
        return carry

    lax.fori_loop(0, n_part, d_attn_rows, 0)

    group = 1
    while 2 * depth * group % LANES:
        group *= 2
    span = 2 * depth * group

    def groups():
        rels = sorted(range(0, n_z, group), key=lambda r: (-(r & 1), -r))
        return [(r, flip_all(z, r) // group) for r in rels]

    def span_of(owner):
        return pl.ds(pl.multiple_of(owner * span, span), span)

    o_src = o_v
    f_o = GradFlow(links, at, o_src, o_land, False, o_out, None)
    for rel, owner in groups():
        lhs = jnp.concatenate([d_proj[b, :, span_of(owner)] for b in range(n_b)], axis=0)
        value = dot(lhs, attn[...], ((0,), (0,))).astype(BF16)
        o_src[pl.ds(owner * group, group)] = value.reshape(group, 2, depth, value.shape[1])
    f_o.first()
    ffn_own.middle()
    gather.drain()
    load_norm = move(norm_attn, d_proj)
    dk_sum[...] = jnp.zeros_like(dk_sum)
    dv_sum[...] = jnp.zeros_like(dv_sum)
    for i in range(full_len // q_block):
        attend_back_rows(
            scale, q_block, i, rot, d_attn, stats, cos, sin, seg_col, seg_row, sel, d_qkv, dk_sum, dv_sum
        )
        if i == 0:
            ffn_own.second()
            f_gu.go()
            f_gu.cross()
        if i == 2:
            f_dn.go()
            f_dn.cross()
    attend_back_keys(scale, n_q, cos, sin, d_qkv, dk_sum, dv_sum)

    load_heads.wait()

    def d_term(r, cols):
        value = d_qkv[pl.ds(pl.multiple_of(flip_all(me, r) * rows, rows), rows), :]
        return dot(value, w3_v[cols, : w_heads.shape[1]], ((1,), (1,)))

    in_cols = slice(w_heads.shape[1], w_heads.shape[1] + spread.shape[0])
    in_src = w3_v.reshape(n_z, 2, depth, w3_v.shape[1]).at[:, :, :, in_cols]
    f_in = GradFlow(links, at, in_src, in_land, False, in_out, None)
    packed = dot(d_qkv[...], spread[...], ((1,), (1,))).astype(BF16)
    load_norm.wait()
    for rel, owner in groups():
        lhs = jnp.concatenate([d_proj[b, :, span_of(owner)] for b in range(n_b)], axis=0)
        w3_v[span_of(owner), in_cols] = dot(lhs, packed, ((0,), (0,))).astype(BF16)
        if group == 1:
            f_in.first(rel)
    if group > 1:
        f_in.first()
    d_in = LayerSum(links, at, rows, bufs_a, d_term, ffn_far)
    d_in.begin()
    f_o.go(2)
    d_in.middle()
    f_gu.cross_far()
    d_in.second()
    f_in.go(2)
    f_dn.cross_far()
    out_g, in_g = TpGather(links, at, output), TpGather(links, at, input_grad)
    stay = []
    for p, value in enumerate(d_in.end()):
        r = slice(p * h, (p + 1) * h)
        value = d_mid[r, :] + norm_back(row_v[0, r, :].astype(F32), gains[0:1, :], value)
        row_v[1, r, :] = value.astype(BF16)
    in_g.own(row_v.at[1])
    stay.append(move(row_v.at[1], input_grad.at[t]))
    for copy in sent_far:
        copy.wait_send()
    for p, value in enumerate(ffn_own.end()):
        r = slice(p * h, (p + 1) * h)
        sent_ffn[p].wait_recv()
        value = value + far_in[1, r, :].astype(F32)
        far_v[0, r, :] = (mid[r, :] + value).astype(BF16)
    out_g.own(far_v.at[0])
    f_in.go(2)
    f_o.go()
    f_o.cross()
    stay.append(move(far_v.at[0], output.at[t]))
    f_in.go()
    f_in.cross()
    for flow in (f_gu, f_dn, f_o, f_in):
        stay.append(move(*flow.mine()))
    in_g.second()
    out_g.second()
    for flow in (in_g, out_g, f_gu, f_dn, f_o, f_in):
        flow.last()
    for copy in stay:
        copy.wait()
    for copy in sent_ffn:
        copy.wait_send()
    links.finish(d_in, ffn_own)


def back(n_z, n_tp, scale, units, wide, *args):
    x_here, w_heads, spread, mid, sel = args[0], args[8], args[20], args[10], args[19]
    d_gu, hidden, gu_src, dn_src, w3, w_o, rot = args[3], args[4], args[5], args[6], args[2], args[7], args[12]
    half_len, width = x_here.shape
    rows = mid.shape[0]
    full_len = 2 * half_len
    depth = gu_src.shape[2]
    heads, compact = w_heads.shape[1], spread.shape[0]
    q_cols = sel.shape[1]
    any_, vmem = pl.BlockSpec(memory_space=pl.ANY), pl.BlockSpec(memory_space=pltpu.VMEM)
    shape = jax.ShapeDtypeStruct
    n_swap, n_add = max(1, n_z - 2), n_z - 1
    n_sems = 120 + 8 * n_z
    return pl.pallas_call(
        lambda *refs: back_kernel(n_z, n_tp, scale, min(256, full_len), units, wide, *refs),
        out_shape=(
            shape((n_tp, rows, width), BF16),
            shape((n_tp, rows, width), BF16),
            shape((2, 2, depth, 2 * units), BF16),
            shape((2, 2, depth, units), BF16),
            shape((2, depth, q_cols), BF16),
            shape((2, depth, compact), BF16),
        ),
        in_specs=[any_] * 10 + [vmem] * 11,
        out_specs=(any_,) * 6,
        scratch_shapes=[
            pltpu.VMEM(w3.shape, BF16),
            pltpu.VMEM(d_gu.shape, BF16),
            pltpu.VMEM(hidden.shape, BF16),
            *sum_scratch(rows, width),
            *sum_scratch(rows, width),
            pltpu.VMEM((2, rows, width), BF16),
            pltpu.VMEM((2, rows, width), BF16),
            pltpu.VMEM((rows, width), F32),
            pltpu.VMEM((2, rows, width), BF16),
            pltpu.VMEM((2 * n_tp, rows, width), BF16),
            pltpu.VMEM((full_len, q_cols), BF16),
            pltpu.VMEM((full_len, heads), BF16),
            pltpu.VMEM((full_len, LANES), F32),
            pltpu.VMEM((full_len, LANES), F32),
            pltpu.VMEM(w_o.shape, BF16),
            pltpu.VMEM((n_swap, 2, depth, 2 * units), BF16),
            pltpu.VMEM((depth, 2 * units), BF16),
            pltpu.VMEM((n_swap, 2, depth, units), BF16),
            pltpu.VMEM((depth, units), BF16),
            pltpu.VMEM((depth, 2 * units), BF16),
            pltpu.VMEM((depth, units), BF16),
            pltpu.VMEM((n_add, 2, depth, q_cols), BF16),
            pltpu.VMEM((n_add, 2, depth, compact), BF16),
            pltpu.SemaphoreType.DMA((n_sems,)),
            pltpu.SemaphoreType.DMA((n_sems,)),
            pltpu.SemaphoreType.DMA((24 + 6 * n_z,)),
        ],
        compiler_params=pltpu.CompilerParams(
            collective_id=2, has_side_effects=True, vmem_limit_bytes=BACK_LIMIT
        ),
        name="back",
    )(*args)


def body(
    tokens,
    segments,
    attn_gain,
    q_weight,
    k_weight,
    v_weight,
    o_weight,
    ffn_gain,
    gate_weight,
    up_weight,
    down_weight,
    cotangent,
):
    n_z = lax.axis_size("fsdp")
    n_tp = lax.axis_size("tp")
    _, half_len, width = tokens.shape
    full_len = segments.shape[1]
    rows = half_len // n_tp
    units = gate_weight.shape[1] // 4
    scale = HEAD_DIM ** (-0.5)

    x_here = tokens.reshape(half_len, width)
    dy_here = cotangent.reshape(half_len, width)
    k_t, v_t, o_t, down_t = k_weight.T, v_weight.T, o_weight.T, down_weight.T
    (
        w_heads, w_o, w3, gains, norm_attn, dy_all, norm_all, attn, rot, stats, mid, cos, sin, spread, sel,
        seg_col,
    ) = front(
        n_z, n_tp, scale, x_here, dy_here,
        (q_weight, k_t, v_t, o_t, gate_weight, up_weight, down_t),
        jnp.stack([attn_gain, ffn_gain]), segments,
    )
    w3 = w3.reshape(width, -1)
    norm_all = norm_all.reshape(4 * n_tp, rows, width)
    dy_all = dy_all.reshape(4 * n_tp, rows, width)
    d_gu, hidden = act(norm_all, dy_all, w3, units)
    gu_src, dn_src = terms(norm_all, dy_all, d_gu, hidden, n_z)
    output, input_grad, gu_four, dn_four, o_two, in_two = back(
        n_z, n_tp, scale, units, wide_of(units),
        x_here, dy_here, w3, d_gu.reshape(2, 2 * n_tp, rows, 2 * units),
        hidden.reshape(2, 2 * n_tp, rows, units), gu_src, dn_src, w_o, w_heads,
        norm_attn.reshape(2 * n_tp, rows, width),
        mid, gains, rot, attn, stats, cos, sin, seg_col, segments, sel, spread,
    )
    q_grad, k_grad, v_grad, sums = finish_in(
        gu_four, in_two, q_weight, k_t, v_t, gate_weight, up_weight
    )
    here, others = sum_tp(sums[:, :2].T)
    gate_grad, up_grad, down_grad, o_grad, output, input_grad = finish(
        gu_four, dn_four, o_two, output, input_grad
    )
    gain_sums = sum(others, here)
    attn_gain_grad = gain_sums[0] / attn_gain.astype(F32)
    ffn_gain_grad = gain_sums[1] / ffn_gain.astype(F32)

    return (
        output.reshape(tokens.shape),
        input_grad.reshape(tokens.shape),
        attn_gain_grad,
        q_grad,
        k_grad.T,
        v_grad.T,
        o_grad.T,
        ffn_gain_grad,
        gate_grad,
        up_grad,
        down_grad.T,
    )


def solution(mesh):
    specs = dict(
        tok=P("fsdp", "ctx", None),
        gain=P(("fsdp", "ctx")),
        row=P(("fsdp", "ctx"), "tp"),
        col=P("tp", ("fsdp", "ctx")),
    )
    tok, gain, row, col = specs["tok"], specs["gain"], specs["row"], specs["col"]
    return jax.shard_map(
        body,
        mesh=mesh,
        in_specs=(tok, P("fsdp", None), gain, row, row, row, col, gain, row, row, col, tok),
        out_specs=(tok, tok, gain, row, row, row, col, gain, row, row, col),
        check_vma=False,
    )
```

```python
import math

import jax
import jax.numpy as jnp
from jax import lax
from jax.experimental import pallas as pl
from jax.experimental.pallas import tpu as pltpu
from jax.sharding import PartitionSpec as P

HEAD_DIM = 80
HALF = HEAD_DIM // 2
LANES = 128
NORM_EPS = 1e-05
ROPE_BASE = 10000.0
MASK_FILL = -1000000000.0
F32 = jnp.float32
BF16 = jnp.bfloat16


def pp(value, axis, mask):
    size = lax.axis_size(axis)
    return lax.ppermute(value, axis, [(i, i ^ mask) for i in range(size)])


def dot(a, b, dims=((1,), (0,))):
    return lax.dot_general(a, b, (dims, ((), ())), preferred_element_type=F32)


def in_order(bit, mine, other, axis=0):
    return jnp.where(
        bit == 0, jnp.stack([mine, other], axis), jnp.stack([other, mine], axis)
    )


def pick(blocks, index):
    return lax.dynamic_index_in_dim(blocks, index, 0, keepdims=False)


def attend_rows(scale, block, i, rot, seg_col, seg_row, sel, attn, stats):
    n_q = rot.shape[1] // LANES - 2
    rows = slice(i * block, (i + 1) * block)
    keys = (i + 1) * block
    q_pos = i * block + lax.broadcasted_iota(jnp.int32, (block, keys), 0)
    k_pos = lax.broadcasted_iota(jnp.int32, (block, keys), 1)
    allowed = (seg_col[rows, :] == seg_row[:, :keys]) & (k_pos <= q_pos)
    k = rot[:keys, n_q * LANES : (n_q + 1) * LANES]
    v = rot[:keys, (n_q + 1) * LANES :]
    outs, maxes, totals = [], [], []
    for h in range(n_q):
        s = dot(rot[rows, h * LANES : (h + 1) * LANES], k, ((1,), (1,))) * scale
        s = jnp.where(allowed, s, MASK_FILL)
        top = jnp.max(s, axis=1, keepdims=True)
        e = jnp.exp(s - top)
        total = jnp.sum(e, axis=1, keepdims=True)
        outs.append(dot((e * (1.0 / total)).astype(BF16), v).astype(BF16))
        maxes.append(top)
        totals.append(total)
    attn[rows, :] = dot(jnp.concatenate(outs, axis=1), sel[...]).astype(BF16)
    stats[rows, :] = jnp.concatenate(maxes + totals, axis=1)


def turn_back(u, cos, sin, rows):
    return (u * cos[rows, :] - pltpu.roll(u, 64, 1) * sin[rows, :]).astype(BF16)


def attend_back_rows(
    scale, block, i, rot, d_attn, stats, cos, sin, seg_col, seg_row, sel, d_qkv, dk_sum, dv_sum
):
    n_q = rot.shape[1] // LANES - 2
    rows = slice(i * block, (i + 1) * block)
    keys = (i + 1) * block
    q_pos = i * block + lax.broadcasted_iota(jnp.int32, (block, keys), 0)
    k_pos = lax.broadcasted_iota(jnp.int32, (block, keys), 1)
    allowed = (seg_col[rows, :] == seg_row[:, :keys]) & (k_pos <= q_pos)
    k = rot[:keys, n_q * LANES : (n_q + 1) * LANES]
    v = rot[:keys, (n_q + 1) * LANES :]
    d_out = dot(d_attn[rows, :], sel[...], ((1,), (1,))).astype(BF16)
    stat = stats[rows, :]
    for h in range(n_q):
        q = rot[rows, h * LANES : (h + 1) * LANES]
        d_h = d_out[:, h * LANES : (h + 1) * LANES]
        s = dot(q, k, ((1,), (1,))) * scale
        s = jnp.where(allowed, s, MASK_FILL)
        p = jnp.exp(s - stat[:, h : h + 1]) * (1.0 / stat[:, n_q + h : n_q + h + 1])
        dv_sum[:keys, :] += dot(p.astype(BF16), d_h, ((0,), (0,)))
        d_p = dot(d_h, v, ((1,), (1,)))
        d_s = (p * (d_p - jnp.sum(p * d_p, axis=1, keepdims=True))).astype(BF16)
        d_q = (dot(d_s, k) * scale).astype(BF16).astype(F32)
        d_qkv[rows, h * LANES : (h + 1) * LANES] = turn_back(d_q, cos, sin, rows)
        dk_sum[:keys, :] += dot(d_s, q, ((0,), (0,)))


def attend_back_keys(scale, n_q, cos, sin, d_qkv, dk_sum, dv_sum):
    d_k = (dk_sum[...] * scale).astype(BF16).astype(F32)
    d_qkv[:, n_q * LANES : (n_q + 1) * LANES] = turn_back(d_k, cos, sin, slice(None))
    d_qkv[:, (n_q + 1) * LANES :] = dv_sum[...].astype(BF16)


VMEM_LIMIT = 56 * 1024 * 1024
BACK_LIMIT = 63 * 1024 * 1024


def sum_tp(value):
    others = [pp(value, "tp", mask) for mask in range(1, lax.axis_size("tp"))]
    return value, others


def below(top):
    masks = []
    while top > 1:
        top //= 2
        masks.append(top)
    return masks


def flip(index, mask):
    return index + mask * (1 - 2 * ((index // mask) % 2))


def flip_all(index, bits):
    mask = 1
    while mask <= bits:
        if bits & mask:
            index = flip(index, mask)
        mask *= 2
    return index


class Links:
    def __init__(self, send_sems, recv_sems):
        self.sems = (send_sems, recv_sems)
        self.copies = []
        self.count = 0

    def send(self, src, dst, peer, kept=False):
        k = self.count
        self.count += 1
        copy = pltpu.make_async_remote_copy(
            src_ref=src,
            dst_ref=dst,
            send_sem=self.sems[0].at[k],
            recv_sem=self.sems[1].at[k],
            device_id=peer,
            device_id_type=pl.DeviceIdType.MESH,
        )
        copy.start()
        if not kept:
            self.copies.append(copy)
        return copy

    def finish(self, *sums):
        for copy in self.copies:
            copy.wait_send()
        for layer in sums:
            layer.drain()


def greet(peers):
    barrier = pltpu.get_barrier_semaphore()
    for peer in peers:
        pl.semaphore_signal(barrier, inc=1, device_id=peer, device_id_type=pl.DeviceIdType.MESH)
    pl.semaphore_wait(barrier, len(peers))


class Place:
    def __init__(self, n_z, n_tp):
        self.n_z, self.n_tp = n_z, n_tp
        self.z, self.y, self.t = (lax.axis_index(a) for a in ("fsdp", "ctx", "tp"))
        self.me = self.y * n_tp + self.t
        self.core = {"tp": flip(self.t, 1)}
        self.x = {"tp": flip(self.t, 2)}
        self.yy = {"ctx": 1 - self.y}
        self.masks = below(n_z)
        self.zb = self.z // (n_z // 2)

    def zz(self, mask):
        return {"fsdp": flip(self.z, mask)}

    def peers(self):
        return [self.core, self.x, self.yy] + [self.zz(m) for m in self.masks]


class WeightFlow:
    def __init__(self, links, at, out, cross, first, second):
        self.links, self.at, self.out = links, at, out
        self.first, self.second = first, second
        self.got = {}
        self.y_copy = links.send(cross, second(None), at.yy)

    def own(self, masks=None):
        at = self.at
        for m in at.masks if masks is None else masks:
            dst = self.out.at[at.z, at.y]
            self.got[m, 0] = self.links.send(self.first(m), dst, at.zz(m))

    def arrived(self):
        self.y_copy.wait_recv()

    def crossed(self, masks=None):
        at = self.at
        for m in at.masks if masks is None else masks:
            dst = self.out.at[at.z, 1 - at.y]
            self.got[m, 1] = self.links.send(self.second(m), dst, at.zz(m))

    def take(self, rel, part):
        at = self.at
        self.got[rel, part].wait_recv()
        low = rel & -rel
        row = at.y if part == 0 else 1 - at.y
        block = self.out.at[flip_all(at.z, rel), row]
        for m in at.masks:
            if m < low:
                self.got[rel ^ m, part] = self.links.send(block, block, at.zz(m))

    def order(self):
        rels = [r for r in range(1, self.at.n_z)]
        return sorted(rels, key=lambda r: (bin(r).count("1"), -(r & -r), r))


def half_rows(ref, part, rows):
    return ref.at[pl.ds(part * (rows // 2), rows // 2)]


class LayerGather:
    def __init__(self, links, at, out, rows):
        self.links, self.at, self.out, self.rows = links, at, out, rows
        self.cores = []
        self.sent = []

    def half(self, index, part):
        return half_rows(self.out.at[index], part, self.rows)

    def send(self, src, dst, peer):
        self.sent.append(self.links.send(src, dst, peer, kept=True))
        return self.sent[-1]

    def pass_on(self, index, part, peer):
        block = self.half(index, part)
        return self.send(block, block, peer)

    def own(self, part, src=None):
        at, me = self.at, self.at.me
        a = self.half(me, part)
        src = a if src is None else src
        send = lambda peer: self.send(src, a, peer)
        if part == 0:
            self.xa, self.ya = send(at.x), send(at.yy)
        else:
            self.yb, self.xb = send(at.yy), send(at.x)
        self.cores.append(send(at.core))

    def to_core(self, index, part):
        self.cores.append(self.pass_on(index, part, self.at.core))

    def far_first(self):
        at = self.at
        self.x_of, self.y_of = flip(at.me, 2), flip(at.me, at.n_tp)
        self.diag = flip(self.x_of, at.n_tp)
        self.xa.wait_recv()
        self.y_fwd = self.pass_on(self.x_of, 0, at.yy)
        self.to_core(self.x_of, 0)
        self.yb.wait_recv()
        self.x_fwd = self.pass_on(self.y_of, 1, at.x)
        self.to_core(self.y_of, 1)

    def far_second(self):
        self.ya.wait_recv()
        self.to_core(self.y_of, 0)
        self.xb.wait_recv()
        self.to_core(self.x_of, 1)
        self.y_fwd.wait_recv()
        self.to_core(self.diag, 0)
        self.x_fwd.wait_recv()
        self.to_core(self.diag, 1)

    def last(self):
        for copy in self.cores:
            copy.wait_recv()

    def drain(self):
        for copy in self.sent:
            copy.wait_send()


class LayerSum:
    def __init__(self, links, at, rows, bufs, product, after=None):
        self.links, self.at, self.rows = links, at, rows
        self.to_core, self.held, self.landed, self.total, self.free = bufs
        self.product = product
        self.after = after

    def peers(self):
        return (self.at.core, self.at.x, self.at.yy)

    def tiles(self, some):
        width = self.total.shape[1]
        tile = 512 if width % 512 == 0 else width

        def body(c, carry):
            some(pl.ds(pl.multiple_of(c * tile, tile), tile))
            return carry

        lax.fori_loop(0, width // tile, body, 0)

    def drain(self):
        for copy in self.sent:
            copy.wait_send()
        self.sent = []

    def release(self):
        self.drain()
        for i, peer in enumerate(self.peers()):
            pl.semaphore_signal(
                self.free.at[i], inc=1, device_id=peer, device_id_type=pl.DeviceIdType.MESH
            )

    def begin(self):
        self.core = {}
        if self.after is not None:
            self.after.drain()
            for i in range(3):
                pl.semaphore_wait(self.free.at[i], 1)
        sent = []
        for i, k in enumerate((3, 1, 2, 0)):
            if i >= 2:
                sent[i - 2].wait_send()


            def some(cols, i=i, k=k):
                self.to_core[i % 2, :, cols] = self.product(2 * k + 1, cols).astype(BF16)

            self.tiles(some)
            self.core[k] = self.links.send(
                self.to_core.at[i % 2], self.held.at[k], self.at.core, kept=True
            )
            sent.append(self.core[k])
        self.sent = sent[2:]

    def middle(self):
        at, rows, h = self.at, self.rows, self.rows // 2
        held, landed = self.held, self.landed
        a, b = slice(0, h), slice(h, rows)

        def level(k):
            self.core[k].wait_recv()

            def some(cols):
                value = self.product(2 * k, cols) + held[k, :, cols].astype(F32)
                if k == 0:
                    self.total[:, cols] = value
                else:
                    held[k, :, cols] = value.astype(BF16)

            self.tiles(some)

        def send(k, i, peer):
            copy = self.links.send(held.at[k, pl.ds((i % 2) * h, h)], landed.at[i], peer, kept=True)
            self.sent.append(copy)
            return copy

        level(3)
        self.x1 = send(3, 0, at.x)
        self.y1 = send(3, 1, at.yy)
        level(1)
        x2 = send(1, 2, at.x)
        level(2)
        y2 = send(2, 3, at.yy)
        level(0)
        self.send, self.tail = send, (x2, y2)

    def second(self):
        at, h = self.at, self.rows // 2
        held, landed = self.held, self.landed
        a, b = slice(0, h), slice(h, self.rows)
        self.x1.wait_recv()
        held[2, a] = (held[2, a].astype(F32) + landed[0].astype(F32)).astype(BF16)
        y3 = self.send(2, 4, at.yy)
        self.y1.wait_recv()
        held[1, b] = (held[1, b].astype(F32) + landed[1].astype(F32)).astype(BF16)
        x3 = self.send(1, 5, at.x)
        self.tail += (y3, x3)

    def end(self):
        h = self.rows // 2
        landed, total = self.landed, self.total
        for copy in self.tail:
            copy.wait_recv()
        top = total[:h, :] + landed[2].astype(F32) + landed[4].astype(F32)
        low = total[h:, :] + landed[3].astype(F32) + landed[5].astype(F32)
        return top, low


def sum_scratch(rows, width):
    return [
        pltpu.VMEM((2, rows, width), BF16),
        pltpu.VMEM((4, rows, width), BF16),
        pltpu.VMEM((6, rows // 2, width), BF16),
        pltpu.VMEM((rows, width), F32),
        pltpu.SemaphoreType.REGULAR((3,)),
    ]


def eye(n):
    shape = (n, n)
    same = lax.broadcasted_iota(jnp.int32, shape, 0) == lax.broadcasted_iota(jnp.int32, shape, 1)
    return same.astype(F32).astype(BF16)


def column(row):
    n = row.shape[1]
    same = lax.broadcasted_iota(jnp.int32, (n, n), 0) == lax.broadcasted_iota(jnp.int32, (n, n), 1)
    return jnp.sum(jnp.where(same, row.astype(F32), 0.0), axis=1, keepdims=True)


def head_spread(n_q, compact):
    shape = (compact, (n_q + 2) * LANES)
    col, lane = (lax.broadcasted_iota(jnp.int32, shape, d) for d in (0, 1))
    at, head = col % HEAD_DIM, col // HEAD_DIM
    spot = head * LANES + at + jnp.where((at >= HALF) & (head < n_q + 1), 64 - HALF, 0)
    return ((spot == lane) & (head < n_q + 2)).astype(F32).astype(BF16)


def head_select(n_q):
    shape = (n_q * LANES, n_q * HEAD_DIM)
    lane, col = (lax.broadcasted_iota(jnp.int32, shape, d) for d in (0, 1))
    return ((col // HEAD_DIM) * LANES + col % HEAD_DIM == lane).astype(F32).astype(BF16)


def front_kernel(
    n_z, n_tp, scale, q_block,
    x_here, dy_here, q_w, k_t, v_t, o_t, gate_w, up_w, down_t, gain_rows, seg_row,
    w_heads, w_o, w3, gains, norm_attn, dy_all, norm_all, attn, rot, stats, mid, cos, sin, spread, sel, seg_col,
    w_in, x_all, qkv, to_core, held, landed, total, free, in_cross, o_cross, w3_cross,
    heads_v, norm_v, own_v, root_v, o_v, in_send, o_send, w3_send, send_sems, recv_sems, sems,
):
    at = Place(n_z, n_tp)
    links = Links(send_sems, recv_sems)
    z, y, t, me = at.z, at.y, at.t, at.me
    zb = z // (n_z // 2)
    n_b, rows, width = 2 * n_tp, x_all.shape[0] // (2 * n_tp), x_all.shape[1]
    depth = in_send.shape[1]
    full_len = x_all.shape[0]
    local = []

    def move(src, dst):
        copy = pltpu.make_async_copy(src, dst, sems.at[len(local)])
        copy.start()
        local.append(copy)
        return copy

    def block_of(ref, index):
        return ref.at[pl.ds(pl.multiple_of(index * rows, rows), rows)]

    q_cols, kv_cols = q_w.shape[1] // 2, k_t.shape[0] // 2
    units = gate_w.shape[1] // 4
    wide = w3_send.shape[3] - units
    extra = jnp.concatenate(
        [column(gain_rows[i : i + 1, :]) for i in range(2)]
        + [jnp.zeros((depth, in_send.shape[2] - q_cols - 2 * kv_cols - 2), F32)],
        axis=1,
    ).astype(BF16)
    for j in range(2):
        kv = slice(j * kv_cols, (j + 1) * kv_cols)
        turned = [dot(w[kv, :], eye(kv_cols), ((0,), (0,))).astype(BF16) for w in (k_t, v_t)]
        in_send[j] = jnp.concatenate(
            [q_w[:, j * q_cols : (j + 1) * q_cols], *turned, extra], axis=1
        )
    greet(at.peers())
    f_in = WeightFlow(
        links, at, w_in, in_send.at[1 - y], lambda m: in_send.at[y], lambda m: in_cross
    )
    f_in.own()
    own_in = move(in_send.at[y], w_in.at[z, y])
    x_mine = block_of(x_here, t)
    tok_y = links.send(x_mine, block_of(x_all, me), at.yy)
    x_own = move(x_here, x_all.at[pl.ds(pl.multiple_of(y * (full_len // 2), full_len // 2), full_len // 2)])
    dy_mine = block_of(dy_here, t)
    dy_in = move(dy_here, norm_v.at[pl.ds(0, full_len // 2)])

    for j in range(2):
        o_send[j] = o_t[:, j * q_cols : (j + 1) * q_cols]
    for j in range(4):
        cols = slice(j * units, (j + 1) * units)
        w3_send[j % 2, j // 2, :, : 2 * units] = jnp.concatenate(
            [gate_w[:, cols], up_w[:, cols]], axis=1
        )
        w3_send[j % 2, j // 2, :, wide:] = down_t[:, cols]
    f_in.arrived()
    f_in.crossed()
    cross_in = move(in_cross, w_in.at[z, 1 - y])
    f_o = WeightFlow(
        links, at, w_o, o_send.at[1 - y], lambda m: o_send.at[y], lambda m: o_cross
    )
    top = n_z // 2
    tok_y.wait_recv()
    f_3 = WeightFlow(
        links, at, w3, w3_send.at[1 - y],
        lambda m: w3_send.at[y, 1 - zb if m == top else zb],
        lambda m: w3_cross if m is None else w3_cross.at[1 - zb if m == top else zb],
    )
    dy_y = links.send(dy_mine, dy_all.at[0, me], at.yy)
    dy_in.wait()
    dy_own = move(
        norm_v.at[pl.ds(0, full_len // 2)].reshape(n_tp, rows, width),
        dy_all.at[0, pl.ds(y * n_tp, n_tp)],
    )
    y_of, x_of = flip(me, n_tp), flip(me, 2)
    y_block = block_of(x_all, y_of)
    tok_x = links.send(y_block, y_block, at.x)
    tok_c = [links.send(y_block, y_block, at.core)]
    ins = [(rel, p) for rel in f_in.order() for p in (0, 1)]
    for rel, p in ins:
        if rel == top:
            f_in.take(rel, p)
    lane = lax.broadcasted_iota(jnp.int32, (1, LANES), 1)
    within = lane % 64
    frequency = jnp.where(
        within < HALF, jnp.exp(within.astype(F32) * (-2.0 * math.log(ROPE_BASE) / HEAD_DIM)), 0.0
    )
    sign = jnp.where(lane < 64, -1.0, 1.0)
    n_q = rot.shape[1] // LANES - 2
    spread[...] = head_spread(n_q, w_in.shape[3])
    sel[...] = head_select(n_q)
    step = min(256, full_len)

    def tables(c, carry):
        at_rows = pl.ds(pl.multiple_of(c * step, step), step)
        mine = jnp.concatenate(
            [
                column(seg_row[:, pl.ds(pl.multiple_of(c * step + i, LANES), LANES)])
                for i in range(0, step, LANES)
            ],
            axis=0,
        ).astype(jnp.int32)
        seg_col[at_rows, :] = mine
        before = jnp.where(seg_row[...] < mine, 1.0, 0.0)
        start = jnp.sum(before, axis=1, keepdims=True)
        position = (c * step + lax.broadcasted_iota(jnp.int32, (step, 1), 0)).astype(F32)
        angles = (position - start) * frequency
        cos[at_rows, :] = jnp.cos(angles)
        sin[at_rows, :] = jnp.sin(angles) * sign
        return carry

    lax.fori_loop(0, full_len // step, tables, 0)
    tok_x.wait_recv()
    diag = block_of(x_all, flip(y_of, 2))
    tok_c.append(links.send(diag, diag, at.core))
    x_own.wait()

    for copy in tok_c:
        copy.wait_recv()

    def find_root(c, carry):
        at_rows = pl.ds(pl.multiple_of(c * step, step), step)
        value = x_all[at_rows, :].astype(F32)
        root_v[at_rows, :] = lax.rsqrt(jnp.mean(value * value, axis=1, keepdims=True) + NORM_EPS)
        return carry

    lax.fori_loop(0, full_len // step, find_root, 0)
    own_in.wait()
    cross_in.wait()
    dy_own.wait()

    pick_gain = (
        lax.broadcasted_iota(jnp.int32, (8, w_in.shape[3]), 1)
        == sel.shape[1] // HEAD_DIM * HEAD_DIM + 2 * HEAD_DIM + lax.broadcasted_iota(jnp.int32, (8, w_in.shape[3]), 0)
    ).astype(F32).astype(BF16)

    group = 1
    while 2 * depth * group % LANES:
        group *= 2
    span = 2 * depth * group

    def project(rel, first):
        owner = flip_all(z, rel) // group
        cols = pl.ds(pl.multiple_of(owner * span, span), span)
        weights = w_in[pl.ds(owner * group, group)].reshape(span, w_in.shape[3])
        gain = dot(pick_gain, weights, ((1,), (1,)))
        gains[:, cols] = gain
        heads = dot(weights, spread[...]).astype(BF16)
        heads_v[cols, :] = heads

        def some_rows(c, carry):
            at_rows = pl.ds(pl.multiple_of(c * step, step), step)
            value = (x_all[at_rows, cols].astype(F32) * root_v[at_rows, :] * gain[0:1, :]).astype(BF16)
            norm_v[at_rows, cols] = value
            term = dot(value, heads)
            qkv[at_rows, :] = term if first else qkv[at_rows, :] + term
            return carry

        lax.fori_loop(0, full_len // step, some_rows, 0)

    f_o.own()
    f_o.arrived()
    f_o.crossed()
    if group == 1:
        project(0, True)
    rest = [rel for rel in f_in.order() if rel != top]
    for rel in [top] + rest:
        if rel != top:
            for p in (0, 1):
                f_in.take(rel, p)
        if group == 1:
            project(rel, False)
    if group > 1:
        for rel in range(0, n_z, group):
            project(rel, rel == 0)
    heads_out = move(heads_v, w_heads)
    norm_out = move(norm_v, norm_attn)
    own_o = [move(o_send.at[y], w_o.at[z, y]), move(o_cross, w_o.at[z, 1 - y])]
    dy_y.wait_recv()
    dy_x = links.send(dy_all.at[0, y_of], dy_all.at[0, y_of], at.x)
    dy_c = [links.send(dy_all.at[0, y_of], dy_all.at[0, y_of], at.core)]
    lower = at.masks[1:]
    dy_z = [
        links.send(half_rows(dy_mine, p, rows), half_rows(dy_all.at[1, me], p, rows), at.zz(top))
        for p in (0, 1)
    ]
    f_3.own([top])
    for p in (0, 1):
        f_o.take(top, p)
    f_3.own(lower)

    def turn(c, carry):
        r = pl.ds(pl.multiple_of(c * step, step), step)
        for h in range(n_q + 1):
            u = qkv[r, h * LANES : (h + 1) * LANES]
            rot[r, h * LANES : (h + 1) * LANES] = (
                u * cos[r, :] + pltpu.roll(u, 64, 1) * sin[r, :]
            ).astype(BF16)
        rot[r, (n_q + 1) * LANES :] = qkv[r, (n_q + 1) * LANES :].astype(BF16)
        return carry

    lax.fori_loop(0, full_len // step, turn, 0)
    dy_far = LayerGather(links, at, dy_all.at[1], rows)
    for i in range(full_len // q_block):
        attend_rows(scale, q_block, i, rot, seg_col, seg_row, sel, attn, stats)
        if i == 0:
            dy_x.wait_recv()
            d_of = flip(y_of, 2)
            dy_c.append(links.send(dy_all.at[0, d_of], dy_all.at[0, d_of], at.core))
        if i == 2:
            f_3.arrived()
            f_3.crossed()
            own_3 = [move(w3_send.at[y, zb], w3.at[z, y]), move(w3_cross.at[zb], w3.at[z, 1 - y])]
    for rel in f_o.order():
        for p in (0, 1):
            if rel != top:
                f_o.take(rel, p)
    for copy in own_o:
        copy.wait()
    load_o = move(w_o.reshape(width, o_v.shape[1]), o_v)
    load_o.wait()

    def product(r, cols):
        lhs = attn[pl.ds(pl.multiple_of(flip_all(me, r) * rows, rows), rows), :]
        return dot(lhs, o_v[cols, :], ((1,), (1,)))

    layer = LayerSum(links, at, rows, (to_core, held, landed, total, free), product)
    layer.begin()
    layer.middle()
    layer.second()
    norm_own = LayerGather(links, at, norm_all.at[0], rows)
    norm_far = LayerGather(links, at, norm_all.at[1], rows)
    far = []
    h = rows // 2
    load_x = move(x_mine, own_v)
    load_x.wait()
    for p, value in enumerate(layer.end()):
        r = slice(p * h, (p + 1) * h)
        value = value + own_v[r, :].astype(F32)
        mid[r, :] = value
        root = lax.rsqrt(jnp.mean(value * value, axis=1, keepdims=True) + NORM_EPS)
        own_v[r, :] = (value * root * gains[1:2, :]).astype(BF16)
        src = own_v.at[pl.ds(p * h, h)]
        far.append(links.send(src, half_rows(norm_all.at[1, me], p, rows), at.zz(top)))
        norm_own.own(p, src)
    keep = move(own_v, norm_all.at[0, me])
    f_3.take(top, 0)
    norm_own.far_first()
    for p in (0, 1):
        dy_z[p].wait_recv()
        dy_far.own(p)
    norm_own.far_second()
    dy_far.far_first()
    for p in (0, 1):
        far[p].wait_recv()
        norm_far.own(p)
    dy_far.far_second()
    f_3.take(top, 1)
    norm_far.far_first()
    norm_far.far_second()
    for rel in f_3.order():
        for p in (0, 1):
            if rel != top:
                f_3.take(rel, p)
    for gather in (norm_own, dy_far, norm_far):
        gather.last()
        gather.drain()
    for copy in dy_c:
        copy.wait_recv()
    for copy in [heads_out, norm_out, keep] + own_3:
        copy.wait()
    links.finish(layer)


def front(n_z, n_tp, scale, x_here, dy_here, weights, gain_rows, seg_row):
    q_w, k_t, _, _, gate_w, _, _ = weights
    half_len, width = x_here.shape
    full_len = 2 * half_len
    rows = half_len // n_tp
    depth, q_cols = q_w.shape[0], q_w.shape[1] // 2
    n_q = q_cols // HEAD_DIM
    heads = (n_q + 2) * LANES
    compact = q_cols + k_t.shape[0] + 32
    units = gate_w.shape[1] // 4
    w3_cols = wide_of(units) + units
    any_, vmem = pl.BlockSpec(memory_space=pl.ANY), pl.BlockSpec(memory_space=pltpu.VMEM)
    n_sems = 80 + 6 * n_z + 32
    shape = jax.ShapeDtypeStruct
    return pl.pallas_call(
        lambda *refs: front_kernel(n_z, n_tp, scale, min(256, full_len), *refs),
        out_shape=(
            shape((width, heads), BF16),
            shape((n_z, 2, depth, q_cols), BF16),
            shape((n_z, 2, depth, w3_cols), BF16),
            shape((8, width), F32),
            shape((full_len, width), BF16),
            shape((2, 2 * n_tp, rows, width), BF16),
            shape((2, 2 * n_tp, rows, width), BF16),
            shape((full_len, q_cols), BF16),
            shape((full_len, heads), BF16),
            shape((full_len, 2 * n_q), F32),
            shape((rows, width), F32),
            shape((full_len, LANES), F32),
            shape((full_len, LANES), F32),
            shape((compact, heads), BF16),
            shape((n_q * LANES, q_cols), BF16),
            shape((full_len, 1), jnp.int32),
        ),
        in_specs=[any_] * 2 + [vmem] * 9,
        out_specs=(any_, any_, any_, vmem, any_, any_, any_) + (vmem,) * 9,
        scratch_shapes=[
            pltpu.VMEM((n_z, 2, depth, compact), BF16),
            pltpu.VMEM((full_len, width), BF16),
            pltpu.VMEM((full_len, heads), F32),
            *sum_scratch(rows, width),
            pltpu.VMEM((depth, compact), BF16),
            pltpu.VMEM((depth, q_cols), BF16),
            pltpu.VMEM((2, depth, w3_cols), BF16),
            pltpu.VMEM((width, heads), BF16),
            pltpu.VMEM((full_len, width), BF16),
            pltpu.VMEM((rows, width), BF16),
            pltpu.VMEM((full_len, 1), F32),
            pltpu.VMEM((width, q_cols), BF16),
            pltpu.VMEM((2, depth, compact), BF16),
            pltpu.VMEM((2, depth, q_cols), BF16),
            pltpu.VMEM((2, 2, depth, w3_cols), BF16),
            pltpu.SemaphoreType.DMA((n_sems,)),
            pltpu.SemaphoreType.DMA((n_sems,)),
            pltpu.SemaphoreType.DMA((16,)),
        ],
        compiler_params=pltpu.CompilerParams(
            collective_id=1, has_side_effects=True, vmem_limit_bytes=VMEM_LIMIT
        ),
        name="front",
    )(x_here, dy_here, *weights, gain_rows, seg_row)


def wide_of(units):
    return -(-2 * units // LANES) * LANES


def act_kernel(norm, dy, w3, d_gu, hidden):
    units = hidden.shape[2]
    n = norm.shape[0] * norm.shape[1]
    wide = w3.shape[1] - units
    gate_up = dot(norm[...].reshape(n, norm.shape[2]), w3[:, : 2 * units])
    d_hidden = dot(dy[...].reshape(n, dy.shape[2]), w3[:, wide:])
    gate, up = gate_up[:, :units], gate_up[:, units:]
    sig = 1.0 / (1.0 + jnp.exp(-gate))
    silu = gate * sig
    hidden[...] = (silu * up).astype(BF16).reshape(hidden.shape)
    d_up = (d_hidden * silu).astype(BF16)
    d_gate = (d_hidden * up * sig * (1.0 + gate * (1.0 - sig))).astype(BF16)
    d_gu[...] = jnp.concatenate([d_gate, d_up], axis=1).reshape(d_gu.shape)


def act(norm, dy, w3, units):
    blocks, rows, width = norm.shape
    per = max(1, 256 // rows)
    one = lambda cols: pl.BlockSpec((per, rows, cols), lambda i: (i, 0, 0))
    return pl.pallas_call(
        act_kernel,
        grid=(blocks // per,),
        out_shape=(
            jax.ShapeDtypeStruct((blocks, rows, 2 * units), BF16),
            jax.ShapeDtypeStruct((blocks, rows, units), BF16),
        ),
        in_specs=[one(width), one(width), pl.BlockSpec(w3.shape, lambda i: (0, 0))],
        out_specs=(one(2 * units), one(units)),
        compiler_params=pltpu.CompilerParams(vmem_limit_bytes=VMEM_LIMIT),
        name="act",
    )(norm, dy, w3)


def terms_kernel(norm, dy, d_gu, hidden, gu, dn):
    def term(lhs, rhs, out):
        n = lhs.shape[0] * lhs.shape[1]
        value = dot(lhs[...].reshape(n, lhs.shape[2]), rhs[...].reshape(n, rhs.shape[2]), ((0,), (0,)))
        out[...] = value.astype(BF16).reshape(out.shape)

    term(norm, d_gu, gu)
    term(dy, hidden, dn)


def terms(norm, dy, d_gu, hidden, n_z):
    blocks, rows, width = norm.shape
    depth, units = width // n_z // 2, hidden.shape[2]
    group = 1
    while 2 * depth * group % LANES:
        group *= 2
    cols = pl.BlockSpec((blocks, rows, 2 * depth * group), lambda i: (0, 0, i))
    whole = lambda a: pl.BlockSpec(a.shape, lambda i: (0, 0, 0))
    out = lambda c: pl.BlockSpec((group, 2, depth, c), lambda i: (i, 0, 0, 0))
    return pl.pallas_call(
        terms_kernel,
        grid=(n_z // group,),
        out_shape=(
            jax.ShapeDtypeStruct((n_z, 2, depth, 2 * units), BF16),
            jax.ShapeDtypeStruct((n_z, 2, depth, units), BF16),
        ),
        in_specs=[cols, cols, whole(d_gu), whole(hidden)],
        out_specs=(out(2 * units), out(units)),
        compiler_params=pltpu.CompilerParams(vmem_limit_bytes=VMEM_LIMIT),
        name="terms",
    )(norm, dy, d_gu, hidden)


def finish_in_kernel(gu, ins, q_w, k_t, v_t, gate_w, up_w, q_grad, k_grad, v_grad, sums):
    depth = q_w.shape[0]
    units, q_cols, kv_cols = gu.shape[3] // 2, q_w.shape[1] // 2, k_t.shape[0] // 2
    one = eye(depth)
    q_grad[...] = jnp.concatenate([ins[j, :, :q_cols].astype(F32) for j in range(2)], axis=1)
    first = jnp.sum(q_w[...].astype(F32) * q_grad[...], axis=1, keepdims=True)
    lo = q_cols
    for w, grad in ((k_t, k_grad), (v_t, v_grad)):
        for j in range(2):
            grad[j * kv_cols : (j + 1) * kv_cols, :] = dot(
                ins[j, :, lo : lo + kv_cols], one, ((0,), (0,))
            )
        lo += kv_cols
        first += column(jnp.sum(w[...].astype(F32) * grad[...], axis=0, keepdims=True))
    second = jnp.zeros((depth, 1), F32)
    for j in range(4):
        cols = slice(j * units, (j + 1) * units)
        weights = jnp.concatenate([gate_w[:, cols], up_w[:, cols]], axis=1).astype(F32)
        second += jnp.sum(weights * gu[j // 2, j % 2].astype(F32), axis=1, keepdims=True)
    lane = lax.broadcasted_iota(jnp.int32, sums.shape, 1)
    sums[...] = jnp.where(lane == 0, first, second)


def finish_in(gu, ins, q_w, k_t, v_t, gate_w, up_w):
    shape = lambda dims: jax.ShapeDtypeStruct(dims, F32)
    return pl.pallas_call(
        finish_in_kernel,
        out_shape=(
            shape(q_w.shape), shape(k_t.shape), shape(v_t.shape), shape((q_w.shape[0], LANES)),
        ),
        compiler_params=pltpu.CompilerParams(vmem_limit_bytes=VMEM_LIMIT),
        name="finish_in",
    )(gu, ins, q_w, k_t, v_t, gate_w, up_w)


def finish_kernel(gu, dn, o, rows_a, rows_b, gate_grad, up_grad, down_grad, o_grad, out_a, out_b):
    out_a[...] = rows_a[...]
    out_b[...] = rows_b[...]
    units = dn.shape[3]
    for grad, part in ((gate_grad, slice(0, units)), (up_grad, slice(units, 2 * units))):
        grad[...] = jnp.concatenate(
            [gu[j // 2, j % 2, :, part].astype(F32) for j in range(4)], axis=1
        )
    down_grad[...] = jnp.concatenate([dn[j // 2, j % 2].astype(F32) for j in range(4)], axis=1)
    o_grad[...] = jnp.concatenate([o[j].astype(F32) for j in range(2)], axis=1)


def finish(gu, dn, o, rows_a, rows_b):
    depth, units, q_cols = dn.shape[2], dn.shape[3], o.shape[2]
    n_rows, width = rows_a.shape[0], rows_a.shape[2]
    steps = n_rows if depth % (16 * n_rows) == 0 else 1
    part = depth // steps
    shape = lambda cols: jax.ShapeDtypeStruct((depth, cols), F32)
    like = lambda a: jax.ShapeDtypeStruct(a.shape, a.dtype)
    four = lambda cols: pl.BlockSpec((2, 2, part, cols), lambda i: (0, 0, i, 0))
    out = lambda cols: pl.BlockSpec((part, cols), lambda i: (i, 0))
    rows = pl.BlockSpec((n_rows // steps, rows_a.shape[1], width), lambda i: (i, 0, 0))
    return pl.pallas_call(
        finish_kernel,
        grid=(steps,),
        out_shape=(
            shape(4 * units), shape(4 * units), shape(4 * units), shape(2 * q_cols),
            like(rows_a), like(rows_b),
        ),
        in_specs=[
            four(2 * units), four(units), pl.BlockSpec((2, part, q_cols), lambda i: (0, i, 0)),
            rows, rows,
        ],
        out_specs=(out(4 * units), out(4 * units), out(4 * units), out(2 * q_cols), rows, rows),
        compiler_params=pltpu.CompilerParams(vmem_limit_bytes=VMEM_LIMIT),
        cost_estimate=pl.CostEstimate(flops=0, bytes_accessed=20 * 2**20, transcendentals=0),
        name="finish",
    )(gu, dn, o, rows_a, rows_b)


class TpGather:
    def __init__(self, links, at, out):
        self.links, self.at, self.out = links, at, out

    def own(self, src):
        at = self.at
        dst = self.out.at[at.t]
        self.x = self.links.send(src, dst, at.x)
        self.cores = [self.links.send(src, dst, at.core)]

    def second(self):
        at = self.at
        self.x.wait_recv()
        block = self.out.at[flip(at.t, 2)]
        self.cores.append(self.links.send(block, block, at.core))

    def last(self):
        for copy in self.cores:
            copy.wait_recv()


class GradFlow:
    def __init__(self, links, at, src, land, swap, out, passing, fetch=None):
        self.links, self.at, self.src, self.land = links, at, src, land
        self.swap, self.out, self.passing, self.fetch = swap, out, passing, fetch
        self.adds = [m for m in reversed(at.masks) if not (swap and m == at.n_z // 2)]
        self.slot = {}
        n = 0
        for m in self.adds:
            for rel in range(0, at.n_z, 2 * m):
                self.slot[m, rel] = n
                n += 1
        self.got = {}
        self.at_mask = {}
        self.steps = None

    def row(self, part):
        return self.at.y if part == 0 else 1 - self.at.y

    def own(self, rel, part):
        return self.src.at[flip_all(self.at.z, rel), self.row(part)]

    def held(self, rel, part):
        m = self.at_mask.get((rel, part))
        if m is None:
            return self.own(rel, part), True
        return self.land.at[self.slot[m, rel], part], False

    def send(self, m, rel, part):
        block, _ = self.held(rel, part)
        self.got[m, rel ^ m, part] = self.links.send(
            block, self.land.at[self.slot[m, rel ^ m], part], self.at.zz(m)
        )

    def first(self, rel=None):
        m = self.adds[0]
        rels = [r for r in range(self.at.n_z) if r & m] if rel is None else [rel] if rel & m else []
        for rel in sorted(rels, reverse=True):
            for part in (1, 0):
                self.send(m, rel, part)

    def add(self, m, rel, part):
        block, is_first = self.held(rel, part)
        if is_first and self.fetch is not None:
            block = self.fetch(block)
        self.got[m, rel, part].wait_recv()
        slot = self.land.at[self.slot[m, rel], part]
        slot[...] = (block[...].astype(F32) + slot[...].astype(F32)).astype(BF16)
        self.at_mask[rel, part] = m

    def plan(self):
        steps = []
        for i, m in enumerate(self.adds):
            left = range(0, self.at.n_z, 2 * m)
            nxt = self.adds[i + 1] if i + 1 < len(self.adds) else (2 * m if self.swap else None)
            for rel in sorted(left, key=lambda r: -(r & (nxt or 0))):
                steps += [(m, nxt, rel, part) for part in (1, 0)]
        return steps

    def go(self, count=None):
        if self.steps is None:
            self.steps = self.plan()
        count = len(self.steps) if count is None else count
        for m, nxt, rel, part in self.steps[:count]:
            self.add(m, rel, part)
            if nxt is not None and rel & nxt:
                if nxt in self.adds:
                    self.send(nxt, rel, part)
                else:
                    self.exchange(nxt, rel, part)
        self.steps = self.steps[count:]

    def exchange(self, m, rel, part):
        block, _ = self.held(rel, part)
        if part == 0:
            dst = self.out.at[self.at.zb, self.at.y]
        else:
            dst = self.passing
        self.got[m, 0, part] = self.links.send(block, dst, self.at.zz(m))

    def cross(self):
        at = self.at
        block, _ = self.held(0, 1)
        dst = self.out.at[at.zb, at.y] if self.swap else self.out.at[at.y]
        self.ends = [self.links.send(block, dst, at.yy)]

    def cross_far(self):
        at = self.at
        self.got[at.n_z // 2, 0, 1].wait_recv()
        self.ends.append(self.links.send(self.passing, self.out.at[1 - at.zb, at.y], at.yy))
        self.ends.append(self.got[at.n_z // 2, 0, 0])

    def mine(self):
        at = self.at
        dst = self.out.at[at.zb, at.y] if self.swap else self.out.at[at.y]
        return self.held(0, 0)[0], dst

    def last(self):
        for copy in self.ends:
            copy.wait_recv()


def back_kernel(
    n_z, n_tp, scale, q_block, units, wide,
    x_here, dy_here, w3, d_gu, hidden, gu_src, dn_src, w_o, w_heads, norm_attn,
    mid, gains, rot, attn, stats, cos, sin, seg_col, seg_row, sel, spread,
    output, input_grad, gu_out, dn_out, o_out, in_out,
    w3_v, gu_v, hid_v,
    to_core_a, held_a, landed_a, total_a, free_a, to_core_b, held_b, landed_b, total_b, free_b,
    far_v, far_in, d_mid, row_v, d_proj, d_attn, d_qkv, dk_sum, dv_sum, o_v,
    gu_land, gu_pass, dn_land, dn_pass, fetch_gu, fetch_dn, o_land, in_land,
    send_sems, recv_sems, sems,
):
    at = Place(n_z, n_tp)
    links = Links(send_sems, recv_sems)
    z, y, t, me = at.z, at.y, at.t, at.me
    top = n_z // 2
    n_b, rows, width = 2 * n_tp, mid.shape[0], mid.shape[1]
    depth = gu_src.shape[2]
    full_len = rot.shape[0]
    h = rows // 2
    n_q = rot.shape[1] // LANES - 2
    local = []

    def move(src, dst):
        copy = pltpu.make_async_copy(src, dst, sems.at[len(local)])
        copy.start()
        local.append(copy)
        return copy

    load_w3 = move(w3, w3_v)
    load_gu, load_hid = move(d_gu, gu_v), move(hidden, hid_v)
    load_o = move(w_o, o_v)
    load_x = move(x_here.at[pl.ds(pl.multiple_of(t * rows, rows), rows)], row_v.at[0])
    load_dy = move(dy_here.at[pl.ds(pl.multiple_of(t * rows, rows), rows)], row_v.at[1])
    greet(at.peers())

    def fetch_with(buf):
        def fetch(block):
            move(block, buf).wait()
            return buf

        return fetch

    f_gu = GradFlow(links, at, gu_src, gu_land, True, gu_out, gu_pass, fetch_with(fetch_gu))
    f_dn = GradFlow(links, at, dn_src, dn_land, True, dn_out, dn_pass, fetch_with(fetch_dn))
    for rel in reversed(range(1, n_z, 2)):
        f_gu.first(rel)
        f_dn.first(rel)

    def term(seq, lhs, lo, hi):
        def product(r, cols):
            return dot(lhs[seq, flip_all(me, r)], w3_v[cols, lo:hi], ((1,), (1,)))

        return product

    bufs_a = (to_core_a, held_a, landed_a, total_a, free_a)
    bufs_b = (to_core_b, held_b, landed_b, total_b, free_b)
    load_w3.wait()
    load_gu.wait()
    far = LayerSum(links, at, rows, bufs_a, term(1, gu_v, 0, 2 * units))
    own = LayerSum(links, at, rows, bufs_b, term(0, gu_v, 0, 2 * units))
    far.begin()
    far.middle()
    own.begin()
    far.second()
    f_gu.go(1)

    def send_far(layer, i):
        sent = []
        for p, value in enumerate(layer.end()):
            far_v[i, pl.ds(p * h, h), :] = value.astype(BF16)
            sent.append(
                links.send(
                    half_rows(far_v.at[i], p, rows), half_rows(far_in.at[i], p, rows), at.zz(top),
                    kept=True,
                )
            )
        layer.release()
        return sent

    own.middle()
    sent_far = send_far(far, 0)
    own.second()
    f_gu.go(1)
    heads_v = w3_v.at[:, : w_heads.shape[1]]
    load_heads = move(w_heads, heads_v)
    load_hid.wait()
    ffn_far = LayerSum(links, at, rows, bufs_a, term(1, hid_v, wide, wide + units), far)
    ffn_own = LayerSum(links, at, rows, bufs_b, term(0, hid_v, wide, wide + units), own)
    ffn_far.begin()
    ffn_far.middle()

    def norm_back(inputs, gain, d_normed):
        root = lax.rsqrt(jnp.mean(inputs * inputs, axis=1, keepdims=True) + NORM_EPS)
        scaled = d_normed * gain
        return root * scaled - inputs * (root * root * root) * jnp.mean(
            scaled * inputs, axis=1, keepdims=True
        )

    load_x.wait()
    load_dy.wait()
    gather = LayerGather(links, at, d_proj, rows)
    for p, value in enumerate(own.end()):
        r = slice(p * h, (p + 1) * h)
        sent_far[p].wait_recv()
        value = value + far_in[0, r, :].astype(F32)
        value = row_v[1, r, :].astype(F32) + norm_back(mid[r, :], gains[1:2, :], value)
        d_mid[r, :] = value
        d_proj[me, r, :] = value.astype(BF16)
        gather.own(p)
    own.release()
    f_dn.go(2)
    gather.far_first()
    ffn_far.second()
    ffn_own.begin()
    gather.far_second()
    sent_ffn = send_far(ffn_far, 1)
    gather.last()

    load_o.wait()
    w_o_all = o_v[...].reshape(width, o_v.shape[3])

    n_part = 4

    def d_attn_rows(c, carry):
        per = n_b // n_part
        r = pl.ds(pl.multiple_of(c * (per * rows), per * rows), per * rows)
        value = d_proj[pl.ds(c * per, per)].reshape(per * rows, width)
        d_attn[r, :] = dot(value, w_o_all).astype(BF16)
        return carry

    lax.fori_loop(0, n_part, d_attn_rows, 0)

    group = 1
    while 2 * depth * group % LANES:
        group *= 2
    span = 2 * depth * group

    def groups():
        rels = sorted(range(0, n_z, group), key=lambda r: (-(r & 1), -r))
        return [(r, flip_all(z, r) // group) for r in rels]

    def span_of(owner):
        return pl.ds(pl.multiple_of(owner * span, span), span)

    o_src = o_v
    f_o = GradFlow(links, at, o_src, o_land, False, o_out, None)
    for rel, owner in groups():
        lhs = jnp.concatenate([d_proj[b, :, span_of(owner)] for b in range(n_b)], axis=0)
        value = dot(lhs, attn[...], ((0,), (0,))).astype(BF16)
        o_src[pl.ds(owner * group, group)] = value.reshape(group, 2, depth, value.shape[1])
    f_o.first()
    ffn_own.middle()
    gather.drain()
    load_norm = move(norm_attn, d_proj)
    dk_sum[...] = jnp.zeros_like(dk_sum)
    dv_sum[...] = jnp.zeros_like(dv_sum)
    for i in range(full_len // q_block):
        attend_back_rows(
            scale, q_block, i, rot, d_attn, stats, cos, sin, seg_col, seg_row, sel, d_qkv, dk_sum, dv_sum
        )
        if i == 0:
            ffn_own.second()
            f_gu.go()
            f_gu.cross()
        if i == 2:
            f_dn.go()
            f_dn.cross()
    attend_back_keys(scale, n_q, cos, sin, d_qkv, dk_sum, dv_sum)

    load_heads.wait()

    def d_term(r, cols):
        value = d_qkv[pl.ds(pl.multiple_of(flip_all(me, r) * rows, rows), rows), :]
        return dot(value, w3_v[cols, : w_heads.shape[1]], ((1,), (1,)))

    in_cols = slice(w_heads.shape[1], w_heads.shape[1] + spread.shape[0])
    in_src = w3_v.reshape(n_z, 2, depth, w3_v.shape[1]).at[:, :, :, in_cols]
    f_in = GradFlow(links, at, in_src, in_land, False, in_out, None)
    packed = dot(d_qkv[...], spread[...], ((1,), (1,))).astype(BF16)
    load_norm.wait()
    for rel, owner in groups():
        lhs = jnp.concatenate([d_proj[b, :, span_of(owner)] for b in range(n_b)], axis=0)
        w3_v[span_of(owner), in_cols] = dot(lhs, packed, ((0,), (0,))).astype(BF16)
        if group == 1:
            f_in.first(rel)
    if group > 1:
        f_in.first()
    d_in = LayerSum(links, at, rows, bufs_a, d_term, ffn_far)
    d_in.begin()
    f_o.go(2)
    d_in.middle()
    f_gu.cross_far()
    d_in.second()
    f_in.go(2)
    f_dn.cross_far()
    out_g, in_g = TpGather(links, at, output), TpGather(links, at, input_grad)
    stay = []
    for p, value in enumerate(d_in.end()):
        r = slice(p * h, (p + 1) * h)
        value = d_mid[r, :] + norm_back(row_v[0, r, :].astype(F32), gains[0:1, :], value)
        row_v[1, r, :] = value.astype(BF16)
    in_g.own(row_v.at[1])
    stay.append(move(row_v.at[1], input_grad.at[t]))
    for copy in sent_far:
        copy.wait_send()
    for p, value in enumerate(ffn_own.end()):
        r = slice(p * h, (p + 1) * h)
        sent_ffn[p].wait_recv()
        value = value + far_in[1, r, :].astype(F32)
        far_v[0, r, :] = (mid[r, :] + value).astype(BF16)
    out_g.own(far_v.at[0])
    f_in.go(2)
    f_o.go()
    f_o.cross()
    stay.append(move(far_v.at[0], output.at[t]))
    f_in.go()
    f_in.cross()
    for flow in (f_gu, f_dn, f_o, f_in):
        stay.append(move(*flow.mine()))
    in_g.second()
    out_g.second()
    for flow in (in_g, out_g, f_gu, f_dn, f_o, f_in):
        flow.last()
    for copy in stay:
        copy.wait()
    for copy in sent_ffn:
        copy.wait_send()
    links.finish(d_in, ffn_own)


def back(n_z, n_tp, scale, units, wide, *args):
    x_here, w_heads, spread, mid, sel = args[0], args[8], args[20], args[10], args[19]
    d_gu, hidden, gu_src, dn_src, w3, w_o, rot = args[3], args[4], args[5], args[6], args[2], args[7], args[12]
    half_len, width = x_here.shape
    rows = mid.shape[0]
    full_len = 2 * half_len
    depth = gu_src.shape[2]
    heads, compact = w_heads.shape[1], spread.shape[0]
    q_cols = sel.shape[1]
    any_, vmem = pl.BlockSpec(memory_space=pl.ANY), pl.BlockSpec(memory_space=pltpu.VMEM)
    shape = jax.ShapeDtypeStruct
    n_swap, n_add = max(1, n_z - 2), n_z - 1
    n_sems = 120 + 8 * n_z
    return pl.pallas_call(
        lambda *refs: back_kernel(n_z, n_tp, scale, min(256, full_len), units, wide, *refs),
        out_shape=(
            shape((n_tp, rows, width), BF16),
            shape((n_tp, rows, width), BF16),
            shape((2, 2, depth, 2 * units), BF16),
            shape((2, 2, depth, units), BF16),
            shape((2, depth, q_cols), BF16),
            shape((2, depth, compact), BF16),
        ),
        in_specs=[any_] * 10 + [vmem] * 11,
        out_specs=(any_,) * 6,
        scratch_shapes=[
            pltpu.VMEM(w3.shape, BF16),
            pltpu.VMEM(d_gu.shape, BF16),
            pltpu.VMEM(hidden.shape, BF16),
            *sum_scratch(rows, width),
            *sum_scratch(rows, width),
            pltpu.VMEM((2, rows, width), BF16),
            pltpu.VMEM((2, rows, width), BF16),
            pltpu.VMEM((rows, width), F32),
            pltpu.VMEM((2, rows, width), BF16),
            pltpu.VMEM((2 * n_tp, rows, width), BF16),
            pltpu.VMEM((full_len, q_cols), BF16),
            pltpu.VMEM((full_len, heads), BF16),
            pltpu.VMEM((full_len, LANES), F32),
            pltpu.VMEM((full_len, LANES), F32),
            pltpu.VMEM(w_o.shape, BF16),
            pltpu.VMEM((n_swap, 2, depth, 2 * units), BF16),
            pltpu.VMEM((depth, 2 * units), BF16),
            pltpu.VMEM((n_swap, 2, depth, units), BF16),
            pltpu.VMEM((depth, units), BF16),
            pltpu.VMEM((depth, 2 * units), BF16),
            pltpu.VMEM((depth, units), BF16),
            pltpu.VMEM((n_add, 2, depth, q_cols), BF16),
            pltpu.VMEM((n_add, 2, depth, compact), BF16),
            pltpu.SemaphoreType.DMA((n_sems,)),
            pltpu.SemaphoreType.DMA((n_sems,)),
            pltpu.SemaphoreType.DMA((24 + 6 * n_z,)),
        ],
        compiler_params=pltpu.CompilerParams(
            collective_id=2, has_side_effects=True, vmem_limit_bytes=BACK_LIMIT
        ),
        name="back",
    )(*args)


def body(
    tokens,
    segments,
    attn_gain,
    q_weight,
    k_weight,
    v_weight,
    o_weight,
    ffn_gain,
    gate_weight,
    up_weight,
    down_weight,
    cotangent,
):
    n_z = lax.axis_size("fsdp")
    n_tp = lax.axis_size("tp")
    _, half_len, width = tokens.shape
    full_len = segments.shape[1]
    rows = half_len // n_tp
    units = gate_weight.shape[1] // 4
    scale = HEAD_DIM ** (-0.5)

    x_here = tokens.reshape(half_len, width)
    dy_here = cotangent.reshape(half_len, width)
    k_t, v_t, o_t, down_t = k_weight.T, v_weight.T, o_weight.T, down_weight.T
    (
        w_heads, w_o, w3, gains, norm_attn, dy_all, norm_all, attn, rot, stats, mid, cos, sin, spread, sel,
        seg_col,
    ) = front(
        n_z, n_tp, scale, x_here, dy_here,
        (q_weight, k_t, v_t, o_t, gate_weight, up_weight, down_t),
        jnp.stack([attn_gain, ffn_gain]), segments,
    )
    w3 = w3.reshape(width, -1)
    norm_all = norm_all.reshape(4 * n_tp, rows, width)
    dy_all = dy_all.reshape(4 * n_tp, rows, width)
    d_gu, hidden = act(norm_all, dy_all, w3, units)
    gu_src, dn_src = terms(norm_all, dy_all, d_gu, hidden, n_z)
    output, input_grad, gu_four, dn_four, o_two, in_two = back(
        n_z, n_tp, scale, units, wide_of(units),
        x_here, dy_here, w3, d_gu.reshape(2, 2 * n_tp, rows, 2 * units),
        hidden.reshape(2, 2 * n_tp, rows, units), gu_src, dn_src, w_o, w_heads,
        norm_attn.reshape(2 * n_tp, rows, width),
        mid, gains, rot, attn, stats, cos, sin, seg_col, segments, sel, spread,
    )
    q_grad, k_grad, v_grad, sums = finish_in(
        gu_four, in_two, q_weight, k_t, v_t, gate_weight, up_weight
    )
    here, others = sum_tp(sums[:, :2].T)
    gate_grad, up_grad, down_grad, o_grad, output, input_grad = finish(
        gu_four, dn_four, o_two, output, input_grad
    )
    gain_sums = sum(others, here)
    attn_gain_grad = gain_sums[0] / attn_gain.astype(F32)
    ffn_gain_grad = gain_sums[1] / ffn_gain.astype(F32)

    return (
        output.reshape(tokens.shape),
        input_grad.reshape(tokens.shape),
        attn_gain_grad,
        q_grad,
        k_grad.T,
        v_grad.T,
        o_grad.T,
        ffn_gain_grad,
        gate_grad,
        up_grad,
        down_grad.T,
    )


def solution(mesh):
    specs = dict(
        tok=P("fsdp", "ctx", None),
        gain=P(("fsdp", "ctx")),
        row=P(("fsdp", "ctx"), "tp"),
        col=P("tp", ("fsdp", "ctx")),
    )
    tok, gain, row, col = specs["tok"], specs["gain"], specs["row"], specs["col"]
    return jax.shard_map(
        body,
        mesh=mesh,
        in_specs=(tok, P("fsdp", None), gain, row, row, row, col, gain, row, row, col, tok),
        out_specs=(tok, tok, gain, row, row, row, col, gain, row, row, col),
        check_vma=False,
    )
```
